32 devices in a mesh: dp: 8 (over y, x, core), mp: 4 (over z).
Axes of the slice: x: 2, y: 2, z: 4, core: 2. Of those that a mesh axis runs over, the one named last changes fastest.
Arguments:
- token_ids: int32 [2048, 2], P('dp'), may hold values from 0 to 32063
- target_ids: int32 [2048, 2], P('dp'), may hold values from 0 to 32063
- counted: int32 [2048, 2], P('dp'), may hold values from 0 to 1, as said below
- routes: int32 [2048, 2, 6], P('dp'), may hold values from 0 to 31, all different within a row; in each aligned block of 512 rows (0 to 511, 512 to 1023, ..., all dimensions but the last counted through in order) at most 192 rows name the same one
- vocab_tables: float32 [2, 1024, 32064], P(None, 'dp', 'mp'), may hold values from -5 to 5
- norm_gains: float32 [3, 1024], P(None, 'dp'), may hold values from 0.3 to 2.4
- attn_in: float32 [1024, 3, 1024], P('dp', None, 'mp'), may hold values from -0.1875 to 0.1875
- attention_output_weight: float32 [1024, 1024], P('mp', 'dp'), may hold values from -0.5 to 0.5
- router: float32 [1024, 32], P('dp'), may hold values from -0.09375 to 0.09375
- shared_in: float32 [1024, 2, 1408], P('dp', None, 'mp'), may hold values from -0.1875 to 0.1875
- shared_out: float32 [1408, 1024], P('mp', 'dp'), may hold values from -0.15625 to 0.15625
- expert_in: float32 [32, 1024, 2, 704], P('mp', 'dp'), may hold values from -0.1875 to 0.1875
- expert_out: float32 [32, 1024, 704], P('mp', 'dp'), may hold values from -0.21875 to 0.21875
- vocab_tables_moment: float32 [2, 1024, 32064], P(None, 'dp', 'mp'), may hold values from -1.4305115e-06 to 1.4305115e-06
- norm_gains_moment: float32 [3, 1024], P(None, 'dp'), may hold values from -3.8146973e-06 to 3.8146973e-06
- attn_in_moment: float32 [1024, 3, 1024], P('dp', None, 'mp'), may hold values from -1.4305115e-06 to 1.4305115e-06
- attn_out_moment: float32 [1024, 1024], P('mp', 'dp'), may hold values from -1.4305115e-06 to 1.4305115e-06
- router_moment: float32 [1024, 32], P('dp'), may hold values from -3.8146973e-06 to 3.8146973e-06
- shared_in_moment: float32 [1024, 2, 1408], P('dp', None, 'mp'), may hold values from -1.4305115e-06 to 1.4305115e-06
- shared_out_moment: float32 [1408, 1024], P('mp', 'dp'), may hold values from -1.4305115e-06 to 1.4305115e-06
- expert_in_moment: float32 [32, 1024, 2, 704], P('mp', 'dp'), may hold values from -1.4305115e-06 to 1.4305115e-06
- expert_out_moment: float32 [32, 1024, 704], P('mp', 'dp'), may hold values from -1.4305115e-06 to 1.4305115e-06
- vocab_tables_square: float32 [2, 1024, 32064], P(None, 'dp', 'mp'), may hold values from 1.8336649e-14 to 2.935258e-13
- norm_gains_square: float32 [3, 1024], P(None, 'dp'), may hold values from 1.65239e-13 to 2.6424297e-12
- attn_in_square: float32 [1024, 3, 1024], P('dp', None, 'mp'), may hold values from 1.8336649e-14 to 2.935258e-13
- attn_out_square: float32 [1024, 1024], P('mp', 'dp'), may hold values from 1.8336649e-14 to 2.935258e-13
- router_square: float32 [1024, 32], P('dp'), may hold values from 1.65239e-13 to 2.6424297e-12
- shared_in_square: float32 [1024, 2, 1408], P('dp', None, 'mp'), may hold values from 1.8336649e-14 to 2.935258e-13
- shared_out_square: float32 [1408, 1024], P('mp', 'dp'), may hold values from 1.8336649e-14 to 2.935258e-13
- expert_in_square: float32 [32, 1024, 2, 704], P('mp', 'dp'), may hold values from 1.8336649e-14 to 2.935258e-13
- expert_out_square: float32 [32, 1024, 704], P('mp', 'dp'), may hold values from 1.8336649e-14 to 2.935258e-13
Outputs:
- loss_sum: float32 [], replicated
- token_count: float32 [], replicated
- grad_norm: float32 [], replicated
- vocab_tables_next: float32 [2, 1024, 32064], P(None, 'dp', 'mp')
- vocab_tables_moment_next: float32 [2, 1024, 32064], P(None, 'dp', 'mp')
- vocab_tables_square_next: float32 [2, 1024, 32064], P(None, 'dp', 'mp')
- norm_gains_next: float32 [3, 1024], P(None, 'dp')
- norm_gains_moment_next: float32 [3, 1024], P(None, 'dp')
- norm_gains_square_next: float32 [3, 1024], P(None, 'dp')
- attn_in_next: float32 [1024, 3, 1024], P('dp', None, 'mp')
- attn_in_moment_next: float32 [1024, 3, 1024], P('dp', None, 'mp')
- attn_in_square_next: float32 [1024, 3, 1024], P('dp', None, 'mp')
- attn_out_next: float32 [1024, 1024], P('mp', 'dp')
- attn_out_moment_next: float32 [1024, 1024], P('mp', 'dp')
- attn_out_square_next: float32 [1024, 1024], P('mp', 'dp')
- router_next: float32 [1024, 32], P('dp')
- router_moment_next: float32 [1024, 32], P('dp')
- router_square_next: float32 [1024, 32], P('dp')
- shared_in_next: float32 [1024, 2, 1408], P('dp', None, 'mp')
- shared_in_moment_next: float32 [1024, 2, 1408], P('dp', None, 'mp')
- shared_in_square_next: float32 [1024, 2, 1408], P('dp', None, 'mp')
- shared_out_next: float32 [1408, 1024], P('mp', 'dp')
- shared_out_moment_next: float32 [1408, 1024], P('mp', 'dp')
- shared_out_square_next: float32 [1408, 1024], P('mp', 'dp')
- expert_in_next: float32 [32, 1024, 2, 704], P('mp', 'dp')
- expert_in_moment_next: float32 [32, 1024, 2, 704], P('mp', 'dp')
- expert_in_square_next: float32 [32, 1024, 2, 704], P('mp', 'dp')
- expert_out_next: float32 [32, 1024, 704], P('mp', 'dp')
- expert_out_moment_next: float32 [32, 1024, 704], P('mp', 'dp')
- expert_out_square_next: float32 [32, 1024, 704], P('mp', 'dp')
The draws below stay inside these ranges and needn't reach their ends.
Inputs may be any that keep to these rules, and one draw needn't show every extreme that they name: `routes`: in the rows of one device (512 tokens of one index of dp) no expert is named by more than 192 rows, a bound that some block reaches; a token's 6 experts differ. The last position of every sequence is counted.
All inputs are finite; a program needn't handle non-finite values.
Results may differ from the reference program's by a relative error of at most 0.028.
The reference program's roundings to bfloat16 on the way count: a program that leaves them out, or rounds other values in their place, can miss the bound.
Values may be sent and summed in bfloat16 or wider, within the bound.
No kernel may reach another device: no remote copies, remote signals or barrier semaphores. Data moves between devices by JAX's collectives and lax.ppermute only.
A program may use at most 272 MiB of HBM per device.

```python
import math
import jax
import jax.numpy as jnp
import numpy as np
from jax import lax

D = 1024
H = 8
HD = 128
FF = 704
SHARED = 2
TOPK = 6
VOCAB = 32064
SEQS = 2
STEP = 10
LENGTH = 2048
TOK_DEV = 512
EXPERTS = 32
CAPACITY = 192
PARAMS = 143428608
N_DP = 8


def draw_counted(key, part):
    key = jax.random.fold_in(key, 37)
    position = jnp.arange(LENGTH, dtype=jnp.int32)[:, None]
    keep_level = 250 + 500 * position // LENGTH
    coin_flip = jax.random.randint(key, (LENGTH, SEQS), 0, 1000)
    picked = (coin_flip < keep_level).astype(jnp.int32)
    return jnp.where(position == LENGTH - 1, 1, picked).astype(jnp.int32)


def draw_vocab_tables(key, part):
    key = jax.random.fold_in(key, 11)
    first_key, second_key = jax.random.split(key)
    rising = jnp.arange(VOCAB, dtype=jnp.float32)[:, None] / VOCAB
    embed_rows = jnp.clip(jax.random.normal(first_key, (VOCAB, D), jnp.float32), -5.0, 5.0)
    head_rows = jnp.clip(jax.random.normal(second_key, (VOCAB, D), jnp.float32), -5.0, 5.0) * (1.0 + 2.0 * rising)
    return jnp.stack([embed_rows, head_rows * D ** (-0.5)]).transpose(0, 2, 1).astype(jnp.float32)


def draw_norm_gains(key, part):
    key = jax.random.fold_in(key, 23)
    rising = jnp.arange(D, dtype=jnp.float32)[None, :] / D
    spread = 0.1 * jnp.clip(jax.random.normal(key, (3, D), jnp.float32), -3.0, 3.0)
    return ((0.6 + 1.2 * rising) * (1.0 + spread)).astype(jnp.float32)


def place_ends(values, rng, smallest, top_value):
    place = [jax.random.randint(jax.random.fold_in(rng, axis), (), 0, length) for axis, length in enumerate(values.shape)]
    main_axis = values.shape.index(max(values.shape))
    next_to = place[:main_axis] + [(place[main_axis] + 1) % values.shape[main_axis]] + place[main_axis + 1:]
    return values.at[tuple(place)].set(smallest).at[tuple(next_to)].set(top_value)


def block_scale(key, extent, cuts, smallest, largest):
    loudness = 1.0
    for dim, blocks in cuts:
        steps = jax.random.uniform(jax.random.fold_in(jax.random.fold_in(key, 6), dim), (blocks,), jnp.float32, smallest / len(cuts), largest / len(cuts))
        loudness = loudness * jnp.repeat(jnp.exp(steps), extent[dim] // blocks).reshape((-1,) + (1,) * (len(extent) - 1 - dim))
    return loudness


def cumulative_ranks(count, skew):
    weights = [(1 << 20) // math.isqrt(standing ** skew) + 1 for standing in range(1, count + 1)]
    width = 1 + sum(weights) // (1 << 30)
    return np.cumsum(np.array([max(1, weight // width) for weight in weights]))


def skewed_ids(own_key, shape, amount, slope):
    table = cumulative_ranks(amount, slope)
    pick = jax.random.randint(jax.random.fold_in(own_key, 1), shape, 0, int(table[amount - 1]))
    rank = jnp.searchsorted(jnp.asarray(table, jnp.int32), pick, side="right")
    return jax.random.permutation(jax.random.fold_in(own_key, 2), amount)[rank].astype(jnp.int32)


def deal_out(key, own, number, rows, count, top, bound, lean):
    ranking = jax.random.permutation(key, count)
    packed, usual = load_shares(count, rows * top, bound, lean, True), load_shares(count, rows * top, bound, lean, False)
    places = jnp.arange(count)

    def named(sizes, turn):
        used = int((sizes > 0).sum())
        fixed = max(1, used // 4)
        shifted = fixed + (places - fixed + turn * (used - fixed)) % max(1, count - fixed)
        return jnp.zeros((count,), jnp.int32).at[ranking[jnp.where(places < fixed, places, shifted)]].set(jnp.asarray(sizes, jnp.int32))

    sizes = jnp.where(number % 4 == 0, named(packed, number // 4), named(usual, number - number // 4 - 1))
    mixed = jax.random.permutation(jax.random.fold_in(own, 3), count)
    giver, taker = mixed[0:count // 2 * 2:2], mixed[1:count // 2 * 2:2]
    slack = jnp.minimum(sizes[giver] - 1, bound - sizes[taker]) // 2
    slack = jnp.where((giver == ranking[0]) | (taker == ranking[0]) | (sizes[taker] == 0), 0, jnp.maximum(slack, 0))
    shifted = jax.random.randint(jax.random.fold_in(own, 4), (count // 2,), 0, 1 << 20) % (slack + 1)
    sizes = sizes.at[giver].add(-shifted).at[taker].add(shifted)
    members = jnp.searchsorted(jnp.cumsum(sizes), jnp.arange(rows * top), side="right").astype(jnp.int32)
    table = members.reshape(top, rows).T
    table = table[jax.random.permutation(jax.random.fold_in(own, 1), rows)]
    turn = jax.random.randint(jax.random.fold_in(own, 2), (rows, 1), 0, top)
    return jnp.take_along_axis(table, (jnp.arange(top)[None, :] + turn) % top, axis=1)


def load_shares(amount, total, most, slope, full):
    weights = [(1 << 20) // math.isqrt(rank ** slope) + 1 for rank in range(1, amount + 1)]
    largest = most if full else min(most, max(-(-total // amount), total * weights[0] // sum(weights)))
    least = 1 if total - largest >= amount - 1 else 0
    counts, surplus = [largest] + [least] * (amount - 1), total - largest - least * (amount - 1)
    while surplus > 0:
        free = [i for i in range(1, amount) if counts[i] < largest] or [i for i in range(1, amount) if counts[i] < most]
        mass, remaining = sum([weights[i] for i in free]), surplus
        for i in free:
            addition = min(most - counts[i], max(1, remaining * weights[i] // mass), surplus)
            counts[i] = counts[i] + addition
            surplus = surplus - addition
    return np.array(counts)


def gaussian(rng, shape, scale, reach, shards=(), held_as=jnp.bfloat16):
    values = jax.random.normal(rng, shape, jnp.float32) * scale
    if len(shards) > 0:
        values = block_scale(rng, shape, shards, -0.22, 0.18) * values
    return jnp.clip(values, min=-reach, max=reach).astype(held_as)


def setup_inputs(seed: int = 0) -> dict:
    streams_of = jax.random.split(jax.random.key(seed), 32)
    token_ids = place_ends(skewed_ids(streams_of[0], (LENGTH, SEQS), VOCAB, 2), jax.random.fold_in(streams_of[0], 3), 0, VOCAB - 1).astype(jnp.int32)
    target_ids = place_ends(skewed_ids(streams_of[1], (LENGTH, SEQS), VOCAB, 2), jax.random.fold_in(streams_of[1], 3), 0, VOCAB - 1).astype(jnp.int32)
    counted = draw_counted(jax.random.fold_in(streams_of[31], 71), 0)
    routes_keys = jax.random.split(jax.random.fold_in(streams_of[3], 1), LENGTH * SEQS // TOK_DEV)
    routes_turns = jax.random.permutation(jax.random.fold_in(streams_of[3], 3), LENGTH * SEQS // TOK_DEV)
    routes = jax.vmap(lambda own, number: deal_out(jax.random.fold_in(streams_of[3], 2), own, number, TOK_DEV, EXPERTS, TOPK, CAPACITY, 1))(routes_keys, routes_turns).reshape((LENGTH, SEQS, TOPK))
    vocab_tables = draw_vocab_tables(jax.random.fold_in(streams_of[31], 71), 0)
    norm_gains = draw_norm_gains(jax.random.fold_in(streams_of[31], 71), 0)
    attn_in = gaussian(streams_of[6], (D, 3, H * HD), D ** -0.5, 0.1875, ((0, 8), (2, 4)), jnp.float32)
    attention_output_weight = gaussian(streams_of[7], (H * HD, D), (H * HD // 8) ** -0.5, 0.5, ((0, 4), (1, 8)), jnp.float32)
    router = gaussian(streams_of[8], (D, EXPERTS), (4 * D) ** -0.5, 0.09375, ((0, 8),), jnp.float32)
    shared_in = gaussian(streams_of[9], (D, 2, SHARED * FF), D ** -0.5, 0.1875, ((0, 8), (2, 4)), jnp.float32)
    shared_out = gaussian(streams_of[10], (SHARED * FF, D), (SHARED * FF) ** -0.5, 0.15625, ((0, 4), (1, 8)), jnp.float32)
    expert_in = gaussian(streams_of[11], (EXPERTS, D, 2, FF), D ** -0.5, 0.1875, ((0, 4), (1, 8)), jnp.float32)
    expert_out = gaussian(streams_of[12], (EXPERTS, D, FF), FF ** -0.5, 0.21875, ((0, 4), (1, 8)), jnp.float32)
    vocab_tables_moment = gaussian(streams_of[13], (2, D, VOCAB), (0.0011 / PARAMS ** 0.5), 1.430511474609375e-06, ((1, 8), (2, 4)), jnp.float32)
    norm_gains_moment = gaussian(streams_of[14], (3, D), (0.0033 / PARAMS ** 0.5), 3.814697265625e-06, ((1, 8),), jnp.float32)
    attn_in_moment = gaussian(streams_of[15], (D, 3, H * HD), (0.0011 / PARAMS ** 0.5), 1.430511474609375e-06, ((0, 8), (2, 4)), jnp.float32)
    attn_out_moment = gaussian(streams_of[16], (H * HD, D), (0.0011 / PARAMS ** 0.5), 1.430511474609375e-06, ((0, 4), (1, 8)), jnp.float32)
    router_moment = gaussian(streams_of[17], (D, EXPERTS), (0.0033 / PARAMS ** 0.5), 3.814697265625e-06, ((0, 8),), jnp.float32)
    shared_in_moment = gaussian(streams_of[18], (D, 2, SHARED * FF), (0.0011 / PARAMS ** 0.5), 1.430511474609375e-06, ((0, 8), (2, 4)), jnp.float32)
    shared_out_moment = gaussian(streams_of[19], (SHARED * FF, D), (0.0011 / PARAMS ** 0.5), 1.430511474609375e-06, ((0, 4), (1, 8)), jnp.float32)
    expert_in_moment = gaussian(streams_of[20], (EXPERTS, D, 2, FF), (0.0011 / PARAMS ** 0.5), 1.430511474609375e-06, ((0, 4), (1, 8)), jnp.float32)
    expert_out_moment = gaussian(streams_of[21], (EXPERTS, D, FF), (0.0011 / PARAMS ** 0.5), 1.430511474609375e-06, ((0, 4), (1, 8)), jnp.float32)
    vocab_tables_square = jnp.clip(jnp.exp(math.log(2.935258102115118e-13) - 2.773064 * jax.random.uniform(streams_of[22], (2, D, VOCAB), jnp.float32) ** block_scale(streams_of[22], (2, D, VOCAB), ((1, 8), (2, 4)), -0.2, 0.2)), 1.8336648863258136e-14, 2.935258102115118e-13)
    norm_gains_square = jnp.clip(jnp.exp(math.log(2.6424296778460032e-12) - 2.772061 * jax.random.uniform(streams_of[23], (3, D), jnp.float32) ** block_scale(streams_of[23], (3, D), ((1, 8),), -0.2, 0.2)), 1.6523899761498873e-13, 2.6424296778460032e-12)
    attn_in_square = jnp.clip(jnp.exp(math.log(2.935258102115118e-13) - 2.773064 * jax.random.uniform(streams_of[24], (D, 3, H * HD), jnp.float32) ** block_scale(streams_of[24], (D, 3, H * HD), ((0, 8), (2, 4)), -0.2, 0.2)), 1.8336648863258136e-14, 2.935258102115118e-13)
    attn_out_square = jnp.clip(jnp.exp(math.log(2.935258102115118e-13) - 2.773064 * jax.random.uniform(streams_of[25], (H * HD, D), jnp.float32) ** block_scale(streams_of[25], (H * HD, D), ((0, 4), (1, 8)), -0.2, 0.2)), 1.8336648863258136e-14, 2.935258102115118e-13)
    router_square = jnp.clip(jnp.exp(math.log(2.6424296778460032e-12) - 2.772061 * jax.random.uniform(streams_of[26], (D, EXPERTS), jnp.float32) ** block_scale(streams_of[26], (D, EXPERTS), ((0, 8),), -0.2, 0.2)), 1.6523899761498873e-13, 2.6424296778460032e-12)
    shared_in_square = jnp.clip(jnp.exp(math.log(2.935258102115118e-13) - 2.773064 * jax.random.uniform(streams_of[27], (D, 2, SHARED * FF), jnp.float32) ** block_scale(streams_of[27], (D, 2, SHARED * FF), ((0, 8), (2, 4)), -0.2, 0.2)), 1.8336648863258136e-14, 2.935258102115118e-13)
    shared_out_square = jnp.clip(jnp.exp(math.log(2.935258102115118e-13) - 2.773064 * jax.random.uniform(streams_of[28], (SHARED * FF, D), jnp.float32) ** block_scale(streams_of[28], (SHARED * FF, D), ((0, 4), (1, 8)), -0.2, 0.2)), 1.8336648863258136e-14, 2.935258102115118e-13)
    expert_in_square = jnp.clip(jnp.exp(math.log(2.935258102115118e-13) - 2.773064 * jax.random.uniform(streams_of[29], (EXPERTS, D, 2, FF), jnp.float32) ** block_scale(streams_of[29], (EXPERTS, D, 2, FF), ((0, 4), (1, 8)), -0.2, 0.2)), 1.8336648863258136e-14, 2.935258102115118e-13)
    expert_out_square = jnp.clip(jnp.exp(math.log(2.935258102115118e-13) - 2.773064 * jax.random.uniform(streams_of[30], (EXPERTS, D, FF), jnp.float32) ** block_scale(streams_of[30], (EXPERTS, D, FF), ((0, 4), (1, 8)), -0.2, 0.2)), 1.8336648863258136e-14, 2.935258102115118e-13)
    return {"token_ids": token_ids, "target_ids": target_ids, "counted": counted, "routes": routes, "vocab_tables": vocab_tables, "norm_gains": norm_gains, "attn_in": attn_in, "attention_output_weight": attention_output_weight, "router": router, "shared_in": shared_in, "shared_out": shared_out, "expert_in": expert_in, "expert_out": expert_out, "vocab_tables_moment": vocab_tables_moment, "norm_gains_moment": norm_gains_moment, "attn_in_moment": attn_in_moment, "attn_out_moment": attn_out_moment, "router_moment": router_moment, "shared_in_moment": shared_in_moment, "shared_out_moment": shared_out_moment, "expert_in_moment": expert_in_moment, "expert_out_moment": expert_out_moment, "vocab_tables_square": vocab_tables_square, "norm_gains_square": norm_gains_square, "attn_in_square": attn_in_square, "attn_out_square": attn_out_square, "router_square": router_square, "shared_in_square": shared_in_square, "shared_out_square": shared_out_square, "expert_in_square": expert_in_square, "expert_out_square": expert_out_square}


FULL_ACCURACY = lax.Precision.HIGHEST
NORM_EPS = 1e-06
Z_COEF = 0.01
CLIP = 0.01
BETA_ONE = 0.9
BETA_TWO = 0.95
ADAM_EPS = 1e-08
TABLE_RATES = (1.0, 0.06)
RATES = (0.0, 1.0, 0.02, 0.05, 0.01, 0.02, 0.02, 0.02, 0.02)
DECAYS = (0.1, 0.0, 0.1, 0.1, 0.1, 0.1, 0.1, 0.1, 0.1)

@jax.custom_vjp
def low(v):
    return lax.optimization_barrier(v.astype(jnp.bfloat16)).astype(jnp.float32)

@jax.custom_vjp
def reduced_backward(v):
    return v

def low_keep(v):
    return (low(v), None)

def low_pass(kept, grad):
    return (grad,)

def back_keep(v):
    return (v, None)

def back_low(kept, grad):
    return (low(grad),)
low.defvjp(low_keep, low_pass)
reduced_backward.defvjp(back_keep, back_low)

def matmul(left, right):
    return jnp.dot(left, right, precision=FULL_ACCURACY)

def normed(values, gain_row):
    return values * lax.rsqrt(lax.optimization_barrier(jnp.mean(values * values, axis=-1, keepdims=True)) + NORM_EPS) * gain_row

def swiglu(gate_up):
    half_width = gate_up.shape[-1] // 2
    return jax.nn.silu(gate_up[..., :half_width]) * gate_up[..., half_width:]

def slot_table(flat_route, experts, capacity):
    row_count = flat_route.shape[0]
    onehot = (flat_route[:, None] == jnp.arange(experts, dtype=jnp.int32)[None, :]).astype(jnp.int32)
    slot_rank = lax.optimization_barrier(jnp.sum((jnp.cumsum(onehot, axis=0) - onehot) * onehot, axis=1)).astype(jnp.int32)
    empty_slots = jnp.full((experts, capacity), row_count, jnp.int32)
    return empty_slots.at[flat_route, slot_rank].set(jnp.arange(row_count, dtype=jnp.int32), mode='drop')

def adam_update(weight, moment, square, grad_item, rate, decay):
    new_moment = BETA_ONE * moment + (1.0 - BETA_ONE) * grad_item
    new_square = BETA_TWO * square + (1.0 - BETA_TWO) * grad_item * grad_item
    step_ratio = new_moment / (1.0 - BETA_ONE ** STEP) / (jnp.sqrt(new_square / (1.0 - BETA_TWO ** STEP)) + ADAM_EPS)
    return (weight - rate * (step_ratio + decay * weight), new_moment, new_square)

def one_head(head_item):
    query_rows, key_rows, value_rows = head_item
    seq_span = query_rows.shape[0]
    scores = reduced_backward(matmul(query_rows, key_rows.T) * HD ** (-0.5))
    position = jnp.arange(seq_span)
    scores = jnp.where(position[None, :] <= position[:, None], scores, -1e+30)
    log_total = jax.nn.logsumexp(scores, axis=1, keepdims=True)
    return matmul(low(jnp.exp(scores - log_total)), value_rows)

def forward(params, token_ids, target_ids, counted, routes):
    vocab_tables, norm_gains, attn_in, attention_output_weight, router, shared_in, shared_out, expert_in, expert_out = [low(weight) for weight in params]
    embedding_rows = vocab_tables[0][token_ids]
    first_in = low(normed(embedding_rows, norm_gains[0]))
    projected = reduced_backward(low(jnp.einsum('lsd,dkf->lskf', first_in, attn_in, precision=FULL_ACCURACY)))
    head_items = projected.reshape(LENGTH, SEQS, 3, H, HD).transpose(2, 1, 3, 0, 4).reshape(3, SEQS * H, LENGTH, HD)
    attention_result = lax.map(jax.checkpoint(one_head), (head_items[0], head_items[1], head_items[2]))
    attention_result = attention_result.reshape(SEQS, H, LENGTH, HD).transpose(2, 0, 1, 3).reshape(LENGTH, SEQS, H * HD)
    attention_result = reduced_backward(low(attention_result))
    post_attention_state = embedding_rows + reduced_backward(jnp.einsum('ncp,pk->nck', attention_result, attention_output_weight, precision=FULL_ACCURACY))
    second_in = low(normed(post_attention_state, norm_gains[1])).reshape(N_DP, TOK_DEV, D)

    def expert_block(block_item):
        token_rows, flat_route = block_item
        router_logits = reduced_backward(matmul(token_rows, router))
        gate_probs = jax.nn.softmax(jnp.take_along_axis(router_logits, flat_route.reshape(TOK_DEV, TOPK), axis=1), axis=1)
        shared_both = reduced_backward(matmul(token_rows, shared_in.reshape(D, -1)))
        shared_part = reduced_backward(matmul(low(swiglu(shared_both)), shared_out))
        slot_index = slot_table(flat_route, EXPERTS, CAPACITY)
        token_of = slot_index // TOPK
        padded = jnp.concatenate([token_rows, jnp.zeros((1, D), jnp.float32)], axis=0)
        picked = padded[token_of]
        expert_both = reduced_backward(jnp.einsum('ecd,edf->ecf', picked, expert_in.reshape(EXPERTS, D, -1), precision=FULL_ACCURACY))
        expert_output = reduced_backward(jnp.einsum('ecf,efd->ecd', low(swiglu(expert_both)), expert_out, precision=FULL_ACCURACY))
        slot_gate = jnp.concatenate([gate_probs.reshape(-1), jnp.zeros((1,), jnp.float32)])[slot_index]
        routed = jnp.zeros((TOK_DEV + 1, D), jnp.float32).at[token_of].add(slot_gate[..., None] * expert_output)
        return shared_part + routed[:TOK_DEV]
    moe_rows = lax.map(jax.checkpoint(expert_block), (second_in, routes.reshape(N_DP, TOK_DEV * TOPK)))
    after_moe = post_attention_state + moe_rows.reshape(LENGTH, SEQS, D)
    third_in = low(normed(after_moe, norm_gains[2])).reshape(N_DP, TOK_DEV, D)
    token_weight = counted.reshape(N_DP, TOK_DEV).astype(jnp.float32)

    def head_block(block_item):
        token_rows, goal_index, weight_rows = block_item
        logits = reduced_backward(matmul(token_rows, vocab_tables[1].T))
        log_total = jax.nn.logsumexp(logits, axis=1)
        goal_logit = jnp.take_along_axis(logits, goal_index[:, None], axis=1)[:, 0]
        return jnp.sum(weight_rows * (log_total - goal_logit + Z_COEF * log_total * log_total))
    loss_sum = jnp.sum(lax.map(jax.checkpoint(head_block), (third_in, target_ids.reshape(N_DP, TOK_DEV), token_weight)))
    return (loss_sum / jnp.sum(token_weight), loss_sum)

def turned(group):
    return tuple((item.transpose(0, 2, 1) if index in (0, 8) else item for index, item in enumerate(group)))

def reference(token_ids, target_ids, counted, routes, vocab_tables, norm_gains, attn_in, attention_output_weight, router, shared_in, shared_out, expert_in, expert_out, vocab_tables_moment, norm_gains_moment, attn_in_moment, attn_out_moment, router_moment, shared_in_moment, shared_out_moment, expert_in_moment, expert_out_moment, vocab_tables_square, norm_gains_square, attn_in_square, attn_out_square, router_square, shared_in_square, shared_out_square, expert_in_square, expert_out_square):
    params = turned((vocab_tables, norm_gains, attn_in, attention_output_weight, router, shared_in, shared_out, expert_in, expert_out))
    moments = turned((vocab_tables_moment, norm_gains_moment, attn_in_moment, attn_out_moment, router_moment, shared_in_moment, shared_out_moment, expert_in_moment, expert_out_moment))
    squares = turned((vocab_tables_square, norm_gains_square, attn_in_square, attn_out_square, router_square, shared_in_square, shared_out_square, expert_in_square, expert_out_square))

    def objective(*weights):
        return forward(weights, token_ids, target_ids, counted, routes)
    objective_value, pullback, loss_sum = jax.vjp(objective, *params, has_aux=True)
    gradients = pullback(jnp.ones_like(objective_value))
    grad_norm = jnp.sqrt(sum((jnp.sum(grad_item * grad_item) for grad_item in gradients)))
    factor = CLIP / jnp.maximum(grad_norm, CLIP)
    results = [loss_sum, jnp.sum(counted).astype(jnp.float32), grad_norm]
    for index in range(9):
        rate = jnp.array(TABLE_RATES, jnp.float32).reshape(2, 1, 1) if index == 0 else RATES[index]
        refreshed_params = adam_update(params[index], moments[index], squares[index], gradients[index] * factor, rate, DECAYS[index])
        if index in (0, 8):
            refreshed_params = tuple((item.transpose(0, 2, 1) for item in refreshed_params))
        results.extend(refreshed_params)
    return tuple(results)
```

```python
import functools

import jax
import jax.numpy as jnp
from jax import lax
from jax.experimental import pallas as pl
from jax.experimental.pallas import tpu as pltpu
from jax.sharding import PartitionSpec as P

D = 1024
HD = 128
TOPK = 6
STEP = 10
LANES = 128
VOCAB_BLOCK = 1024
VMEM_BYTES = 50 * 1024 * 1024

NORM_EPS = 1e-06
Z_COEF = 0.01
CLIP = 0.01
BETA_ONE = 0.9
BETA_TWO = 0.95
ADAM_EPS = 1e-08
TABLE_RATES = (1.0, 0.06)
RATES = (0.0, 1.0, 0.02, 0.05, 0.01, 0.02, 0.02, 0.02, 0.02)
DECAYS = (0.1, 0.0, 0.1, 0.1, 0.1, 0.1, 0.1, 0.1, 0.1)
FAR = -1e30
LOW = jnp.bfloat16
FULL = jnp.float32


def dot_nn(left, right):
    return lax.dot_general(left, right, (((1,), (0,)), ((), ())), preferred_element_type=FULL)


def dot_nt(left, right):
    return lax.dot_general(left, right, (((1,), (1,)), ((), ())), preferred_element_type=FULL)


def dot_tn(left, right):
    return lax.dot_general(left, right, (((0,), (0,)), ((), ())), preferred_element_type=FULL)


def params_of(dims=1):
    return pltpu.CompilerParams(
        dimension_semantics=("arbitrary",) * dims, vmem_limit_bytes=VMEM_BYTES
    )


def round_up(number, unit):
    return (number + unit - 1) // unit * unit


def normed(values, gain_row):
    return (
        values * lax.rsqrt(jnp.mean(values * values, axis=-1, keepdims=True) + NORM_EPS) * gain_row
    )


def norm_back(values, gain_row, upstream):
    inv_rms = lax.rsqrt(jnp.mean(values * values, axis=-1, keepdims=True) + NORM_EPS)
    unit_rows = values * inv_rms
    scaled = upstream * gain_row
    gain_grad = jnp.sum(upstream * unit_rows, axis=0)
    return (
        inv_rms * (scaled - unit_rows * jnp.mean(scaled * unit_rows, axis=-1, keepdims=True)),
        gain_grad,
    )


def swiglu_grads(gate_part, up_part, upstream):
    sigmoid_gate = jax.nn.sigmoid(gate_part)
    silu_gate = gate_part * sigmoid_gate
    gate_grad = upstream * up_part * sigmoid_gate * (1.0 + gate_part * (1.0 - sigmoid_gate))
    return gate_grad, upstream * silu_gate


def adam_update(weight, moment, square, grad_item, rate, decay):
    new_moment = BETA_ONE * moment + (1.0 - BETA_ONE) * grad_item
    new_square = BETA_TWO * square + (1.0 - BETA_TWO) * grad_item * grad_item
    step_ratio = (
        new_moment
        / (1.0 - BETA_ONE**STEP)
        / (jnp.sqrt(new_square / (1.0 - BETA_TWO**STEP)) + ADAM_EPS)
    )
    return (weight - rate * (step_ratio + decay * weight), new_moment, new_square)


def sum_rows(partial):
    size = lax.axis_size("mp")
    place = lax.axis_index("mp")
    pieces = partial.reshape((size, partial.shape[0] // size) + partial.shape[1:])
    total = lax.dynamic_index_in_dim(pieces, place, 0, keepdims=False).astype(FULL)
    for step in range(1, size):
        sent = lax.dynamic_index_in_dim(pieces, (place + step) % size, 0, keepdims=False)
        got = lax.ppermute(sent, "mp", [(i, (i + step) % size) for i in range(size)])
        total = total + got.astype(FULL)
    return total


def gather_rows(rows):
    size = lax.axis_size("mp")
    place = lax.axis_index("mp")
    count = rows.shape[0]
    whole = jnp.zeros((size * count,) + rows.shape[1:], rows.dtype)
    rest = (0,) * (rows.ndim - 1)
    whole = lax.dynamic_update_slice(whole, rows, (place * count,) + rest)
    for step in range(1, size):
        got = lax.ppermute(rows, "mp", [(i, (i + step) % size) for i in range(size)])
        whole = lax.dynamic_update_slice(whole, got, ((place - step) % size * count,) + rest)
    return whole


def swap(item, mask):
    size = lax.axis_size("dp")
    return lax.ppermute(item, "dp", [(i, i ^ mask) for i in range(size)])


def gather_keys(item):
    size = lax.axis_size("dp")
    blocks = [item if mask == 0 else swap(item, mask) for mask in range(0, size, 2)]
    both = []
    for block in blocks:
        both.extend([block, swap(block, 1)])
    return both


def scatter_keys(blocks):
    size = lax.axis_size("dp")
    total = None
    for mask in range(0, size, 2):
        pair = blocks[mask].astype(FULL) + swap(blocks[mask + 1], 1).astype(FULL)
        if mask > 0:
            pair = swap(pair.astype(LOW), mask).astype(FULL)
        total = pair if total is None else total + pair
    return total


def lookup_kernel(ids_ref, table_ref, out_ref):
    base = pl.program_id(0) * out_ref.shape[0]

    def copy_rows(step, carry):
        for inner in range(8):
            row = step * 8 + inner
            out_ref[pl.ds(row, 1), :] = table_ref[0, pl.ds(ids_ref[base + row], 1), :]
        return carry

    lax.fori_loop(0, out_ref.shape[0] // 8, copy_rows, 0)


def lookup(ids, tables):
    count = ids.shape[0]
    vocab, width = tables.shape[1:]
    block = 512
    return pl.pallas_call(
        lookup_kernel,
        grid_spec=pltpu.PrefetchScalarGridSpec(
            num_scalar_prefetch=1,
            grid=(count // block,),
            in_specs=[pl.BlockSpec((1, vocab, width), lambda i, ids_ref: (0, 0, 0))],
            out_specs=pl.BlockSpec((block, width), lambda i, ids_ref: (i, 0)),
        ),
        out_shape=jax.ShapeDtypeStruct((count, width), FULL),
        compiler_params=params_of(),
        name="lookup",
    )(ids, tables)


def table_grad_kernel(ids_ref, rows_ref, after_ref, out_ref):
    del after_ref
    block = out_ref.shape[0]
    span = 512
    first = pl.program_id(0) * block
    token_of = first + lax.broadcasted_iota(jnp.int32, (block, span), 0)
    total = jnp.zeros(out_ref.shape, FULL)
    for start in range(0, rows_ref.shape[0], span):
        hit = (token_of == ids_ref[:, start : start + span]).astype(FULL).astype(LOW)
        total = total + dot_nn(hit, rows_ref[start : start + span, :])
    out_ref[...] = total


def table_grad(ids, rows, vocab, after):
    count, width = rows.shape
    return pl.pallas_call(
        table_grad_kernel,
        grid=(pl.cdiv(vocab, VOCAB_BLOCK),),
        in_specs=[
            pl.BlockSpec((1, count), lambda j: (0, 0)),
            pl.BlockSpec((count, width), lambda j: (0, 0)),
            pl.BlockSpec(memory_space=pl.ANY),
        ],
        out_specs=pl.BlockSpec((VOCAB_BLOCK, width), lambda j: (j, 0)),
        out_shape=jax.ShapeDtypeStruct((vocab, width), FULL),
        compiler_params=params_of(),
        name="table_grad",
    )(ids.reshape(1, count), rows, after)


def masked_scores(place, query, keys, rows, blocks):
    scores = dot_nt(query, keys) * HD ** (-0.5)
    offset = lax.broadcasted_iota(jnp.int32, (1, rows), 1)
    key_pos = jnp.concatenate(
        [jnp.bitwise_xor(place, mask) * rows + offset for mask in range(blocks)], axis=1
    )
    query_pos = place * rows + lax.broadcasted_iota(jnp.int32, (rows, 1), 0)
    return jnp.where(key_pos <= query_pos, scores, FAR)


def head_cols(refs, index):
    return jnp.concatenate([ref[:, index * HD : (index + 1) * HD] for ref in refs], axis=0)


def attend_kernel(blocks, place_ref, query_ref, *refs):
    key_refs = refs[:blocks]
    out_ref, log_ref = refs[blocks:]
    place = place_ref[0]
    rows, width = query_ref.shape
    heads = width // HD
    for head in range(heads):
        cols = slice(head * HD, (head + 1) * HD)
        keys = head_cols(key_refs, head)
        values = head_cols(key_refs, heads + head)
        scores = masked_scores(place, query_ref[:, cols], keys, rows, blocks)
        top = jnp.max(scores, axis=1, keepdims=True)
        powers = jnp.exp(scores - top)
        total = jnp.sum(powers, axis=1, keepdims=True)
        probs = (powers * (1.0 / total)).astype(LOW)
        out_ref[:, cols] = dot_nn(probs, values).astype(LOW)
        log_ref[0, :, head : head + 1] = top + jnp.log(total)


def attend(place, projected, key_blocks, seqs):
    blocks = len(key_blocks)
    tokens = projected.shape[0]
    rows = tokens // seqs
    width = projected.shape[1] // 3
    heads = width // HD
    return pl.pallas_call(
        functools.partial(attend_kernel, blocks),
        grid_spec=pltpu.PrefetchScalarGridSpec(
            num_scalar_prefetch=1,
            grid=(seqs,),
            in_specs=[pl.BlockSpec((rows, width), lambda s, place_ref: (s, 0))]
            + [pl.BlockSpec((rows, 2 * width), lambda s, place_ref: (s, 0))] * blocks,
            out_specs=[
                pl.BlockSpec((rows, width), lambda s, place_ref: (s, 0)),
                pl.BlockSpec((1, rows, heads), lambda s, place_ref: (s, 0, 0)),
            ],
        ),
        out_shape=[
            jax.ShapeDtypeStruct((tokens, width), LOW),
            jax.ShapeDtypeStruct((seqs, rows, heads), FULL),
        ],
        compiler_params=params_of(),
        name="attend",
    )(place, projected, *key_blocks)


def attend_back_kernel(blocks, place_ref, query_ref, log_ref, grad_ref, after_ref, *refs):
    del after_ref
    key_refs = refs[:blocks]
    query_grad_ref = refs[blocks]
    key_grad_refs = refs[blocks + 1 :]
    place = place_ref[0]
    rows, width = query_ref.shape
    heads = width // HD
    for head in range(heads):
        cols = slice(head * HD, (head + 1) * HD)
        keys = head_cols(key_refs, head)
        values = head_cols(key_refs, heads + head)
        query = query_ref[:, cols]
        out_grad = grad_ref[:, cols]
        scores = masked_scores(place, query, keys, rows, blocks)
        probs = jnp.exp(scores - log_ref[0, :, head : head + 1])
        prob_grad = dot_nt(out_grad, values)
        delta = jnp.sum(probs * prob_grad, axis=1, keepdims=True)
        score_grad = (probs * (prob_grad - delta)).astype(LOW)
        query_grad_ref[:, cols] = (dot_nn(score_grad, keys) * HD ** (-0.5)).astype(LOW)
        key_grad = (dot_tn(score_grad, query) * HD ** (-0.5)).astype(LOW)
        value_grad = dot_tn(probs.astype(LOW), out_grad).astype(LOW)
        value_cols = slice((heads + head) * HD, (heads + head + 1) * HD)
        for mask in range(blocks):
            part = slice(mask * rows, (mask + 1) * rows)
            key_grad_refs[mask][:, cols] = key_grad[part]
            key_grad_refs[mask][:, value_cols] = value_grad[part]


def attend_back(place, projected, log_total, out_grad, key_blocks, seqs, after):
    blocks = len(key_blocks)
    tokens = projected.shape[0]
    rows = tokens // seqs
    width = projected.shape[1] // 3
    heads = width // HD
    row_spec = pl.BlockSpec((rows, width), lambda s, place_ref: (s, 0))
    key_spec = pl.BlockSpec((rows, 2 * width), lambda s, place_ref: (s, 0))
    return pl.pallas_call(
        functools.partial(attend_back_kernel, blocks),
        grid_spec=pltpu.PrefetchScalarGridSpec(
            num_scalar_prefetch=1,
            grid=(seqs,),
            in_specs=[
                row_spec,
                pl.BlockSpec((1, rows, heads), lambda s, place_ref: (s, 0, 0)),
                row_spec,
                pl.BlockSpec(memory_space=pl.ANY),
            ]
            + [key_spec] * blocks,
            out_specs=[row_spec] + [key_spec] * blocks,
        ),
        out_shape=[jax.ShapeDtypeStruct((tokens, width), LOW)]
        + [jax.ShapeDtypeStruct((tokens, 2 * width), LOW)] * blocks,
        compiler_params=params_of(),
        name="attend_back",
    )(place, projected, log_total, out_grad, after, *key_blocks)


def column_of(table, index):
    lane = lax.broadcasted_iota(jnp.int32, table.shape, 1)
    return jnp.sum(jnp.where(lane == index, table, 0), axis=1, keepdims=True)


def expert_kernel(
    capacity,
    first_ref,
    rank_row_ref,
    rank_col_ref,
    gate_ref,
    rows_ref,
    weight_ref,
    base_ref,
    out_ref,
    gate_part_ref,
    up_part_ref,
    total,
):
    expert = pl.program_id(0)
    tokens = rows_ref.shape[0]
    hidden_width = weight_ref.shape[0] // 3

    @pl.when(expert == 0)
    def _():
        total[...] = base_ref[...]

    number = first_ref[0] + expert
    slot = lax.broadcasted_iota(jnp.int32, (capacity, tokens), 0)
    pick = (slot == rank_row_ref[0]).astype(FULL).astype(LOW)
    picked = dot_nn(pick, rows_ref[...]).astype(LOW)
    gate_part = dot_nt(picked, weight_ref[:hidden_width, :])
    up_part = dot_nt(picked, weight_ref[hidden_width : 2 * hidden_width, :])
    gate_part_ref[0] = gate_part
    up_part_ref[0] = up_part
    hidden = (gate_part * jax.nn.sigmoid(gate_part) * up_part).astype(LOW)
    output = dot_nn(hidden, weight_ref[2 * hidden_width :, :]).astype(LOW)
    rank_col = column_of(rank_col_ref[...], number)
    back = lax.broadcasted_iota(jnp.int32, (tokens, capacity), 1) == rank_col
    spread = dot_nn(back.astype(FULL).astype(LOW), output)
    total[...] += column_of(gate_ref[...], number) * spread

    @pl.when(expert == pl.num_programs(0) - 1)
    def _():
        out_ref[...] = total[...].astype(LOW)


def run_experts(first, rank_rows, rank_cols, gates, rows, weights, base, capacity):
    experts = rank_rows.shape[0]
    tokens = rows.shape[0]
    block = weights.shape[0] // experts
    hidden_width = block // 3
    whole = lambda e, first_ref: (0, 0)
    part = lambda e, first_ref: (e, 0, 0)
    return pl.pallas_call(
        functools.partial(expert_kernel, capacity),
        grid_spec=pltpu.PrefetchScalarGridSpec(
            num_scalar_prefetch=1,
            grid=(experts,),
            in_specs=[
                pl.BlockSpec((1, 1, tokens), part),
                pl.BlockSpec(rank_cols.shape, whole),
                pl.BlockSpec(gates.shape, whole),
                pl.BlockSpec((tokens, D), whole),
                pl.BlockSpec((block, D), lambda e, first_ref: (e, 0)),
                pl.BlockSpec((tokens, D), whole),
            ],
            out_specs=[
                pl.BlockSpec((tokens, D), whole),
                pl.BlockSpec((1, capacity, hidden_width), part),
                pl.BlockSpec((1, capacity, hidden_width), part),
            ],
            scratch_shapes=[pltpu.VMEM((tokens, D), FULL)],
        ),
        out_shape=[
            jax.ShapeDtypeStruct((tokens, D), LOW),
            jax.ShapeDtypeStruct((experts, capacity, hidden_width), FULL),
            jax.ShapeDtypeStruct((experts, capacity, hidden_width), FULL),
        ],
        compiler_params=params_of(),
        name="experts",
    )(first, rank_rows, rank_cols, gates, rows, weights, base)


def expert_back_kernel(
    capacity,
    first_ref,
    rank_row_ref,
    rank_col_ref,
    gate_row_ref,
    rows_ref,
    grad_ref,
    weight_ref,
    gate_part_ref,
    up_part_ref,
    base_ref,
    out_ref,
    weight_grad_ref,
    total,
    gate_total,
):
    expert = pl.program_id(0)
    tokens = rows_ref.shape[0]
    hidden_width = weight_ref.shape[0] // 3
    shards, _, width = weight_grad_ref.shape

    @pl.when(expert == 0)
    def _():
        total[...] = base_ref[...]
        gate_total[...] = jnp.zeros_like(gate_total)

    number = first_ref[0] + expert
    slot = lax.broadcasted_iota(jnp.int32, (capacity, tokens), 0)
    hit = slot == rank_row_ref[0]
    pick = hit.astype(FULL).astype(LOW)
    slot_gate = jnp.sum(jnp.where(hit, gate_row_ref[0], 0.0), axis=1, keepdims=True)
    picked = dot_nn(pick, rows_ref[...]).astype(LOW)
    upstream = dot_nn(pick, grad_ref[...])
    gated = (slot_gate * upstream).astype(LOW)
    gate_part = gate_part_ref[0]
    up_part = up_part_ref[0]
    hidden = (gate_part * jax.nn.sigmoid(gate_part) * up_part).astype(LOW)
    plain = dot_nt(upstream.astype(LOW), weight_ref[2 * hidden_width :, :])
    slot_grad = jnp.sum(hidden.astype(FULL) * plain, axis=1, keepdims=True)
    gate_grad, up_grad = swiglu_grads(gate_part, up_part, slot_gate * plain)
    gate_grad = gate_grad.astype(LOW)
    up_grad = up_grad.astype(LOW)

    def put(start, grads):
        grads = grads.astype(LOW)
        for shard in range(shards):
            weight_grad_ref[shard, start : start + hidden_width, :] = grads[
                :, shard * width : (shard + 1) * width
            ]

    put(0, dot_tn(gate_grad, picked))
    put(hidden_width, dot_tn(up_grad, picked))
    put(2 * hidden_width, dot_tn(hidden, gated))
    row_grad = dot_nn(gate_grad, weight_ref[:hidden_width, :])
    row_grad += dot_nn(up_grad, weight_ref[hidden_width : 2 * hidden_width, :])
    rank_col = column_of(rank_col_ref[...], number)
    back = lax.broadcasted_iota(jnp.int32, (tokens, capacity), 1) == rank_col
    back = back.astype(FULL).astype(LOW)
    total[...] += dot_nn(back, row_grad.astype(LOW))
    lane = lax.broadcasted_iota(jnp.int32, (capacity, gate_total.shape[1]), 1)
    gate_total[...] += dot_nn(back, jnp.where(lane == number, slot_grad, 0.0).astype(LOW))

    @pl.when(expert == pl.num_programs(0) - 1)
    def _():
        out_ref[:, :D] = total[...].astype(LOW)
        out_ref[:, D:] = gate_total[...].astype(LOW)


def run_experts_back(
    first, rank_rows, rank_cols, gate_rows, rows, grads, weights, gate_part, up_part, base,
    capacity, shards, gate_lanes,
):
    experts = rank_rows.shape[0]
    tokens = rows.shape[0]
    block = weights.shape[0] // experts
    hidden_width = block // 3
    whole = lambda e, first_ref: (0, 0)
    part = lambda e, first_ref: (e, 0, 0)
    return pl.pallas_call(
        functools.partial(expert_back_kernel, capacity),
        grid_spec=pltpu.PrefetchScalarGridSpec(
            num_scalar_prefetch=1,
            grid=(experts,),
            in_specs=[
                pl.BlockSpec((1, 1, tokens), part),
                pl.BlockSpec(rank_cols.shape, whole),
                pl.BlockSpec((1, 1, tokens), part),
                pl.BlockSpec((tokens, D), whole),
                pl.BlockSpec((tokens, D), whole),
                pl.BlockSpec((block, D), lambda e, first_ref: (e, 0)),
                pl.BlockSpec((1, capacity, hidden_width), part),
                pl.BlockSpec((1, capacity, hidden_width), part),
                pl.BlockSpec((tokens, D), whole),
            ],
            out_specs=[
                pl.BlockSpec((tokens, D + gate_lanes), whole),
                pl.BlockSpec((shards, block, D // shards), lambda e, first_ref: (0, e, 0)),
            ],
            scratch_shapes=[
                pltpu.VMEM((tokens, D), FULL),
                pltpu.VMEM((tokens, gate_lanes), FULL),
            ],
        ),
        out_shape=[
            jax.ShapeDtypeStruct((tokens, D + gate_lanes), LOW),
            jax.ShapeDtypeStruct((shards, experts * block, D // shards), LOW),
        ],
        compiler_params=params_of(),
        name="experts_back",
    )(first, rank_rows, rank_cols, gate_rows, rows, grads, weights, gate_part, up_part, base)


def head_kernel(valid, rows_ref, table_ref, goal_ref, logit_ref, stat_ref, top, total, goal):
    step = pl.program_id(0)
    tokens = rows_ref.shape[0]
    block = table_ref.shape[0]

    @pl.when(step == 0)
    def _():
        top[...] = jnp.full_like(top, FAR)
        total[...] = jnp.zeros_like(total)
        goal[...] = jnp.zeros_like(goal)

    logits = dot_nt(rows_ref[...], table_ref[...])
    place = step * block + lax.broadcasted_iota(jnp.int32, (tokens, block), 1)
    logits = jnp.where(place < valid, logits, FAR)
    logit_ref[...] = logits
    new_top = jnp.maximum(top[...], jnp.max(logits, axis=1, keepdims=True))
    total[...] = total[...] * jnp.exp(top[...] - new_top) + jnp.sum(
        jnp.exp(logits - new_top), axis=1, keepdims=True
    )
    top[...] = new_top
    goal[...] += jnp.sum(jnp.where(place == goal_ref[...], logits, 0.0), axis=1, keepdims=True)

    @pl.when(step == pl.num_programs(0) - 1)
    def _():
        lane = lax.broadcasted_iota(jnp.int32, (tokens, LANES), 1)
        stat_ref[...] = jnp.where(
            lane == 0, top[...], jnp.where(lane == 1, total[...], goal[...])
        )


def run_head(rows, table, goal_local, valid):
    tokens = rows.shape[0]
    padded = table.shape[0]
    return pl.pallas_call(
        functools.partial(head_kernel, valid),
        grid=(padded // VOCAB_BLOCK,),
        in_specs=[
            pl.BlockSpec((tokens, D), lambda j: (0, 0)),
            pl.BlockSpec((VOCAB_BLOCK, D), lambda j: (j, 0)),
            pl.BlockSpec((tokens, 1), lambda j: (0, 0)),
        ],
        out_specs=[
            pl.BlockSpec((tokens, VOCAB_BLOCK), lambda j: (0, j)),
            pl.BlockSpec((tokens, LANES), lambda j: (0, 0)),
        ],
        out_shape=[
            jax.ShapeDtypeStruct((tokens, padded), FULL),
            jax.ShapeDtypeStruct((tokens, LANES), FULL),
        ],
        scratch_shapes=[pltpu.VMEM((tokens, 1), FULL)] * 3,
        compiler_params=params_of(),
        name="head",
    )(rows, table, goal_local)


def head_back_kernel(
    rows_ref, table_ref, goal_ref, scale_ref, logit_ref, out_ref, table_grad_ref, total
):
    step = pl.program_id(0)
    tokens = rows_ref.shape[0]
    block = table_ref.shape[0]
    shards, _, width = table_grad_ref.shape

    @pl.when(step == 0)
    def _():
        total[...] = jnp.zeros_like(total)

    place = step * block + lax.broadcasted_iota(jnp.int32, (tokens, block), 1)
    share = scale_ref[:, 2:3]
    grads = jnp.exp(logit_ref[...] - scale_ref[:, 0:1]) * scale_ref[:, 1:2]
    grads = (jnp.where(place == goal_ref[...], grads - 1.0, grads) * share).astype(LOW)
    table_part = dot_tn(grads, rows_ref[...]).astype(LOW)
    for shard in range(shards):
        table_grad_ref[shard] = table_part[:, shard * width : (shard + 1) * width]
    total[...] += dot_nn(grads, table_ref[...])

    @pl.when(step == pl.num_programs(0) - 1)
    def _():
        out_ref[...] = total[...].astype(LOW)


def run_head_back(rows, table, goal_local, scales, logits, shards):
    tokens = rows.shape[0]
    padded = table.shape[0]
    return pl.pallas_call(
        head_back_kernel,
        grid=(padded // VOCAB_BLOCK,),
        in_specs=[
            pl.BlockSpec((tokens, D), lambda j: (0, 0)),
            pl.BlockSpec((VOCAB_BLOCK, D), lambda j: (j, 0)),
            pl.BlockSpec((tokens, 1), lambda j: (0, 0)),
            pl.BlockSpec((tokens, 4), lambda j: (0, 0)),
            pl.BlockSpec((tokens, VOCAB_BLOCK), lambda j: (0, j)),
        ],
        out_specs=[
            pl.BlockSpec((tokens, D), lambda j: (0, 0)),
            pl.BlockSpec((shards, VOCAB_BLOCK, D // shards), lambda j: (0, j, 0)),
        ],
        out_shape=[
            jax.ShapeDtypeStruct((tokens, D), LOW),
            jax.ShapeDtypeStruct((shards, padded, D // shards), LOW),
        ],
        scratch_shapes=[pltpu.VMEM((tokens, D), FULL)],
        compiler_params=params_of(),
        name="head_back",
    )(rows, table, goal_local, scales, logits)


def table_step_kernel(
    factor_ref, weight_ref, moment_ref, square_ref, first_ref, second_ref, *out_refs
):
    factor = factor_ref[0]

    def step(grads, rate):
        results = adam_update(
            weight_ref[0], moment_ref[0], square_ref[0], grads * factor, rate, DECAYS[0]
        )
        for ref, value in zip(out_refs, results):
            ref[0] = value

    @pl.when(pl.program_id(0) == 0)
    def _():
        step(first_ref[...], TABLE_RATES[0])

    @pl.when(pl.program_id(0) == 1)
    def _():
        step(second_ref[...].astype(FULL), TABLE_RATES[1])


def table_step(factor, weight, moment, square, first, second):
    vocab, width = weight.shape[1:]
    steps = pl.cdiv(vocab, VOCAB_BLOCK)
    block = pl.BlockSpec((1, VOCAB_BLOCK, width), lambda t, j, factor_ref: (t, j, 0))
    return pl.pallas_call(
        table_step_kernel,
        grid_spec=pltpu.PrefetchScalarGridSpec(
            num_scalar_prefetch=1,
            grid=(2, steps),
            in_specs=[
                block,
                block,
                block,
                pl.BlockSpec(
                    (VOCAB_BLOCK, width),
                    lambda t, j, factor_ref: (jnp.where(t == 0, j, steps - 1), 0),
                ),
                pl.BlockSpec(
                    (VOCAB_BLOCK, width), lambda t, j, factor_ref: (jnp.where(t == 1, j, 0), 0)
                ),
            ],
            out_specs=[block] * 3,
        ),
        out_shape=[jax.ShapeDtypeStruct(weight.shape, FULL)] * 3,
        compiler_params=params_of(2),
        name="table_step",
    )(factor, weight, moment, square, first, second)


def turn_first(item):
    return jnp.moveaxis(item, 0, -1)


def rows_of_attention(item):
    return item.transpose(1, 2, 0).reshape(-1, item.shape[0])


def rows_of_shared(item):
    return item.transpose(1, 2, 0).reshape(-1, item.shape[0])


def rows_of_experts(expert_in, expert_out):
    experts, width, _, hidden_width = expert_in.shape
    return jnp.concatenate(
        [
            expert_in.transpose(0, 2, 3, 1).reshape(experts, 2 * hidden_width, width),
            expert_out.transpose(0, 2, 1),
        ],
        axis=1,
    ).reshape(-1, width)


def shards(
    token_ids,
    target_ids,
    counted,
    routes,
    vocab_tables,
    norm_gains,
    attn_in,
    attention_output_weight,
    router,
    shared_in,
    shared_out,
    expert_in,
    expert_out,
    vocab_tables_moment,
    norm_gains_moment,
    attn_in_moment,
    attn_out_moment,
    router_moment,
    shared_in_moment,
    shared_out_moment,
    expert_in_moment,
    expert_out_moment,
    vocab_tables_square,
    norm_gains_square,
    attn_in_square,
    attn_out_square,
    router_square,
    shared_in_square,
    shared_out_square,
    expert_in_square,
    expert_out_square,
):
    seq_rows, seqs = token_ids.shape
    tokens = seq_rows * seqs
    model_size = lax.axis_size("mp")
    model_place = lax.axis_index("mp")
    data_size = lax.axis_size("dp")
    data_place = lax.axis_index("dp")
    width = vocab_tables.shape[1]
    vocab = vocab_tables.shape[2]
    experts = expert_in.shape[0]
    expert_total = experts * model_size
    capacity = min(2 * tokens * TOPK // expert_total, tokens)
    hidden_width = expert_out.shape[2]
    head_width = attention_output_weight.shape[0]
    shared_width = shared_out.shape[0]
    own = tokens // model_size
    gate_lanes = round_up(expert_total, LANES)
    place = data_place.reshape(1).astype(jnp.int32)

    counts = counted.T.reshape(tokens).astype(FULL)
    small = jnp.concatenate(
        [
            token_ids.T.reshape(tokens).astype(FULL),
            norm_gains.astype(LOW).astype(FULL).reshape(-1),
            jnp.sum(counts).reshape(1),
        ]
    )
    small = jnp.pad(small, (0, round_up(small.shape[0], 1024) - small.shape[0]))
    small = lax.all_gather(small, "dp", axis=0, tiled=False)
    ids = small[:, :tokens].astype(jnp.int32)
    gains = small[:, tokens : tokens + 3 * width].reshape(data_size, 3, width)
    gains = gains.transpose(1, 0, 2).reshape(3, D)
    token_count = jnp.sum(small[:, tokens + 3 * width])

    small_rows = jnp.concatenate(
        [
            rows_of_attention(attn_in),
            attention_output_weight,
            rows_of_shared(shared_in),
            shared_out,
            router.T,
        ]
    ).astype(LOW)
    small_all = lax.all_gather(small_rows, "dp", axis=1, tiled=True)
    expert_all = lax.all_gather(
        rows_of_experts(expert_in, expert_out).astype(LOW), "dp", axis=1, tiled=True
    )
    tables = vocab_tables.transpose(0, 2, 1)
    padded = round_up(vocab, VOCAB_BLOCK)
    table_all = lax.all_gather(
        jnp.pad(tables[1].astype(LOW), ((0, padded - vocab), (0, 0))), "dp", axis=1, tiled=True
    )
    bounds = [0, 3 * head_width, head_width, 2 * shared_width, shared_width, expert_total]
    ends = [sum(bounds[: index + 1]) for index in range(len(bounds))]
    weight_qkv, weight_out, weight_shared_in, weight_shared_out, weight_router = [
        small_all[ends[index] : ends[index + 1]] for index in range(5)
    ]

    local_ids = ids.reshape(data_size, model_size, own).transpose(1, 0, 2).reshape(-1)
    local_ids = local_ids - model_place * vocab
    inside = (local_ids >= 0) & (local_ids < vocab)
    looked_up = lookup(jnp.clip(local_ids, 0, vocab - 1), tables)
    looked_up = jnp.where(inside[:, None], looked_up, 0.0).astype(LOW)
    embedded = sum_rows(looked_up).astype(LOW).reshape(data_size, own, width)
    embedded = lax.all_to_all(embedded, "dp", 0, 0, tiled=True)
    state_zero = embedded.transpose(1, 0, 2).reshape(own, D).astype(FULL)

    first_in = gather_rows(normed(state_zero, gains[0]).astype(LOW))
    projected = dot_nt(first_in, weight_qkv).astype(LOW)
    key_blocks = gather_keys(projected[:, head_width:])
    attended, log_total = attend(place, projected, key_blocks, seqs)
    state_one = state_zero + sum_rows(dot_nn(attended, weight_out).astype(LOW))

    route_rows = routes.transpose(2, 1, 0).reshape(TOPK, tokens)
    expert_ids = jnp.arange(expert_total, dtype=jnp.int32)
    named = jnp.any(route_rows[:, None, :] == expert_ids[None, :, None], axis=0)
    earlier = jnp.arange(tokens)[:, None] < jnp.arange(tokens)[None, :]
    ranks = dot_nn(named.astype(LOW), earlier.astype(LOW)).astype(jnp.int32)
    ranks = jnp.where(named, ranks, -1)
    rank_cols = ranks.T
    first_expert = (model_place * experts).reshape(1).astype(jnp.int32)
    local_rows = lambda table: lax.dynamic_slice_in_dim(table, model_place * experts, experts, 0)[
        :, None, :
    ]
    rank_rows = local_rows(ranks)
    second_in = gather_rows(normed(state_one, gains[1]).astype(LOW))
    router_logits = dot_nt(second_in, weight_router)
    gates = jax.nn.softmax(jnp.where(named.T, router_logits, FAR), axis=1)
    gates = jnp.where(named.T, gates, 0.0)
    gate_rows = local_rows(gates.T)
    shared_both = dot_nt(second_in, weight_shared_in)
    shared_gate, shared_up = shared_both[:, :shared_width], shared_both[:, shared_width:]
    shared_hidden = (jax.nn.silu(shared_gate) * shared_up).astype(LOW)
    shared_part = dot_nn(shared_hidden, weight_shared_out)
    moe_part, gate_part, up_part = run_experts(
        first_expert, rank_rows, rank_cols, gates, second_in, expert_all, shared_part, capacity
    )
    state_two = state_one + sum_rows(moe_part)

    third_in = gather_rows(normed(state_two, gains[2]).astype(LOW))
    goal_local = (target_ids.T.reshape(tokens, 1) - model_place * vocab).astype(jnp.int32)
    goal_local = jnp.where(goal_local < vocab, goal_local, -1)
    logits, stats = run_head(third_in, table_all, goal_local, vocab)
    stats = lax.all_gather(stats[:, :3].T, "mp", axis=0, tiled=False)
    top = jnp.max(stats[:, 0], axis=0)
    log_head = top + jnp.log(jnp.sum(stats[:, 1] * jnp.exp(stats[:, 0] - top), axis=0))
    goal_logit = jnp.sum(stats[:, 2], axis=0)
    loss_part = jnp.sum(counts * (log_head - goal_logit + Z_COEF * log_head * log_head))
    scales = jnp.stack(
        [log_head, 1.0 + 2.0 * Z_COEF * log_head, counts / token_count, counts], axis=1
    )
    third_part, table_part = run_head_back(
        third_in, table_all, goal_local, scales, logits, data_size
    )
    table_second = lax.psum_scatter(table_part, "dp", scatter_dimension=0, tiled=False)
    state_two_grad, gain_three = norm_back(state_two, gains[2], sum_rows(third_part))

    two_low = gather_rows(state_two_grad.astype(LOW))
    shared_out_grad = dot_tn(shared_hidden, two_low)
    shared_gate_grad, shared_up_grad = swiglu_grads(
        shared_gate, shared_up, dot_nt(two_low, weight_shared_out)
    )
    shared_both_grad = jnp.concatenate([shared_gate_grad, shared_up_grad], axis=1).astype(LOW)
    shared_in_grad = dot_tn(shared_both_grad, second_in)
    second_part, expert_part = run_experts_back(
        first_expert, rank_rows, rank_cols, gate_rows, second_in, two_low, expert_all, gate_part,
        up_part, dot_nn(shared_both_grad, weight_shared_in), capacity, data_size, gate_lanes,
    )
    expert_grad = lax.psum_scatter(expert_part, "dp", scatter_dimension=0, tiled=False)
    second_sum = sum_rows(second_part)
    second_grad = second_sum[:, :D]
    gate_grad = second_sum[:, D : D + expert_total]
    own_gates = lax.dynamic_slice_in_dim(gates, model_place * own, own, 0)
    choice_grad = own_gates * (
        gate_grad - jnp.sum(own_gates * gate_grad, axis=1, keepdims=True)
    )
    choice_grad = choice_grad.astype(LOW)
    second_grad = second_grad + dot_nn(choice_grad, weight_router)
    norm_grad, gain_two = norm_back(state_one, gains[1], second_grad)
    state_one_grad = state_two_grad + norm_grad

    sent = jnp.concatenate(
        [
            state_one_grad.astype(LOW),
            jnp.pad(choice_grad, ((0, 0), (0, gate_lanes - expert_total))),
        ],
        axis=1,
    )
    sent = gather_rows(sent)
    one_low = sent[:, :D]
    router_grad = dot_tn(sent[:, D : D + expert_total], second_in)
    attn_out_grad = dot_tn(attended, one_low)
    out_grad = dot_nt(one_low, weight_out).astype(LOW)
    query_grad, *key_parts = attend_back(
        place, projected, log_total, out_grad, key_blocks, seqs, table_second
    )
    key_grad = scatter_keys(key_parts).astype(LOW)
    projected_grad = jnp.concatenate([query_grad, key_grad], axis=1)
    first_part = dot_nn(projected_grad, weight_qkv).astype(LOW)
    attn_in_grad = dot_tn(projected_grad, first_in)
    small_part = jnp.concatenate(
        [attn_in_grad, attn_out_grad, shared_in_grad, shared_out_grad, router_grad]
    ).astype(LOW)
    small_part = small_part.reshape(-1, data_size, width).transpose(1, 0, 2)
    norm_grad, gain_one = norm_back(state_zero, gains[0], sum_rows(first_part))
    state_zero_grad = state_one_grad + norm_grad

    gain_pad = 16
    gain_part = jnp.stack([gain_one, gain_two, gain_three]).astype(LOW)
    gain_part = jnp.pad(gain_part, ((0, gain_pad - 3), (0, 0)))
    back_rows = jnp.concatenate([state_zero_grad.astype(LOW), gain_part])
    back_rows = back_rows.reshape(own + gain_pad, data_size, width).transpose(1, 0, 2)
    back_rows = lax.all_to_all(back_rows, "dp", 0, 0, tiled=True)
    back_rows = gather_rows(back_rows)
    small_part, expert_grad, back_rows = lax.optimization_barrier(
        (small_part, expert_grad, back_rows)
    )
    small_grad = lax.psum_scatter(small_part, "dp", scatter_dimension=0, tiled=False)
    gain_grad = jnp.sum(back_rows[:, own : own + 3].astype(FULL), axis=0)
    table_first = table_grad(local_ids, back_rows[:, :own].reshape(-1, width), vocab, expert_grad)

    table_second = table_second[:vocab]
    small_grad = small_grad.astype(FULL)
    expert_grad = expert_grad.reshape(experts, 3 * hidden_width, width)
    shared_end = ends[4]
    square = lambda item: jnp.sum(jnp.square(item.astype(FULL)))
    local_square = (
        square(table_first)
        + square(table_second)
        + square(expert_grad)
        + square(small_grad[:shared_end])
        + (square(small_grad[shared_end:]) + square(gain_grad)) / model_size
    )
    sums = lax.psum(jnp.stack([local_square, loss_part / model_size]), ("dp", "mp"))
    grad_norm = jnp.sqrt(sums[0])
    factor = CLIP / jnp.maximum(grad_norm, CLIP)

    table_results = table_step(
        factor.reshape(1),
        tables,
        vocab_tables_moment.transpose(0, 2, 1),
        vocab_tables_square.transpose(0, 2, 1),
        table_first,
        table_second,
    )
    results = [sums[1], token_count, grad_norm]
    results.extend(item.transpose(0, 2, 1) for item in table_results)
    small_grads = [small_grad[ends[index] : ends[index + 1]] for index in range(5)]
    gradients = (
        gain_grad,
        small_grads[0].reshape(3, head_width, width).transpose(2, 0, 1),
        small_grads[1],
        small_grads[4].T,
        small_grads[2].reshape(2, shared_width, width).transpose(2, 0, 1),
        small_grads[3],
        expert_grad[:, : 2 * hidden_width]
        .astype(FULL)
        .reshape(experts, 2, hidden_width, width)
        .transpose(0, 3, 1, 2),
        expert_grad[:, 2 * hidden_width :].astype(FULL).transpose(0, 2, 1),
    )
    params = (
        norm_gains, attn_in, attention_output_weight, router, shared_in, shared_out, expert_in,
        expert_out,
    )
    moments = (
        norm_gains_moment, attn_in_moment, attn_out_moment, router_moment, shared_in_moment,
        shared_out_moment, expert_in_moment, expert_out_moment,
    )
    squares = (
        norm_gains_square, attn_in_square, attn_out_square, router_square, shared_in_square,
        shared_out_square, expert_in_square, expert_out_square,
    )
    for index in range(8):
        results.extend(
            adam_update(
                params[index],
                moments[index],
                squares[index],
                gradients[index] * factor,
                RATES[index + 1],
                DECAYS[index + 1],
            )
        )
    return tuple(results)


def solution(mesh):
    in_specs = (
        P("dp", None),
        P("dp", None),
        P("dp", None),
        P("dp", None, None),
        P(None, "dp", "mp"),
        P(None, "dp"),
        P("dp", None, "mp"),
        P("mp", "dp"),
        P("dp", None),
        P("dp", None, "mp"),
        P("mp", "dp"),
        P("mp", "dp", None, None),
        P("mp", "dp", None),
        P(None, "dp", "mp"),
        P(None, "dp"),
        P("dp", None, "mp"),
        P("mp", "dp"),
        P("dp", None),
        P("dp", None, "mp"),
        P("mp", "dp"),
        P("mp", "dp", None, None),
        P("mp", "dp", None),
        P(None, "dp", "mp"),
        P(None, "dp"),
        P("dp", None, "mp"),
        P("mp", "dp"),
        P("dp", None),
        P("dp", None, "mp"),
        P("mp", "dp"),
        P("mp", "dp", None, None),
        P("mp", "dp", None),
    )
    out_specs = (
        P(),
        P(),
        P(),
        P(None, "dp", "mp"),
        P(None, "dp", "mp"),
        P(None, "dp", "mp"),
        P(None, "dp"),
        P(None, "dp"),
        P(None, "dp"),
        P("dp", None, "mp"),
        P("dp", None, "mp"),
        P("dp", None, "mp"),
        P("mp", "dp"),
        P("mp", "dp"),
        P("mp", "dp"),
        P("dp", None),
        P("dp", None),
        P("dp", None),
        P("dp", None, "mp"),
        P("dp", None, "mp"),
        P("dp", None, "mp"),
        P("mp", "dp"),
        P("mp", "dp"),
        P("mp", "dp"),
        P("mp", "dp", None, None),
        P("mp", "dp", None, None),
        P("mp", "dp", None, None),
        P("mp", "dp", None),
        P("mp", "dp", None),
        P("mp", "dp", None),
    )
    return jax.shard_map(shards, mesh=mesh, in_specs=in_specs, out_specs=out_specs, check_vma=False)
```

```python
import functools

import jax
import jax.numpy as jnp
from jax import lax
from jax.experimental import pallas as pl
from jax.experimental.pallas import tpu as pltpu
from jax.sharding import PartitionSpec as P

D = 1024
HD = 128
TOPK = 6
STEP = 10
LANES = 128
VOCAB_BLOCK = 1024
STEP_BLOCK = 2048
VMEM_BYTES = 50 * 1024 * 1024

NORM_EPS = 1e-06
Z_COEF = 0.01
CLIP = 0.01
BETA_ONE = 0.9
BETA_TWO = 0.95
ADAM_EPS = 1e-08
TABLE_RATES = (1.0, 0.06)
RATES = (0.0, 1.0, 0.02, 0.05, 0.01, 0.02, 0.02, 0.02, 0.02)
DECAYS = (0.1, 0.0, 0.1, 0.1, 0.1, 0.1, 0.1, 0.1, 0.1)
FAR = -1e30
LOW = jnp.bfloat16
FULL = jnp.float32


def dot_nn(left, right):
    return lax.dot_general(left, right, (((1,), (0,)), ((), ())), preferred_element_type=FULL)


def dot_nt(left, right):
    return lax.dot_general(left, right, (((1,), (1,)), ((), ())), preferred_element_type=FULL)


def dot_tn(left, right):
    return lax.dot_general(left, right, (((0,), (0,)), ((), ())), preferred_element_type=FULL)


def params_of(dims=1):
    return pltpu.CompilerParams(
        dimension_semantics=("arbitrary",) * dims, vmem_limit_bytes=VMEM_BYTES
    )


def round_up(number, unit):
    return (number + unit - 1) // unit * unit


def normed(values, gain_row):
    return (
        values * lax.rsqrt(jnp.mean(values * values, axis=-1, keepdims=True) + NORM_EPS) * gain_row
    )


def norm_back(values, gain_row, upstream):
    inv_rms = lax.rsqrt(jnp.mean(values * values, axis=-1, keepdims=True) + NORM_EPS)
    unit_rows = values * inv_rms
    scaled = upstream * gain_row
    gain_grad = jnp.sum(upstream * unit_rows, axis=0)
    return (
        inv_rms * (scaled - unit_rows * jnp.mean(scaled * unit_rows, axis=-1, keepdims=True)),
        gain_grad,
    )


def swiglu_grads(gate_part, up_part, upstream):
    sigmoid_gate = jax.nn.sigmoid(gate_part)
    silu_gate = gate_part * sigmoid_gate
    gate_grad = upstream * up_part * sigmoid_gate * (1.0 + gate_part * (1.0 - sigmoid_gate))
    return gate_grad, upstream * silu_gate


def adam_update(weight, moment, square, grad_item, rate, decay):
    new_moment = BETA_ONE * moment + (1.0 - BETA_ONE) * grad_item
    new_square = BETA_TWO * square + (1.0 - BETA_TWO) * grad_item * grad_item
    step_ratio = (new_moment * (1.0 / (1.0 - BETA_ONE**STEP))) / (
        jnp.sqrt(new_square * (1.0 / (1.0 - BETA_TWO**STEP))) + ADAM_EPS
    )
    return (weight - rate * (step_ratio + decay * weight), new_moment, new_square)


def sum_rows(partial):
    size = lax.axis_size("mp")
    place = lax.axis_index("mp")
    pieces = partial.reshape((size, partial.shape[0] // size) + partial.shape[1:])
    total = lax.dynamic_index_in_dim(pieces, place, 0, keepdims=False).astype(FULL)
    for step in range(1, size):
        sent = lax.dynamic_index_in_dim(pieces, (place + step) % size, 0, keepdims=False)
        got = lax.ppermute(sent, "mp", [(i, (i + step) % size) for i in range(size)])
        total = total + got.astype(FULL)
    return total


def gather_rows(rows):
    size = lax.axis_size("mp")
    place = lax.axis_index("mp")
    count = rows.shape[0]
    whole = jnp.zeros((size * count,) + rows.shape[1:], rows.dtype)
    rest = (0,) * (rows.ndim - 1)
    whole = lax.dynamic_update_slice(whole, rows, (place * count,) + rest)
    for step in range(1, size):
        got = lax.ppermute(rows, "mp", [(i, (i + step) % size) for i in range(size)])
        whole = lax.dynamic_update_slice(whole, got, ((place - step) % size * count,) + rest)
    return whole


def swap(item, mask):
    size = lax.axis_size("dp")
    return lax.ppermute(item, "dp", [(i, i ^ mask) for i in range(size)])


def chips_of(size):
    return [list(range(core, size, 2)) for core in range(2)]


def core_place():
    return lax.axis_index("dp") % 2


def pair_rows(rows):
    return jnp.concatenate([rows, swap(rows, 1)])


def sum_pair(partial):
    count = partial.shape[0] // 2
    return (partial[:count].astype(FULL) + swap(partial[count:], 1).astype(FULL)).astype(LOW)


def in_order(mine, other, axis):
    first = core_place() == 0
    return jnp.concatenate(
        [jnp.where(first, mine, other), jnp.where(first, other, mine)], axis=axis
    )


def own_half(rows):
    halves = rows.reshape(2, -1, rows.shape[-1])
    place = core_place()
    mine = lax.dynamic_index_in_dim(halves, place, 0, keepdims=False)
    return mine, swap(lax.dynamic_index_in_dim(halves, 1 - place, 0, keepdims=False), 1)


def gather_half(halves):
    size = lax.axis_size("dp")
    return lax.all_gather(
        in_order(*halves, 1), "dp", axis=1, tiled=True, axis_index_groups=chips_of(size)
    )


def scatter_half(grads):
    size = lax.axis_size("dp")
    part = lax.psum_scatter(
        grads, "dp", scatter_dimension=0, tiled=False, axis_index_groups=chips_of(size)
    )
    return lax.optimization_barrier(part)


def halves_back(part):
    width = part.shape[1] // 2
    place = core_place()
    mine = lax.dynamic_slice_in_dim(part, place * width, width, 1)
    return mine, swap(lax.dynamic_slice_in_dim(part, (1 - place) * width, width, 1), 1)


def by_place(pieces):
    place = lax.axis_index("dp")
    stacked = jnp.stack(pieces)
    return [
        lax.dynamic_index_in_dim(stacked, jnp.bitwise_xor(place, index), 0, keepdims=False)
        for index in range(len(pieces))
    ]


def scatter_features(grads):
    size = lax.axis_size("dp")
    place = lax.axis_index("dp")
    width = grads.shape[1] // size
    pieces = grads.astype(LOW).reshape(-1, size, width).transpose(1, 0, 2)
    return scatter_blocks(
        [
            lax.dynamic_index_in_dim(pieces, jnp.bitwise_xor(place, mask), 0, keepdims=False)
            for mask in range(size)
        ],
        False,
    )


def tree_sum(items):
    while len(items) > 1:
        items = [items[index] + items[index + 1] for index in range(0, len(items), 2)]
    return items[0]


def add_all(item):
    item = item + swap(item, 1)
    item = tree_sum([item] + [swap(item, mask) for mask in range(2, lax.axis_size("dp"), 2)])
    size = lax.axis_size("mp")
    return tree_sum(
        [item]
        + [
            lax.ppermute(item, "mp", [(i, i ^ mask) for i in range(size)])
            for mask in range(1, size)
        ]
    )


def send_blocks(item, mask, keep):
    size = lax.axis_size("dp")
    return lax.ppermute(item, "dp", [(i, i ^ mask) for i in range(size) if keep(i)])


def gather_blocks(item, causal):
    both = []
    for mask in range(0, lax.axis_size("dp"), 2):
        block, keep = item, lambda i: not causal or i % 2 == 0
        if mask > 0:
            block = send_blocks(item, mask, lambda i: not causal or i ^ mask > i)
            keep = lambda i: not causal or i ^ mask < i
        both.extend([block, send_blocks(block, 1, keep)])
    return both


def scatter_blocks(blocks, causal):
    total = None
    for mask in range(0, lax.axis_size("dp"), 2):
        keep = lambda i: not causal or (i ^ mask < i if mask > 0 else i % 2 == 1)
        pair = blocks[mask].astype(FULL) + send_blocks(blocks[mask + 1], 1, keep).astype(FULL)
        if mask > 0:
            keep = lambda i: not causal or i ^ mask < i
            pair = send_blocks(pair.astype(LOW), mask, keep).astype(FULL)
        total = pair if total is None else total + pair
    return total


def lookup_kernel(ids_ref, table_ref, out_ref):
    base = pl.program_id(0) * out_ref.shape[0]

    def copy_rows(step, carry):
        for inner in range(8):
            row = step * 8 + inner
            out_ref[pl.ds(row, 1), :] = table_ref[0, pl.ds(ids_ref[base + row], 1), :]
        return carry

    lax.fori_loop(0, out_ref.shape[0] // 8, copy_rows, 0)


def lookup(ids, tables):
    count = ids.shape[0]
    vocab, width = tables.shape[1:]
    block = 512
    return pl.pallas_call(
        lookup_kernel,
        grid_spec=pltpu.PrefetchScalarGridSpec(
            num_scalar_prefetch=1,
            grid=(count // block,),
            in_specs=[pl.BlockSpec((1, vocab, width), lambda i, ids_ref: (0, 0, 0))],
            out_specs=pl.BlockSpec((block, width), lambda i, ids_ref: (i, 0)),
        ),
        out_shape=jax.ShapeDtypeStruct((count, width), FULL),
        compiler_params=params_of(),
        name="lookup",
    )(ids, tables)


def table_grad_kernel(ids_ref, rows_ref, after_ref, out_ref):
    del after_ref
    block = out_ref.shape[0]
    span = 512
    first = pl.program_id(0) * block
    token_of = first + lax.broadcasted_iota(jnp.int32, (block, span), 0)
    total = jnp.zeros(out_ref.shape, FULL)
    for start in range(0, rows_ref.shape[0], span):
        hit = (token_of == ids_ref[:, start : start + span]).astype(FULL).astype(LOW)
        total = total + dot_nn(hit, rows_ref[start : start + span, :])
    out_ref[...] = total


def table_grad(ids, rows, vocab, after):
    count, width = rows.shape
    return pl.pallas_call(
        table_grad_kernel,
        grid=(pl.cdiv(vocab, VOCAB_BLOCK),),
        in_specs=[
            pl.BlockSpec((1, count), lambda j: (0, 0)),
            pl.BlockSpec((count, width), lambda j: (0, 0)),
            pl.BlockSpec(memory_space=pl.ANY),
        ],
        out_specs=pl.BlockSpec((VOCAB_BLOCK, width), lambda j: (j, 0)),
        out_shape=jax.ShapeDtypeStruct((vocab, width), FULL),
        compiler_params=params_of(),
        name="table_grad",
    )(ids.reshape(1, count), rows, after)


def masked_scores(place, query, keys, rows, blocks):
    scores = dot_nt(query, keys) * HD ** (-0.5)
    offset = lax.broadcasted_iota(jnp.int32, (1, rows), 1)
    key_pos = jnp.concatenate(
        [jnp.bitwise_xor(place, mask) * rows + offset for mask in range(blocks)], axis=1
    )
    query_pos = place * rows + lax.broadcasted_iota(jnp.int32, (rows, 1), 0)
    return jnp.where(key_pos <= query_pos, scores, FAR)


def head_cols(refs, index):
    return jnp.concatenate([ref[:, index * HD : (index + 1) * HD] for ref in refs], axis=0)


def attend_kernel(blocks, place_ref, query_ref, *refs):
    key_refs = refs[:blocks]
    out_ref, log_ref = refs[blocks:]
    place = place_ref[0]
    rows, width = query_ref.shape
    heads = width // HD
    for head in range(heads):
        cols = slice(head * HD, (head + 1) * HD)
        keys = head_cols(key_refs, head)
        values = head_cols(key_refs, heads + head)
        scores = masked_scores(place, query_ref[:, cols], keys, rows, blocks)
        top = jnp.max(scores, axis=1, keepdims=True)
        powers = jnp.exp(scores - top)
        total = jnp.sum(powers, axis=1, keepdims=True)
        probs = (powers * (1.0 / total)).astype(LOW)
        out_ref[:, cols] = dot_nn(probs, values).astype(LOW)
        log_ref[0, :, head : head + 1] = top + jnp.log(total)


def attend(place, projected, key_blocks, seqs):
    blocks = len(key_blocks)
    tokens = projected.shape[0]
    rows = tokens // seqs
    width = projected.shape[1] // 3
    heads = width // HD
    return pl.pallas_call(
        functools.partial(attend_kernel, blocks),
        grid_spec=pltpu.PrefetchScalarGridSpec(
            num_scalar_prefetch=1,
            grid=(seqs,),
            in_specs=[pl.BlockSpec((rows, width), lambda s, place_ref: (s, 0))]
            + [pl.BlockSpec((rows, 2 * width), lambda s, place_ref: (s, 0))] * blocks,
            out_specs=[
                pl.BlockSpec((rows, width), lambda s, place_ref: (s, 0)),
                pl.BlockSpec((1, rows, heads), lambda s, place_ref: (s, 0, 0)),
            ],
        ),
        out_shape=[
            jax.ShapeDtypeStruct((tokens, width), LOW),
            jax.ShapeDtypeStruct((seqs, rows, heads), FULL),
        ],
        compiler_params=params_of(),
        name="attend",
    )(place, projected, *key_blocks)


def attend_back_kernel(blocks, place_ref, query_ref, log_ref, grad_ref, after_ref, *refs):
    del after_ref
    key_refs = refs[:blocks]
    query_grad_ref = refs[blocks]
    key_grad_refs = refs[blocks + 1 :]
    place = place_ref[0]
    rows, width = query_ref.shape
    heads = width // HD
    for head in range(heads):
        cols = slice(head * HD, (head + 1) * HD)
        keys = head_cols(key_refs, head)
        values = head_cols(key_refs, heads + head)
        query = query_ref[:, cols]
        out_grad = grad_ref[:, cols]
        scores = masked_scores(place, query, keys, rows, blocks)
        probs = jnp.exp(scores - log_ref[0, :, head : head + 1])
        prob_grad = dot_nt(out_grad, values)
        delta = jnp.sum(probs * prob_grad, axis=1, keepdims=True)
        score_grad = (probs * (prob_grad - delta)).astype(LOW)
        query_grad_ref[:, cols] = (dot_nn(score_grad, keys) * HD ** (-0.5)).astype(LOW)
        key_grad = (dot_tn(score_grad, query) * HD ** (-0.5)).astype(LOW)
        value_grad = dot_tn(probs.astype(LOW), out_grad).astype(LOW)
        value_cols = slice((heads + head) * HD, (heads + head + 1) * HD)
        for mask in range(blocks):
            part = slice(mask * rows, (mask + 1) * rows)
            key_grad_refs[mask][:, cols] = key_grad[part]
            key_grad_refs[mask][:, value_cols] = value_grad[part]


def attend_back(place, projected, log_total, out_grad, key_blocks, seqs, after):
    blocks = len(key_blocks)
    tokens = projected.shape[0]
    rows = tokens // seqs
    width = projected.shape[1] // 3
    heads = width // HD
    row_spec = pl.BlockSpec((rows, width), lambda s, place_ref: (s, 0))
    key_spec = pl.BlockSpec((rows, 2 * width), lambda s, place_ref: (s, 0))
    return pl.pallas_call(
        functools.partial(attend_back_kernel, blocks),
        grid_spec=pltpu.PrefetchScalarGridSpec(
            num_scalar_prefetch=1,
            grid=(seqs,),
            in_specs=[
                row_spec,
                pl.BlockSpec((1, rows, heads), lambda s, place_ref: (s, 0, 0)),
                row_spec,
                pl.BlockSpec(memory_space=pl.ANY),
            ]
            + [key_spec] * blocks,
            out_specs=[row_spec] + [key_spec] * blocks,
        ),
        out_shape=[jax.ShapeDtypeStruct((tokens, width), LOW)]
        + [jax.ShapeDtypeStruct((tokens, 2 * width), LOW)] * blocks,
        compiler_params=params_of(),
        name="attend_back",
    )(place, projected, log_total, out_grad, after, *key_blocks)


def column_of(table, index):
    lane = lax.broadcasted_iota(jnp.int32, table.shape, 1)
    return jnp.sum(jnp.where(lane == index, table, 0), axis=1, keepdims=True)


def swiglu_low(gate_part, up_part):
    return (gate_part * jax.nn.sigmoid(gate_part) * up_part).astype(LOW)


def expert_kernel(
    capacity,
    experts,
    shared_width,
    first_ref,
    rank_row_ref,
    rank_col_ref,
    gate_ref,
    mine_ref,
    other_ref,
    weight_ref,
    out_ref,
    gate_part_ref,
    up_part_ref,
    total,
):
    expert = pl.program_id(0)
    row_refs = (mine_ref, other_ref)
    tokens = mine_ref.shape[0]
    blocks = [slice(index * tokens, (index + 1) * tokens) for index in range(2)]
    hidden_width = weight_ref.shape[0] // 3

    @pl.when(expert == 0)
    def _():
        total[...] = jnp.zeros_like(total)

    @pl.when(expert < experts)
    def _():
        number = first_ref[0] + expert
        slot = lax.broadcasted_iota(jnp.int32, (capacity, tokens), 0)
        parts = []
        for block, rows_ref in zip(blocks, row_refs):
            pick = (slot == rank_row_ref[0, :, block]).astype(FULL).astype(LOW)
            parts.append(dot_nn(pick, rows_ref[...]).astype(LOW))
        picked = jnp.concatenate(parts)
        gate_part = dot_nt(picked, weight_ref[:hidden_width, :])
        up_part = dot_nt(picked, weight_ref[hidden_width : 2 * hidden_width, :])
        gate_part_ref[0] = gate_part
        up_part_ref[0] = up_part
        hidden = swiglu_low(gate_part, up_part)
        output = dot_nn(hidden, weight_ref[2 * hidden_width :, :]).astype(LOW)
        for index, block in enumerate(blocks):
            rank_col = column_of(rank_col_ref[block, :], number)
            back = lax.broadcasted_iota(jnp.int32, (tokens, capacity), 1) == rank_col
            spread = dot_nn(
                back.astype(FULL).astype(LOW), output[index * capacity : (index + 1) * capacity]
            )
            total[block, :] += column_of(gate_ref[block, :], number) * spread

    @pl.when(expert == experts)
    def _():
        for block, rows_ref in zip(blocks, row_refs):
            rows = rows_ref[...]
            gate_part = dot_nt(rows, weight_ref[:shared_width, :])
            up_part = dot_nt(rows, weight_ref[shared_width : 2 * shared_width, :])
            hidden = swiglu_low(gate_part, up_part)
            part = dot_nn(hidden, weight_ref[2 * shared_width : 3 * shared_width, :])
            out_ref[block, :] = (total[block, :] + part).astype(LOW)


def expert_specs(experts, hidden_width, slots, tokens):
    whole = lambda e, first_ref: (0, 0)
    fixed = lambda item: pl.BlockSpec(item.shape, whole, pipeline_mode=pl.Buffered(1))
    part = lambda e, first_ref: (jnp.minimum(e, experts - 1), 0, 0)
    return (
        whole,
        fixed,
        pl.BlockSpec((1, 1, tokens), part),
        pl.BlockSpec((3 * hidden_width, D), lambda e, first_ref: (e, 0)),
        pl.BlockSpec((1, slots, hidden_width), part),
    )


def run_experts(
    first, rank_rows, rank_cols, gates, mine, other, weights, capacity, hidden_width, shared_width
):
    experts = rank_rows.shape[0]
    tokens = 2 * mine.shape[0]
    slots = 2 * capacity
    whole, fixed, row_spec, weight_spec, part_spec = expert_specs(
        experts, hidden_width, slots, tokens
    )
    return pl.pallas_call(
        functools.partial(expert_kernel, capacity, experts, shared_width),
        grid_spec=pltpu.PrefetchScalarGridSpec(
            num_scalar_prefetch=1,
            grid=(experts + 1,),
            in_specs=[
                row_spec,
                fixed(rank_cols),
                fixed(gates),
                fixed(mine),
                fixed(other),
                weight_spec,
            ],
            out_specs=[pl.BlockSpec((tokens, D), whole), part_spec, part_spec],
            scratch_shapes=[pltpu.VMEM((tokens, D), FULL)],
        ),
        out_shape=[
            jax.ShapeDtypeStruct((tokens, D), LOW),
            jax.ShapeDtypeStruct((experts, slots, hidden_width), FULL),
            jax.ShapeDtypeStruct((experts, slots, hidden_width), FULL),
        ],
        compiler_params=params_of(),
        name="experts",
    )(first, rank_rows, rank_cols, gates, mine, other, weights)


def expert_back_kernel(
    capacity,
    experts,
    shared_width,
    first_ref,
    rank_row_ref,
    rank_col_ref,
    gate_row_ref,
    mine_ref,
    other_ref,
    mine_grad_ref,
    other_grad_ref,
    weight_ref,
    gate_part_ref,
    up_part_ref,
    out_ref,
    weight_grad_ref,
    total,
    gate_total,
):
    expert = pl.program_id(0)
    row_refs = (mine_ref, other_ref)
    grad_refs = (mine_grad_ref, other_grad_ref)
    tokens = mine_ref.shape[0]
    blocks = [slice(index * tokens, (index + 1) * tokens) for index in range(2)]
    hidden_width = weight_ref.shape[0] // 3
    shards, _, width = weight_grad_ref.shape

    @pl.when(expert == 0)
    def _():
        total[...] = jnp.zeros_like(total)
        gate_total[...] = jnp.zeros_like(gate_total)

    def put(start, grads):
        grads = grads.astype(LOW)
        for shard in range(shards):
            weight_grad_ref[shard, start : start + grads.shape[0], :] = grads[
                :, shard * width : (shard + 1) * width
            ]

    @pl.when(expert < experts)
    def _():
        number = first_ref[0] + expert
        slot = lax.broadcasted_iota(jnp.int32, (capacity, tokens), 0)
        slot_gates, parts, grad_parts = [], [], []
        for block, rows_ref, grad_ref in zip(blocks, row_refs, grad_refs):
            hit = slot == rank_row_ref[0, :, block]
            pick = hit.astype(FULL).astype(LOW)
            slot_gates.append(
                jnp.sum(jnp.where(hit, gate_row_ref[0, :, block], 0.0), axis=1, keepdims=True)
            )
            parts.append(dot_nn(pick, rows_ref[...]).astype(LOW))
            grad_parts.append(dot_nn(pick, grad_ref[...]))
        slot_gate = jnp.concatenate(slot_gates)
        picked = jnp.concatenate(parts)
        upstream = jnp.concatenate(grad_parts)
        gated = (slot_gate * upstream).astype(LOW)
        gate_part = gate_part_ref[0]
        up_part = up_part_ref[0]
        hidden = swiglu_low(gate_part, up_part)
        plain = dot_nt(upstream.astype(LOW), weight_ref[2 * hidden_width :, :])
        slot_grad = jnp.sum(hidden.astype(FULL) * plain, axis=1, keepdims=True)
        gate_grad, up_grad = swiglu_grads(gate_part, up_part, slot_gate * plain)
        gate_grad = gate_grad.astype(LOW)
        up_grad = up_grad.astype(LOW)
        put(0, dot_tn(gate_grad, picked))
        put(hidden_width, dot_tn(up_grad, picked))
        put(2 * hidden_width, dot_tn(hidden, gated))
        row_grad = dot_nn(gate_grad, weight_ref[:hidden_width, :])
        row_grad += dot_nn(up_grad, weight_ref[hidden_width : 2 * hidden_width, :])
        row_grad = row_grad.astype(LOW)
        lane = lax.broadcasted_iota(jnp.int32, (picked.shape[0], gate_total.shape[1]), 1)
        slot_grad = jnp.where(lane == number, slot_grad, 0.0).astype(LOW)
        for index, block in enumerate(blocks):
            rank_col = column_of(rank_col_ref[block, :], number)
            back = lax.broadcasted_iota(jnp.int32, (tokens, capacity), 1) == rank_col
            back = back.astype(FULL).astype(LOW)
            part = slice(index * capacity, (index + 1) * capacity)
            total[block, :] += dot_nn(back, row_grad[part])
            gate_total[block, :] += dot_nn(back, slot_grad[part])

    @pl.when(expert == experts)
    def _():
        weight_gate = weight_ref[:shared_width, :]
        weight_up = weight_ref[shared_width : 2 * shared_width, :]
        weight_down = weight_ref[2 * shared_width : 3 * shared_width, :]
        sums = [0.0, 0.0, 0.0]
        for block, rows_ref, grad_ref in zip(blocks, row_refs, grad_refs):
            rows = rows_ref[...]
            grads = grad_ref[...]
            gate_part = dot_nt(rows, weight_gate)
            up_part = dot_nt(rows, weight_up)
            hidden = swiglu_low(gate_part, up_part)
            gate_grad, up_grad = swiglu_grads(gate_part, up_part, dot_nt(grads, weight_down))
            gate_grad = gate_grad.astype(LOW)
            up_grad = up_grad.astype(LOW)
            pairs = ((gate_grad, rows), (up_grad, rows), (hidden, grads))
            sums = [item + dot_tn(*pair) for item, pair in zip(sums, pairs)]
            row_grad = dot_nn(gate_grad, weight_gate) + dot_nn(up_grad, weight_up)
            out_ref[block, :D] = (total[block, :] + row_grad).astype(LOW)
        for index, item in enumerate(sums):
            put(index * shared_width, item)
        out_ref[:, D:] = gate_total[...].astype(LOW)


def run_experts_back(
    first, rank_rows, rank_cols, gate_rows, mine, other, mine_grad, other_grad, weights,
    gate_part, up_part, capacity, hidden_width, shared_width, shards, gate_lanes,
):
    experts = rank_rows.shape[0]
    tokens = 2 * mine.shape[0]
    slots = 2 * capacity
    whole, fixed, row_spec, weight_spec, part_spec = expert_specs(
        experts, hidden_width, slots, tokens
    )
    return pl.pallas_call(
        functools.partial(expert_back_kernel, capacity, experts, shared_width),
        grid_spec=pltpu.PrefetchScalarGridSpec(
            num_scalar_prefetch=1,
            grid=(experts + 1,),
            in_specs=[
                row_spec,
                fixed(rank_cols),
                row_spec,
                fixed(mine),
                fixed(other),
                fixed(mine_grad),
                fixed(other_grad),
                weight_spec,
                part_spec,
                part_spec,
            ],
            out_specs=[
                pl.BlockSpec((tokens, D + gate_lanes), whole),
                pl.BlockSpec(
                    (shards, 3 * hidden_width, D // shards), lambda e, first_ref: (0, e, 0)
                ),
            ],
            scratch_shapes=[
                pltpu.VMEM((tokens, D), FULL),
                pltpu.VMEM((tokens, gate_lanes), FULL),
            ],
        ),
        out_shape=[
            jax.ShapeDtypeStruct((tokens, D + gate_lanes), LOW),
            jax.ShapeDtypeStruct((shards, weights.shape[0], D // shards), LOW),
        ],
        compiler_params=params_of(),
        name="experts_back",
    )(
        first, rank_rows, rank_cols, gate_rows, mine, other, mine_grad, other_grad, weights,
        gate_part, up_part,
    )


def head_kernel(valid_ref, rows_ref, table_ref, goal_ref, logit_ref, stat_ref, top, total, goal):
    step = pl.program_id(0)
    tokens = rows_ref.shape[0]
    block = table_ref.shape[0]

    @pl.when(step == 0)
    def _():
        top[...] = jnp.full_like(top, FAR)
        total[...] = jnp.zeros_like(total)
        goal[...] = jnp.zeros_like(goal)

    logits = dot_nt(rows_ref[...], table_ref[...])
    place = step * block + lax.broadcasted_iota(jnp.int32, (tokens, block), 1)
    logits = jnp.where(place < valid_ref[0], logits, FAR)
    logit_ref[...] = logits
    new_top = jnp.maximum(top[...], jnp.max(logits, axis=1, keepdims=True))
    total[...] = total[...] * jnp.exp(top[...] - new_top) + jnp.sum(
        jnp.exp(logits - new_top), axis=1, keepdims=True
    )
    top[...] = new_top
    goal[...] += jnp.sum(jnp.where(place == goal_ref[...], logits, 0.0), axis=1, keepdims=True)

    @pl.when(step == pl.num_programs(0) - 1)
    def _():
        lane = lax.broadcasted_iota(jnp.int32, (tokens, LANES), 1)
        stat_ref[...] = jnp.where(
            lane == 0, top[...], jnp.where(lane == 1, total[...], goal[...])
        )


def run_head(rows, table, goal_local, valid):
    tokens = rows.shape[0]
    padded = table.shape[0]
    return pl.pallas_call(
        head_kernel,
        grid_spec=pltpu.PrefetchScalarGridSpec(
            num_scalar_prefetch=1,
            grid=(padded // VOCAB_BLOCK,),
            in_specs=[
                pl.BlockSpec((tokens, D), lambda j, valid_ref: (0, 0)),
                pl.BlockSpec((VOCAB_BLOCK, D), lambda j, valid_ref: (j, 0)),
                pl.BlockSpec((tokens, 1), lambda j, valid_ref: (0, 0)),
            ],
            out_specs=[
                pl.BlockSpec((tokens, VOCAB_BLOCK), lambda j, valid_ref: (0, j)),
                pl.BlockSpec((tokens, LANES), lambda j, valid_ref: (0, 0)),
            ],
            scratch_shapes=[pltpu.VMEM((tokens, 1), FULL)] * 3,
        ),
        out_shape=[
            jax.ShapeDtypeStruct((tokens, padded), FULL),
            jax.ShapeDtypeStruct((tokens, LANES), FULL),
        ],
        compiler_params=params_of(),
        name="head",
    )(valid, rows, table, goal_local)


def head_back_kernel(
    rows_ref, table_ref, goal_ref, scale_ref, logit_ref, out_ref, table_grad_ref, total
):
    step = pl.program_id(0)
    tokens = rows_ref.shape[0]
    block = table_ref.shape[0]
    shards, _, width = table_grad_ref.shape

    @pl.when(step == 0)
    def _():
        total[...] = jnp.zeros_like(total)

    place = step * block + lax.broadcasted_iota(jnp.int32, (tokens, block), 1)
    share = scale_ref[:, 2:3]
    grads = jnp.exp(logit_ref[...] - scale_ref[:, 0:1]) * scale_ref[:, 1:2]
    grads = (jnp.where(place == goal_ref[...], grads - 1.0, grads) * share).astype(LOW)
    table_part = dot_tn(grads, rows_ref[...]).astype(LOW)
    for shard in range(shards):
        table_grad_ref[shard] = table_part[:, shard * width : (shard + 1) * width]
    total[...] += dot_nn(grads, table_ref[...])

    @pl.when(step == pl.num_programs(0) - 1)
    def _():
        out_ref[...] = total[...].astype(LOW)


def run_head_back(rows, table, goal_local, scales, logits, shards):
    tokens = rows.shape[0]
    padded = table.shape[0]
    return pl.pallas_call(
        head_back_kernel,
        grid=(padded // VOCAB_BLOCK,),
        in_specs=[
            pl.BlockSpec((tokens, D), lambda j: (0, 0)),
            pl.BlockSpec((VOCAB_BLOCK, D), lambda j: (j, 0)),
            pl.BlockSpec((tokens, 1), lambda j: (0, 0)),
            pl.BlockSpec((tokens, 4), lambda j: (0, 0)),
            pl.BlockSpec((tokens, VOCAB_BLOCK), lambda j: (0, j)),
        ],
        out_specs=[
            pl.BlockSpec((tokens, D), lambda j: (0, 0)),
            pl.BlockSpec((shards, VOCAB_BLOCK, D // shards), lambda j: (0, j, 0)),
        ],
        out_shape=[
            jax.ShapeDtypeStruct((tokens, D), LOW),
            jax.ShapeDtypeStruct((shards, padded, D // shards), LOW),
        ],
        scratch_shapes=[pltpu.VMEM((tokens, D), FULL)],
        compiler_params=params_of(),
        name="head_back",
    )(rows, table, goal_local, scales, logits)


def table_step_kernel(
    factor_ref, weight_ref, moment_ref, square_ref, first_ref, second_ref, *out_refs
):
    factor = factor_ref[0]

    def step(grads, rate):
        results = adam_update(
            weight_ref[0], moment_ref[0], square_ref[0], grads * factor, rate, DECAYS[0]
        )
        for ref, value in zip(out_refs, results):
            ref[0] = value

    @pl.when(pl.program_id(0) == 0)
    def _():
        step(first_ref[...], TABLE_RATES[0])

    @pl.when(pl.program_id(0) == 1)
    def _():
        step(second_ref[...].astype(FULL), TABLE_RATES[1])


def table_step(factor, weight, moment, square, first, second):
    vocab, width = weight.shape[1:]
    steps = pl.cdiv(vocab, STEP_BLOCK)
    block = pl.BlockSpec((1, STEP_BLOCK, width), lambda t, j, factor_ref: (t, j, 0))
    return pl.pallas_call(
        table_step_kernel,
        grid_spec=pltpu.PrefetchScalarGridSpec(
            num_scalar_prefetch=1,
            grid=(2, steps),
            in_specs=[
                block,
                block,
                block,
                pl.BlockSpec(
                    (STEP_BLOCK, width),
                    lambda t, j, factor_ref: (jnp.where(t == 0, j, steps - 1), 0),
                ),
                pl.BlockSpec(
                    (STEP_BLOCK, width), lambda t, j, factor_ref: (jnp.where(t == 1, j, 0), 0)
                ),
            ],
            out_specs=[block] * 3,
        ),
        out_shape=[jax.ShapeDtypeStruct(weight.shape, FULL)] * 3,
        compiler_params=params_of(2),
        name="table_step",
    )(factor, weight, moment, square, first, second)


def expert_step_kernel(factor_ref, core_ref, mine_ref, other_ref, *refs):
    factor = factor_ref[0]
    inner, outer = refs[:3], refs[3:6]
    inner_out, outer_out = refs[6:9], refs[9:]
    split = inner[0].shape[1]
    rows = mine_ref.shape[0]
    half = pl.num_programs(0) // 2

    def step(grads):
        for part, ins, outs, rate in (
            (slice(0, split), inner, inner_out, 6),
            (slice(split, rows), outer, outer_out, 7),
        ):
            results = adam_update(
                ins[0][0],
                ins[1][0],
                ins[2][0],
                grads[part, :].astype(FULL) * factor,
                RATES[rate + 1],
                DECAYS[rate + 1],
            )
            for ref, value in zip(outs, results):
                ref[0] = value

    is_mine = pl.program_id(0) // half == core_ref[0]

    @pl.when(is_mine)
    def _():
        step(mine_ref)

    @pl.when(jnp.logical_not(is_mine))
    def _():
        step(other_ref)


def expert_step(factor, core, mine, other, inner, outer):
    experts, _, width = inner[0].shape
    half = experts // 2
    rows = inner[0].shape[1] + outer[0].shape[1]
    spec = lambda item: pl.BlockSpec((1,) + item.shape[1:], lambda e, f_ref, c_ref: (e, 0, 0))
    held = lambda turn: pl.BlockSpec(
        (rows, width),
        lambda e, f_ref, c_ref: (
            jnp.clip(e - jnp.bitwise_xor(c_ref[0], turn) * half, 0, half - 1),
            0,
        ),
    )
    return pl.pallas_call(
        expert_step_kernel,
        grid_spec=pltpu.PrefetchScalarGridSpec(
            num_scalar_prefetch=2,
            grid=(experts,),
            in_specs=[held(0), held(1)] + [spec(item) for item in inner + outer],
            out_specs=[spec(item) for item in inner + outer],
        ),
        out_shape=[jax.ShapeDtypeStruct(item.shape, FULL) for item in inner + outer],
        compiler_params=params_of(),
        name="expert_step",
    )(factor, core, mine, other, *inner, *outer)


def rows_of_attention(item):
    return item.transpose(1, 2, 0).reshape(-1, item.shape[0])


def rows_of_experts(expert_in, expert_out, shared_in, shared_out, shared_pad):
    experts, width, _, hidden_width = expert_in.shape
    routed = jnp.concatenate(
        [
            expert_in.transpose(0, 2, 3, 1).reshape(experts, 2 * hidden_width, width),
            expert_out.transpose(0, 2, 1),
        ],
        axis=1,
    ).reshape(2, -1, width)
    shared = jnp.concatenate([shared_in.transpose(1, 2, 0), shared_out[None]])
    shared = shared.reshape(3, 2, -1, width).transpose(1, 0, 2, 3)
    shared = jnp.pad(shared, ((0, 0), (0, 0), (0, shared_pad - shared.shape[2]), (0, 0)))
    return jnp.concatenate([routed, shared.reshape(2, -1, width)], axis=1)


def shards(
    token_ids,
    target_ids,
    counted,
    routes,
    vocab_tables,
    norm_gains,
    attn_in,
    attention_output_weight,
    router,
    shared_in,
    shared_out,
    expert_in,
    expert_out,
    vocab_tables_moment,
    norm_gains_moment,
    attn_in_moment,
    attn_out_moment,
    router_moment,
    shared_in_moment,
    shared_out_moment,
    expert_in_moment,
    expert_out_moment,
    vocab_tables_square,
    norm_gains_square,
    attn_in_square,
    attn_out_square,
    router_square,
    shared_in_square,
    shared_out_square,
    expert_in_square,
    expert_out_square,
):
    seq_rows, seqs = token_ids.shape
    tokens = seq_rows * seqs
    model_size = lax.axis_size("mp")
    model_place = lax.axis_index("mp")
    data_size = lax.axis_size("dp")
    data_place = lax.axis_index("dp")
    width = vocab_tables.shape[1]
    vocab = vocab_tables.shape[2]
    experts = expert_in.shape[0]
    expert_total = experts * model_size
    capacity = min(2 * tokens * TOPK // expert_total, tokens)
    hidden_width = expert_out.shape[2]
    head_width = attention_output_weight.shape[0]
    shared_width = shared_out.shape[0]
    own = tokens // model_size
    gate_lanes = round_up(expert_total, LANES)
    place = data_place.reshape(1).astype(jnp.int32)

    counts = counted.T.reshape(tokens).astype(FULL)
    small = jnp.concatenate(
        [
            token_ids.T.reshape(tokens).astype(FULL),
            lax.optimization_barrier(norm_gains.astype(LOW)).astype(FULL).reshape(-1),
            jnp.sum(counts).reshape(1),
        ]
    )
    small = jnp.pad(small, (0, round_up(small.shape[0], 1024) - small.shape[0]))
    small = lax.all_gather(small, "dp", axis=0, tiled=False)
    shared_half = shared_width // 2
    shared_pad = round_up(shared_half, 16)
    expert_low = rows_of_experts(expert_in, expert_out, shared_in, shared_out, shared_pad)
    expert_low = expert_low.astype(LOW)
    expert_halves = own_half(expert_low)
    small, expert_halves = lax.optimization_barrier((small, expert_halves))
    ids = small[:, :tokens].astype(jnp.int32)
    gains = small[:, tokens : tokens + 3 * width].reshape(data_size, 3, width)
    gains = gains.transpose(1, 0, 2).reshape(3, D)
    token_count = jnp.sum(small[:, tokens + 3 * width])

    marks = jnp.concatenate(
        [
            routes.transpose(2, 1, 0).reshape(TOPK, tokens),
            target_ids.T.reshape(1, tokens),
            counted.T.reshape(1, tokens),
        ]
    )
    marks = jnp.stack([marks, swap(marks, 1)], axis=1)
    core = core_place()

    small_pieces = gather_blocks(
        jnp.concatenate([rows_of_attention(attn_in), attention_output_weight, router.T]).astype(
            LOW
        ),
        False,
    )
    expert_all = gather_half(expert_halves)
    tables = vocab_tables.transpose(0, 2, 1)
    padded = round_up(vocab, 2 * VOCAB_BLOCK)
    table_all = gather_half(
        own_half(jnp.pad(tables[1].astype(LOW), ((0, padded - vocab), (0, 0))))
    )
    local_ids = ids.reshape(data_size, model_size, own).transpose(1, 0, 2).reshape(-1)
    local_ids = local_ids - model_place * vocab
    inside = (local_ids >= 0) & (local_ids < vocab)
    looked_up = lookup(jnp.clip(local_ids, 0, vocab - 1), tables)
    looked_up = jnp.where(inside[:, None], looked_up, 0.0).astype(LOW)
    embedded = sum_rows(looked_up).astype(LOW).reshape(data_size, own, width)
    state_zero = lax.all_to_all(embedded, "dp", 0, 0, tiled=True)
    state_zero, *small_pieces = lax.optimization_barrier((state_zero, *small_pieces))
    small_all = jnp.concatenate(by_place(small_pieces), axis=1)
    attn_width = 4 * head_width
    weight_qkv = small_all[: 3 * head_width]
    weight_out = small_all[3 * head_width : attn_width]
    weight_router = small_all[attn_width:]
    state_zero = state_zero.transpose(1, 0, 2).reshape(own, D).astype(FULL)

    first_in = gather_rows(normed(state_zero, gains[0]).astype(LOW))
    projected = dot_nt(first_in, weight_qkv).astype(LOW)
    key_blocks = gather_blocks(projected[:, head_width:], True)
    attended, log_total = attend(place, projected, key_blocks, seqs)
    state_one = state_zero + sum_rows(dot_nn(attended, weight_out).astype(LOW))

    expert_ids = jnp.arange(expert_total, dtype=jnp.int32)
    named = jnp.any(marks[:TOPK, :, None, :] == expert_ids[None, None, :, None], axis=0)
    earlier = jnp.arange(tokens)[:, None] < jnp.arange(tokens)[None, :]
    ranks = dot_nn(named.reshape(-1, tokens).astype(LOW), earlier.astype(LOW)).astype(jnp.int32)
    ranks = jnp.where(named, ranks.reshape(named.shape), -1)
    named_cols = named.transpose(0, 2, 1).reshape(2 * tokens, expert_total)
    rank_cols = ranks.transpose(0, 2, 1).reshape(2 * tokens, expert_total)
    part_experts = experts // 2
    first_expert = model_place * experts + core * part_experts
    local_rows = lambda table: lax.dynamic_slice_in_dim(table, first_expert, part_experts, 0)[
        :, None, :
    ]
    rank_rows = local_rows(ranks.transpose(1, 0, 2).reshape(expert_total, 2 * tokens))
    first_place = first_expert.reshape(1).astype(jnp.int32)
    second_in = gather_rows(normed(state_one, gains[1]).astype(LOW))
    second_other = swap(second_in, 1)
    router_logits = jnp.concatenate(
        [dot_nt(second_in, weight_router), dot_nt(second_other, weight_router)]
    )
    gates = jax.nn.softmax(jnp.where(named_cols, router_logits, FAR), axis=1)
    gates = jnp.where(named_cols, gates, 0.0)
    gate_rows = local_rows(gates.T)
    moe_part, gate_part, up_part = run_experts(
        first_place, rank_rows, rank_cols, gates, second_in, second_other, expert_all, capacity,
        hidden_width, shared_pad,
    )
    state_two = state_one + sum_rows(sum_pair(moe_part))

    third_in = pair_rows(gather_rows(normed(state_two, gains[2]).astype(LOW)))
    half_vocab = padded // 2
    goal_local = marks[TOPK].reshape(2 * tokens, 1) - model_place * vocab
    goal_local = jnp.where(goal_local < vocab, goal_local - core * half_vocab, -1)
    valid = (vocab - core * half_vocab).reshape(1).astype(jnp.int32)
    logits, stats = run_head(third_in, table_all, goal_local, valid)
    stats = stats[:, :3].T
    stats = lax.all_gather(jnp.stack([stats, swap(stats, 1)]), "mp", axis=0, tiled=False)
    stats = stats.reshape(model_size, 2, 3, 2, tokens)
    stats = jnp.concatenate([stats[:, 0], stats[:, 1, :, ::-1]]).reshape(-1, 3, 2 * tokens)
    top = jnp.max(stats[:, 0], axis=0)
    log_head = top + jnp.log(jnp.sum(stats[:, 1] * jnp.exp(stats[:, 0] - top), axis=0))
    goal_logit = jnp.sum(stats[:, 2], axis=0)
    pair_counts = marks[TOPK + 1].reshape(2 * tokens).astype(FULL)
    loss_rows = pair_counts * (log_head - goal_logit + Z_COEF * log_head * log_head)
    loss_part = jnp.sum(loss_rows[:tokens])
    scales = jnp.stack(
        [log_head, 1.0 + 2.0 * Z_COEF * log_head, pair_counts / token_count, pair_counts], axis=1
    )
    third_part, table_part = run_head_back(
        third_in, table_all, goal_local, scales, logits, data_size // 2
    )
    table_second = scatter_half(table_part)
    state_two_grad, gain_three = norm_back(state_two, gains[2], sum_rows(sum_pair(third_part)))

    two_low = gather_rows(state_two_grad.astype(LOW))
    second_part, expert_part = run_experts_back(
        first_place, rank_rows, rank_cols, gate_rows, second_in, second_other, two_low,
        swap(two_low, 1), expert_all, gate_part, up_part, capacity, hidden_width, shared_pad,
        data_size // 2, gate_lanes,
    )
    expert_grad = scatter_half(expert_part)
    second_sum = sum_rows(sum_pair(second_part))
    second_grad = second_sum[:, :D]
    gate_grad = second_sum[:, D : D + expert_total]
    own_gates = lax.dynamic_slice_in_dim(gates, model_place * own, own, 0)
    choice_grad = own_gates * (
        gate_grad - jnp.sum(own_gates * gate_grad, axis=1, keepdims=True)
    )
    choice_grad = choice_grad.astype(LOW)
    second_grad = second_grad + dot_nn(choice_grad, weight_router)
    norm_grad, gain_two = norm_back(state_one, gains[1], second_grad)
    state_one_grad = state_two_grad + norm_grad

    sent = jnp.concatenate(
        [
            state_one_grad.astype(LOW),
            jnp.pad(choice_grad, ((0, 0), (0, gate_lanes - expert_total))),
        ],
        axis=1,
    )
    sent = gather_rows(sent)
    one_low = sent[:, :D]
    router_grad = dot_tn(sent[:, D : D + expert_total], second_in)
    attn_out_grad = dot_tn(attended, one_low)
    out_grad = dot_nt(one_low, weight_out).astype(LOW)
    query_grad, *key_parts = attend_back(
        place, projected, log_total, out_grad, key_blocks, seqs, table_second
    )
    key_grad = scatter_blocks(key_parts, True).astype(LOW)
    projected_grad = jnp.concatenate([query_grad, key_grad], axis=1)
    first_part = dot_nn(projected_grad, weight_qkv).astype(LOW)
    attn_in_grad = dot_tn(projected_grad, first_in)
    attn_sums = scatter_features(jnp.concatenate([attn_in_grad, attn_out_grad, router_grad]))
    norm_grad, gain_one = norm_back(state_zero, gains[0], sum_rows(first_part))
    state_zero_grad = state_one_grad + norm_grad

    gain_pad = 16
    gain_part = jnp.stack([gain_one, gain_two, gain_three]).astype(LOW)
    gain_part = jnp.pad(gain_part, ((0, gain_pad - 3), (0, 0)))
    back_rows = jnp.concatenate([state_zero_grad.astype(LOW), gain_part])
    back_rows = back_rows.reshape(own + gain_pad, data_size, width).transpose(1, 0, 2)
    back_rows = gather_rows(lax.all_to_all(back_rows, "dp", 0, 0, tiled=True))
    gain_grad = jnp.sum(back_rows[:, own : own + 3].astype(FULL), axis=0)
    table_first = table_grad(local_ids, back_rows[:, :own].reshape(-1, width), vocab, expert_grad)

    square = lambda item: jnp.sum(jnp.square(item.astype(FULL)))
    local_square = (
        square(table_first)
        + square(table_second)
        + square(expert_grad)
        + square(attn_sums[:attn_width])
        + (square(attn_sums[attn_width:]) + square(gain_grad)) / model_size
    )
    table_second = in_order(*halves_back(table_second), 0)[:vocab]
    expert_grads = halves_back(expert_grad)
    shared_sums = in_order(
        *[
            item[3 * part_experts * hidden_width :].reshape(3, shared_pad, width)[:, :shared_half]
            for item in expert_grads
        ],
        1,
    ).astype(FULL)
    sums = jnp.stack([local_square, loss_part / model_size])
    sums = add_all(jnp.broadcast_to(sums[:, None], (2, LANES)))[:, 0]
    grad_norm = jnp.sqrt(sums[0])
    factor = CLIP / jnp.maximum(grad_norm, CLIP)

    table_results = table_step(
        factor.reshape(1),
        tables,
        vocab_tables_moment.transpose(0, 2, 1),
        vocab_tables_square.transpose(0, 2, 1),
        table_first,
        table_second,
    )
    results = [sums[1], token_count, grad_norm]
    results.extend(item.transpose(0, 2, 1) for item in table_results)
    gradients = (
        gain_grad,
        attn_sums[: 3 * head_width].reshape(3, head_width, width).transpose(2, 0, 1),
        attn_sums[3 * head_width : attn_width],
        attn_sums[attn_width:].T,
        shared_sums[:2].transpose(2, 0, 1),
        shared_sums[2],
    )
    params = (
        norm_gains, attn_in, attention_output_weight, router, shared_in, shared_out,
    )
    moments = (
        norm_gains_moment, attn_in_moment, attn_out_moment, router_moment, shared_in_moment,
        shared_out_moment,
    )
    squares = (
        norm_gains_square, attn_in_square, attn_out_square, router_square, shared_in_square,
        shared_out_square,
    )
    for index in range(6):
        results.extend(
            adam_update(
                params[index],
                moments[index],
                squares[index],
                gradients[index] * factor,
                RATES[index + 1],
                DECAYS[index + 1],
            )
        )
    expert_results = expert_step(
        factor.reshape(1),
        core.reshape(1).astype(jnp.int32),
        *expert_grads,
        [
            item.transpose(0, 2, 3, 1).reshape(experts, 2 * hidden_width, width)
            for item in (expert_in, expert_in_moment, expert_in_square)
        ],
        [
            item.transpose(0, 2, 1)
            for item in (expert_out, expert_out_moment, expert_out_square)
        ],
    )
    results.extend(
        item.reshape(experts, 2, hidden_width, width).transpose(0, 3, 1, 2)
        for item in expert_results[:3]
    )
    results.extend(item.transpose(0, 2, 1) for item in expert_results[3:])
    return tuple(results)


def solution(mesh):
    in_specs = (
        P("dp", None),
        P("dp", None),
        P("dp", None),
        P("dp", None, None),
        P(None, "dp", "mp"),
        P(None, "dp"),
        P("dp", None, "mp"),
        P("mp", "dp"),
        P("dp", None),
        P("dp", None, "mp"),
        P("mp", "dp"),
        P("mp", "dp", None, None),
        P("mp", "dp", None),
        P(None, "dp", "mp"),
        P(None, "dp"),
        P("dp", None, "mp"),
        P("mp", "dp"),
        P("dp", None),
        P("dp", None, "mp"),
        P("mp", "dp"),
        P("mp", "dp", None, None),
        P("mp", "dp", None),
        P(None, "dp", "mp"),
        P(None, "dp"),
        P("dp", None, "mp"),
        P("mp", "dp"),
        P("dp", None),
        P("dp", None, "mp"),
        P("mp", "dp"),
        P("mp", "dp", None, None),
        P("mp", "dp", None),
    )
    out_specs = (
        P(),
        P(),
        P(),
        P(None, "dp", "mp"),
        P(None, "dp", "mp"),
        P(None, "dp", "mp"),
        P(None, "dp"),
        P(None, "dp"),
        P(None, "dp"),
        P("dp", None, "mp"),
        P("dp", None, "mp"),
        P("dp", None, "mp"),
        P("mp", "dp"),
        P("mp", "dp"),
        P("mp", "dp"),
        P("dp", None),
        P("dp", None),
        P("dp", None),
        P("dp", None, "mp"),
        P("dp", None, "mp"),
        P("dp", None, "mp"),
        P("mp", "dp"),
        P("mp", "dp"),
        P("mp", "dp"),
        P("mp", "dp", None, None),
        P("mp", "dp", None, None),
        P("mp", "dp", None, None),
        P("mp", "dp", None),
        P("mp", "dp", None),
        P("mp", "dp", None),
    )
    return jax.shard_map(shards, mesh=mesh, in_specs=in_specs, out_specs=out_specs, check_vma=False)
```

```python
import functools

import jax
import jax.numpy as jnp
from jax import lax
from jax.experimental import pallas as pl
from jax.experimental.pallas import tpu as pltpu
from jax.sharding import PartitionSpec as P

D = 1024
HD = 128
TOPK = 6
STEP = 10
LANES = 128
VOCAB_BLOCK = 1024
STEP_BLOCK = 2672
PAIR_BLOCK = 2304
ROW_BLOCK = 256

NORM_EPS = 1e-06
Z_COEF = 0.01
CLIP = 0.01
BETA_ONE = 0.9
BETA_TWO = 0.95
ADAM_EPS = 1e-08
TABLE_RATES = (1.0, 0.06)
RATES = (0.0, 1.0, 0.02, 0.05, 0.01, 0.02, 0.02, 0.02, 0.02)
DECAYS = (0.1, 0.0, 0.1, 0.1, 0.1, 0.1, 0.1, 0.1, 0.1)
FAR = -1e30
LOW = jnp.bfloat16
FULL = jnp.float32


def dot_nn(left, right):
    return lax.dot_general(left, right, (((1,), (0,)), ((), ())), preferred_element_type=FULL)


def dot_nt(left, right):
    return lax.dot_general(left, right, (((1,), (1,)), ((), ())), preferred_element_type=FULL)


def dot_tn(left, right):
    return lax.dot_general(left, right, (((0,), (0,)), ((), ())), preferred_element_type=FULL)


def params_of(dims=1, mib=50):
    return pltpu.CompilerParams(
        dimension_semantics=("arbitrary",) * dims, vmem_limit_bytes=mib * 1024 * 1024
    )


def round_up(number, unit):
    return (number + unit - 1) // unit * unit


def normed(values, gain_row):
    return (
        values * lax.rsqrt(jnp.mean(values * values, axis=-1, keepdims=True) + NORM_EPS) * gain_row
    )


def norm_back(values, gain_row, upstream):
    inv_rms = lax.rsqrt(jnp.mean(values * values, axis=-1, keepdims=True) + NORM_EPS)
    unit_rows = values * inv_rms
    scaled = upstream * gain_row
    gain_grad = jnp.sum(upstream * unit_rows, axis=0)
    return (
        inv_rms * (scaled - unit_rows * jnp.mean(scaled * unit_rows, axis=-1, keepdims=True)),
        gain_grad,
    )


def swiglu_grads(gate_part, up_part, upstream):
    sigmoid_gate = jax.nn.sigmoid(gate_part)
    silu_gate = gate_part * sigmoid_gate
    gate_grad = upstream * up_part * sigmoid_gate * (1.0 + gate_part * (1.0 - sigmoid_gate))
    return gate_grad, upstream * silu_gate


def adam_update(weight, moment, square, grad_item, rate, decay):
    new_moment = BETA_ONE * moment + (1.0 - BETA_ONE) * grad_item
    new_square = BETA_TWO * square + (1.0 - BETA_TWO) * grad_item * grad_item
    scaled = new_square * (1.0 / (1.0 - BETA_TWO**STEP))
    step_ratio = (new_moment * (1.0 / (1.0 - BETA_ONE**STEP))) / (
        scaled * lax.rsqrt(scaled) + ADAM_EPS
    )
    return (weight - rate * (step_ratio + decay * weight), new_moment, new_square)


def sum_rows(partial):
    size = lax.axis_size("mp")
    place = lax.axis_index("mp")
    pieces = partial.reshape((size, partial.shape[0] // size) + partial.shape[1:])
    total = lax.dynamic_index_in_dim(pieces, place, 0, keepdims=False).astype(FULL)
    for step in range(1, size):
        sent = lax.dynamic_index_in_dim(pieces, (place + step) % size, 0, keepdims=False)
        got = lax.ppermute(sent, "mp", [(i, (i + step) % size) for i in range(size)])
        total = total + got.astype(FULL)
    return total


def gather_rows(rows):
    size = lax.axis_size("mp")
    place = lax.axis_index("mp")
    count = rows.shape[0]
    whole = jnp.zeros((size * count,) + rows.shape[1:], rows.dtype)
    rest = (0,) * (rows.ndim - 1)
    whole = lax.dynamic_update_slice(whole, rows, (place * count,) + rest)
    for step in range(1, size):
        got = lax.ppermute(rows, "mp", [(i, (i + step) % size) for i in range(size)])
        whole = lax.dynamic_update_slice(whole, got, ((place - step) % size * count,) + rest)
    return whole


def swap(item, mask):
    size = lax.axis_size("dp")
    return lax.ppermute(item, "dp", [(i, i ^ mask) for i in range(size)])


def chips_of(size):
    return [list(range(core, size, 2)) for core in range(2)]


def core_place():
    return lax.axis_index("dp") % 2


def pair_rows(rows):
    return jnp.concatenate([rows, swap(rows, 1)])


def sum_pair(partial):
    count = partial.shape[0] // 2
    return (partial[:count].astype(FULL) + swap(partial[count:], 1).astype(FULL)).astype(LOW)


def in_order(mine, other, axis):
    first = core_place() == 0
    return jnp.concatenate(
        [jnp.where(first, mine, other), jnp.where(first, other, mine)], axis=axis
    )


def gather_half(core, mine, other):
    size = lax.axis_size("dp")
    return lax.all_gather(
        pair_features(core, mine, swap(other, 1)),
        "dp",
        axis=1,
        tiled=True,
        axis_index_groups=chips_of(size),
    )


def scatter_half(grads):
    size = lax.axis_size("dp")
    part = lax.psum_scatter(
        grads, "dp", scatter_dimension=0, tiled=False, axis_index_groups=chips_of(size)
    )
    return lax.optimization_barrier(part)


def halves_back(part):
    width = part.shape[1] // 2
    place = core_place()
    mine = lax.dynamic_slice_in_dim(part, place * width, width, 1)
    return mine, swap(lax.dynamic_slice_in_dim(part, (1 - place) * width, width, 1), 1)


def by_place(pieces):
    place = lax.axis_index("dp")
    stacked = jnp.stack(pieces)
    return [
        lax.dynamic_index_in_dim(stacked, jnp.bitwise_xor(place, index), 0, keepdims=False)
        for index in range(len(pieces))
    ]


def scatter_features(grads):
    size = lax.axis_size("dp")
    place = lax.axis_index("dp")
    width = grads.shape[1] // size
    pieces = grads.astype(LOW).reshape(-1, size, width).transpose(1, 0, 2)
    picked = lambda core: jnp.stack(
        [
            lax.dynamic_index_in_dim(pieces, jnp.bitwise_xor(place, mask), 0, keepdims=False)
            for mask in range(core, size, 2)
        ]
    )
    return scatter_blocks(picked(0), picked(1), False)


def tree_sum(items):
    while len(items) > 1:
        items = [items[index] + items[index + 1] for index in range(0, len(items), 2)]
    return items[0]


def add_all(item):
    item = item + swap(item, 1)
    item = tree_sum([item] + [swap(item, mask) for mask in range(2, lax.axis_size("dp"), 2)])
    size = lax.axis_size("mp")
    return tree_sum(
        [item]
        + [
            lax.ppermute(item, "mp", [(i, i ^ mask) for i in range(size)])
            for mask in range(1, size)
        ]
    )


def send_blocks(item, mask, keep):
    size = lax.axis_size("dp")
    return lax.ppermute(item, "dp", [(i, i ^ mask) for i in range(size) if keep(i)])


def gather_blocks(item, causal):
    both = []
    for mask in range(0, lax.axis_size("dp"), 2):
        block, keep = item, lambda i: not causal or i % 2 == 0
        if mask > 0:
            block = send_blocks(item, mask, lambda i: not causal or i ^ mask > i)
            keep = lambda i: not causal or i ^ mask < i
        both.extend([block, send_blocks(block, 1, keep)])
    return both


def scatter_blocks(even, odd, causal):
    pairs = even.astype(FULL) + swap(odd, 1).astype(FULL)
    total = pairs[0]
    for index in range(1, even.shape[0]):
        mask = 2 * index
        keep = lambda i: not causal or i ^ mask < i
        total = total + send_blocks(pairs[index].astype(LOW), mask, keep).astype(FULL)
    return total


def shift(item, step):
    size = lax.axis_size("mp")
    return lax.ppermute(item, "mp", [(i, (i + step) % size) for i in range(size)])


def join_stats(parts):
    parts = jnp.stack(parts)
    top = jnp.max(parts[:, 0], axis=0)
    total = jnp.sum(parts[:, 1] * jnp.exp(parts[:, 0] - top), axis=0)
    return jnp.stack([top, total, jnp.sum(parts[:, 2], axis=0)])


def split_kernel(core_ref, inner_ref, outer_ref, shared_ref, mine_ref, other_ref):
    step = pl.program_id(0)
    steps = pl.num_programs(0) // 2
    split = inner_ref.shape[1]

    def fill(out_ref):
        @pl.when(step % steps < steps - 1)
        def _():
            out_ref[:split, :] = inner_ref[0].astype(LOW)
            out_ref[split:, :] = outer_ref[0].astype(LOW)

        @pl.when(step % steps == steps - 1)
        def _():
            out_ref[: shared_ref.shape[1], :] = shared_ref[0].astype(LOW)

    @pl.when(step < steps)
    def _():
        fill(mine_ref)

    @pl.when(step >= steps)
    def _():
        fill(other_ref)


def split_experts(core, expert_in, expert_out, shared):
    experts, width, _, hidden_width = expert_in.shape
    half = experts // 2
    steps = half + 1
    rows = 3 * hidden_width
    total = half * rows + shared.shape[1]

    def expert_of(step, core_ref):
        turn = jnp.bitwise_xor(step // steps, core_ref[0])
        return (turn * half + jnp.minimum(step % steps, half - 1), 0, 0)

    return pl.pallas_call(
        split_kernel,
        grid_spec=pltpu.PrefetchScalarGridSpec(
            num_scalar_prefetch=1,
            grid=(2 * steps,),
            in_specs=[
                pl.BlockSpec((1, 2 * hidden_width, width), expert_of),
                pl.BlockSpec((1, hidden_width, width), expert_of),
                pl.BlockSpec(
                    (1,) + shared.shape[1:],
                    lambda j, core_ref: (jnp.bitwise_xor(j // steps, core_ref[0]), 0, 0),
                ),
            ],
            out_specs=[
                pl.BlockSpec((rows, width), lambda j, core_ref: (jnp.minimum(j, half), 0)),
                pl.BlockSpec((rows, width), lambda j, core_ref: (jnp.maximum(j - steps, 0), 0)),
            ],
        ),
        out_shape=[jax.ShapeDtypeStruct((total, width), LOW)] * 2,
        compiler_params=params_of(),
        name="split_experts",
    )(
        core,
        expert_in.transpose(0, 2, 3, 1).reshape(experts, 2 * hidden_width, width),
        expert_out.transpose(0, 2, 1),
        shared,
    )


def pair_kernel(core_ref, mine_ref, other_ref, out_ref):
    width = mine_ref.shape[1]

    @pl.when(core_ref[0] == 0)
    def _():
        out_ref[:, :width] = mine_ref[...]
        out_ref[:, width:] = other_ref[...]

    @pl.when(core_ref[0] != 0)
    def _():
        out_ref[:, :width] = other_ref[...]
        out_ref[:, width:] = mine_ref[...]


def pair_features(core, mine, other):
    rows, width = mine.shape
    spec = pl.BlockSpec((PAIR_BLOCK, width), lambda j, core_ref: (j, 0))
    return pl.pallas_call(
        pair_kernel,
        grid_spec=pltpu.PrefetchScalarGridSpec(
            num_scalar_prefetch=1,
            grid=(pl.cdiv(rows, PAIR_BLOCK),),
            in_specs=[spec, spec],
            out_specs=pl.BlockSpec((PAIR_BLOCK, 2 * width), lambda j, core_ref: (j, 0)),
        ),
        out_shape=jax.ShapeDtypeStruct((rows, 2 * width), LOW),
        compiler_params=params_of(),
        name="pair_features",
    )(core, mine, other)


def lookup_kernel(ids_ref, table_ref, out_ref):
    base = pl.program_id(0) * out_ref.shape[0]

    def copy_rows(step, carry):
        for inner in range(8):
            row = step * 8 + inner
            out_ref[pl.ds(row, 1), :] = table_ref[0, pl.ds(ids_ref[base + row], 1), :]
        return carry

    lax.fori_loop(0, out_ref.shape[0] // 8, copy_rows, 0)


def lookup(ids, tables):
    count = ids.shape[0]
    vocab, width = tables.shape[1:]
    block = 512
    return pl.pallas_call(
        lookup_kernel,
        grid_spec=pltpu.PrefetchScalarGridSpec(
            num_scalar_prefetch=1,
            grid=(count // block,),
            in_specs=[pl.BlockSpec((1, vocab, width), lambda i, ids_ref: (0, 0, 0))],
            out_specs=pl.BlockSpec((block, width), lambda i, ids_ref: (i, 0)),
        ),
        out_shape=jax.ShapeDtypeStruct((count, width), FULL),
        compiler_params=params_of(),
        name="lookup",
    )(ids, tables)


def table_grad_kernel(vocab, ids_ref, rows_ref, *refs):
    *before_refs, out_ref, square_ref = refs
    block = out_ref.shape[0]
    span = 512
    step = pl.program_id(0)
    token_of = step * block + lax.broadcasted_iota(jnp.int32, (block, span), 0)
    total = jnp.zeros(out_ref.shape, FULL)
    for start in range(0, rows_ref.shape[0], span):
        hit = (token_of == ids_ref[:, start : start + span]).astype(FULL).astype(LOW)
        total = total + dot_nn(hit, rows_ref[start : start + span, :])
    for before_ref in before_refs:
        total = total + before_ref[...]
    out_ref[...] = total

    @pl.when(step == 0)
    def _():
        square_ref[...] = jnp.zeros_like(square_ref)

    row = step * block + lax.broadcasted_iota(jnp.int32, total.shape, 0)
    kept = jnp.where(row < vocab, total * total, 0.0)
    square_ref[...] += jnp.sum(kept.reshape(-1, 8, total.shape[1]), axis=0)


def table_grad(ids, rows, vocab, *before):
    count, width = rows.shape
    block = pl.BlockSpec((VOCAB_BLOCK, width), lambda j: (j, 0))
    return pl.pallas_call(
        functools.partial(table_grad_kernel, vocab),
        grid=(pl.cdiv(vocab, VOCAB_BLOCK),),
        in_specs=[
            pl.BlockSpec((1, count), lambda j: (0, 0)),
            pl.BlockSpec((count, width), lambda j: (0, 0)),
        ]
        + [block] * len(before),
        out_specs=[block, pl.BlockSpec((8, width), lambda j: (0, 0))],
        out_shape=[
            jax.ShapeDtypeStruct((vocab, width), FULL),
            jax.ShapeDtypeStruct((8, width), FULL),
        ],
        compiler_params=params_of(),
        cost_estimate=pl.CostEstimate(
            flops=4 * count * vocab * width, bytes_accessed=8 * vocab * width, transcendentals=0
        ),
        name="table_grad",
    )(ids.reshape(1, count), rows, *before)


def masked_scores(place, query, keys, rows, blocks):
    scores = dot_nt(query, keys) * HD ** (-0.5)
    offset = lax.broadcasted_iota(jnp.int32, (1, rows), 1)
    key_pos = jnp.concatenate(
        [jnp.bitwise_xor(place, mask) * rows + offset for mask in range(blocks)], axis=1
    )
    query_pos = place * rows + lax.broadcasted_iota(jnp.int32, (rows, 1), 0)
    return jnp.where(key_pos <= query_pos, scores, FAR)


def head_cols(refs, index):
    return jnp.concatenate([ref[:, index * HD : (index + 1) * HD] for ref in refs], axis=0)


def attend_kernel(blocks, place_ref, query_ref, *refs):
    key_refs = refs[:blocks]
    out_ref, log_ref = refs[blocks:]
    place = place_ref[0]
    rows, width = query_ref.shape
    heads = width // HD
    for head in range(heads):
        cols = slice(head * HD, (head + 1) * HD)
        keys = head_cols(key_refs, head)
        values = head_cols(key_refs, heads + head)
        scores = masked_scores(place, query_ref[:, cols], keys, rows, blocks)
        top = jnp.max(scores, axis=1, keepdims=True)
        powers = jnp.exp(scores - top)
        total = jnp.sum(powers, axis=1, keepdims=True)
        probs = (powers * (1.0 / total)).astype(LOW)
        out_ref[:, cols] = dot_nn(probs, values).astype(LOW)
        log_ref[0, :, head : head + 1] = top + jnp.log(total)


def attend(place, projected, key_blocks, seqs):
    blocks = len(key_blocks)
    tokens = projected.shape[0]
    rows = tokens // seqs
    width = projected.shape[1] // 3
    heads = width // HD
    return pl.pallas_call(
        functools.partial(attend_kernel, blocks),
        grid_spec=pltpu.PrefetchScalarGridSpec(
            num_scalar_prefetch=1,
            grid=(seqs,),
            in_specs=[pl.BlockSpec((rows, width), lambda s, place_ref: (s, 0))]
            + [pl.BlockSpec((rows, 2 * width), lambda s, place_ref: (s, 0))] * blocks,
            out_specs=[
                pl.BlockSpec((rows, width), lambda s, place_ref: (s, 0)),
                pl.BlockSpec((1, rows, heads), lambda s, place_ref: (s, 0, 0)),
            ],
        ),
        out_shape=[
            jax.ShapeDtypeStruct((tokens, width), LOW),
            jax.ShapeDtypeStruct((seqs, rows, heads), FULL),
        ],
        compiler_params=params_of(),
        name="attend",
    )(place, projected, *key_blocks)


def attend_back_kernel(blocks, place_ref, query_ref, log_ref, grad_ref, after_ref, *refs):
    del after_ref
    key_refs = refs[:blocks]
    query_grad_ref = refs[blocks]
    key_grad_refs = refs[blocks + 1 :]
    place = place_ref[0]
    rows, width = query_ref.shape
    heads = width // HD
    for head in range(heads):
        cols = slice(head * HD, (head + 1) * HD)
        keys = head_cols(key_refs, head)
        values = head_cols(key_refs, heads + head)
        query = query_ref[:, cols]
        out_grad = grad_ref[:, cols]
        scores = masked_scores(place, query, keys, rows, blocks)
        probs = jnp.exp(scores - log_ref[0, :, head : head + 1])
        prob_grad = dot_nt(out_grad, values)
        delta = jnp.sum(probs * prob_grad, axis=1, keepdims=True)
        score_grad = (probs * (prob_grad - delta)).astype(LOW)
        query_grad_ref[:, cols] = (dot_nn(score_grad, keys) * HD ** (-0.5)).astype(LOW)
        key_grad = (dot_tn(score_grad, query) * HD ** (-0.5)).astype(LOW)
        value_grad = dot_tn(probs.astype(LOW), out_grad).astype(LOW)
        value_cols = slice((heads + head) * HD, (heads + head + 1) * HD)
        for mask in range(blocks):
            part = slice(mask * rows, (mask + 1) * rows)
            key_grad_refs[mask % 2][mask // 2, :, cols] = key_grad[part]
            key_grad_refs[mask % 2][mask // 2, :, value_cols] = value_grad[part]


def attend_back(place, projected, log_total, out_grad, key_blocks, seqs, after):
    blocks = len(key_blocks)
    tokens = projected.shape[0]
    rows = tokens // seqs
    width = projected.shape[1] // 3
    heads = width // HD
    row_spec = pl.BlockSpec((rows, width), lambda s, place_ref: (s, 0))
    key_spec = pl.BlockSpec((rows, 2 * width), lambda s, place_ref: (s, 0))
    return pl.pallas_call(
        functools.partial(attend_back_kernel, blocks),
        grid_spec=pltpu.PrefetchScalarGridSpec(
            num_scalar_prefetch=1,
            grid=(seqs,),
            in_specs=[
                row_spec,
                pl.BlockSpec((1, rows, heads), lambda s, place_ref: (s, 0, 0)),
                row_spec,
                pl.BlockSpec(memory_space=pl.ANY),
            ]
            + [key_spec] * blocks,
            out_specs=[row_spec]
            + [pl.BlockSpec((blocks // 2, rows, 2 * width), lambda s, place_ref: (0, s, 0))] * 2,
        ),
        out_shape=[jax.ShapeDtypeStruct((tokens, width), LOW)]
        + [jax.ShapeDtypeStruct((blocks // 2, tokens, 2 * width), LOW)] * 2,
        compiler_params=params_of(),
        name="attend_back",
    )(place, projected, log_total, out_grad, after, *key_blocks)


def column_of(table, index):
    lane = lax.broadcasted_iota(jnp.int32, table.shape, 1)
    return jnp.sum(jnp.where(lane == index, table, 0), axis=1, keepdims=True)


def swiglu_low(gate_part, up_part):
    return (gate_part * jax.nn.sigmoid(gate_part) * up_part).astype(LOW)


def expert_kernel(
    capacity,
    experts,
    shared_width,
    first_ref,
    rank_row_ref,
    rank_col_ref,
    gate_ref,
    mine_ref,
    other_ref,
    weight_ref,
    out_ref,
    gate_part_ref,
    up_part_ref,
    total,
):
    expert = pl.program_id(0)
    row_refs = (mine_ref, other_ref)
    tokens = mine_ref.shape[0]
    blocks = [slice(index * tokens, (index + 1) * tokens) for index in range(2)]
    hidden_width = weight_ref.shape[0] // 3

    @pl.when(expert == 0)
    def _():
        total[...] = jnp.zeros_like(total)

    @pl.when(expert < experts)
    def _():
        number = first_ref[0] + expert
        slot = lax.broadcasted_iota(jnp.int32, (capacity, tokens), 0)
        parts = []
        for block, rows_ref in zip(blocks, row_refs):
            pick = (slot == rank_row_ref[0, :, block]).astype(FULL).astype(LOW)
            parts.append(dot_nn(pick, rows_ref[...]).astype(LOW))
        picked = jnp.concatenate(parts)
        gate_part = dot_nt(picked, weight_ref[:hidden_width, :])
        up_part = dot_nt(picked, weight_ref[hidden_width : 2 * hidden_width, :])
        gate_part_ref[0] = gate_part
        up_part_ref[0] = up_part
        hidden = swiglu_low(gate_part, up_part)
        output = dot_nn(hidden, weight_ref[2 * hidden_width :, :]).astype(LOW)
        for index, block in enumerate(blocks):
            rank_col = column_of(rank_col_ref[block, :], number)
            back = lax.broadcasted_iota(jnp.int32, (tokens, capacity), 1) == rank_col
            spread = dot_nn(
                back.astype(FULL).astype(LOW), output[index * capacity : (index + 1) * capacity]
            )
            total[block, :] += column_of(gate_ref[block, :], number) * spread

    @pl.when(expert == experts)
    def _():
        for block, rows_ref in zip(blocks, row_refs):
            rows = rows_ref[...]
            gate_part = dot_nt(rows, weight_ref[:shared_width, :])
            up_part = dot_nt(rows, weight_ref[shared_width : 2 * shared_width, :])
            hidden = swiglu_low(gate_part, up_part)
            part = dot_nn(hidden, weight_ref[2 * shared_width : 3 * shared_width, :])
            out_ref[block, :] = (total[block, :] + part).astype(LOW)


def expert_specs(experts, hidden_width, slots, tokens):
    whole = lambda e, first_ref: (0, 0)
    fixed = lambda item: pl.BlockSpec(item.shape, whole, pipeline_mode=pl.Buffered(1))
    part = lambda e, first_ref: (jnp.minimum(e, experts - 1), 0, 0)
    return (
        whole,
        fixed,
        pl.BlockSpec((1, 1, tokens), part),
        pl.BlockSpec((3 * hidden_width, D), lambda e, first_ref: (e, 0)),
        pl.BlockSpec((1, slots, hidden_width), part),
    )


def run_experts(
    first, rank_rows, rank_cols, gates, mine, other, weights, capacity, hidden_width, shared_width
):
    experts = rank_rows.shape[0]
    tokens = 2 * mine.shape[0]
    slots = 2 * capacity
    whole, fixed, row_spec, weight_spec, part_spec = expert_specs(
        experts, hidden_width, slots, tokens
    )
    return pl.pallas_call(
        functools.partial(expert_kernel, capacity, experts, shared_width),
        grid_spec=pltpu.PrefetchScalarGridSpec(
            num_scalar_prefetch=1,
            grid=(experts + 1,),
            in_specs=[
                row_spec,
                fixed(rank_cols),
                fixed(gates),
                fixed(mine),
                fixed(other),
                weight_spec,
            ],
            out_specs=[pl.BlockSpec((tokens, D), whole), part_spec, part_spec],
            scratch_shapes=[pltpu.VMEM((tokens, D), FULL)],
        ),
        out_shape=[
            jax.ShapeDtypeStruct((tokens, D), LOW),
            jax.ShapeDtypeStruct((experts, slots, hidden_width), FULL),
            jax.ShapeDtypeStruct((experts, slots, hidden_width), FULL),
        ],
        compiler_params=params_of(),
        name="experts",
    )(first, rank_rows, rank_cols, gates, mine, other, weights)


def expert_back_kernel(
    capacity,
    experts,
    shared_width,
    first_ref,
    rank_row_ref,
    rank_col_ref,
    gate_row_ref,
    mine_ref,
    other_ref,
    mine_grad_ref,
    other_grad_ref,
    weight_ref,
    gate_part_ref,
    up_part_ref,
    out_ref,
    weight_grad_ref,
    total,
    gate_total,
):
    expert = pl.program_id(0)
    row_refs = (mine_ref, other_ref)
    grad_refs = (mine_grad_ref, other_grad_ref)
    tokens = mine_ref.shape[0]
    blocks = [slice(index * tokens, (index + 1) * tokens) for index in range(2)]
    hidden_width = weight_ref.shape[0] // 3
    shards, _, width = weight_grad_ref.shape

    @pl.when(expert == 0)
    def _():
        total[...] = jnp.zeros_like(total)
        gate_total[...] = jnp.zeros_like(gate_total)

    def put(start, grads):
        grads = grads.astype(LOW)
        for shard in range(shards):
            weight_grad_ref[shard, start : start + grads.shape[0], :] = grads[
                :, shard * width : (shard + 1) * width
            ]

    @pl.when(expert < experts)
    def _():
        number = first_ref[0] + expert
        slot = lax.broadcasted_iota(jnp.int32, (capacity, tokens), 0)
        slot_gates, parts, grad_parts = [], [], []
        for block, rows_ref, grad_ref in zip(blocks, row_refs, grad_refs):
            hit = slot == rank_row_ref[0, :, block]
            pick = hit.astype(FULL).astype(LOW)
            slot_gates.append(
                jnp.sum(jnp.where(hit, gate_row_ref[0, :, block], 0.0), axis=1, keepdims=True)
            )
            parts.append(dot_nn(pick, rows_ref[...]).astype(LOW))
            grad_parts.append(dot_nn(pick, grad_ref[...]))
        slot_gate = jnp.concatenate(slot_gates)
        picked = jnp.concatenate(parts)
        upstream = jnp.concatenate(grad_parts)
        gated = (slot_gate * upstream).astype(LOW)
        gate_part = gate_part_ref[0]
        up_part = up_part_ref[0]
        hidden = swiglu_low(gate_part, up_part)
        plain = dot_nt(upstream.astype(LOW), weight_ref[2 * hidden_width :, :])
        slot_grad = jnp.sum(hidden.astype(FULL) * plain, axis=1, keepdims=True)
        gate_grad, up_grad = swiglu_grads(gate_part, up_part, slot_gate * plain)
        gate_grad = gate_grad.astype(LOW)
        up_grad = up_grad.astype(LOW)
        put(0, dot_tn(gate_grad, picked))
        put(hidden_width, dot_tn(up_grad, picked))
        put(2 * hidden_width, dot_tn(hidden, gated))
        row_grad = dot_nn(gate_grad, weight_ref[:hidden_width, :])
        row_grad += dot_nn(up_grad, weight_ref[hidden_width : 2 * hidden_width, :])
        row_grad = row_grad.astype(LOW)
        lane = lax.broadcasted_iota(jnp.int32, (picked.shape[0], gate_total.shape[1]), 1)
        slot_grad = jnp.where(lane == number, slot_grad, 0.0).astype(LOW)
        for index, block in enumerate(blocks):
            rank_col = column_of(rank_col_ref[block, :], number)
            back = lax.broadcasted_iota(jnp.int32, (tokens, capacity), 1) == rank_col
            back = back.astype(FULL).astype(LOW)
            part = slice(index * capacity, (index + 1) * capacity)
            total[block, :] += dot_nn(back, row_grad[part])
            gate_total[block, :] += dot_nn(back, slot_grad[part])

    @pl.when(expert == experts)
    def _():
        weight_gate = weight_ref[:shared_width, :]
        weight_up = weight_ref[shared_width : 2 * shared_width, :]
        weight_down = weight_ref[2 * shared_width : 3 * shared_width, :]
        sums = [0.0, 0.0, 0.0]
        for block, rows_ref, grad_ref in zip(blocks, row_refs, grad_refs):
            rows = rows_ref[...]
            grads = grad_ref[...]
            gate_part = dot_nt(rows, weight_gate)
            up_part = dot_nt(rows, weight_up)
            hidden = swiglu_low(gate_part, up_part)
            gate_grad, up_grad = swiglu_grads(gate_part, up_part, dot_nt(grads, weight_down))
            gate_grad = gate_grad.astype(LOW)
            up_grad = up_grad.astype(LOW)
            pairs = ((gate_grad, rows), (up_grad, rows), (hidden, grads))
            sums = [item + dot_tn(*pair) for item, pair in zip(sums, pairs)]
            row_grad = dot_nn(gate_grad, weight_gate) + dot_nn(up_grad, weight_up)
            out_ref[block, :D] = (total[block, :] + row_grad).astype(LOW)
        for index, item in enumerate(sums):
            put(index * shared_width, item)
        out_ref[:, D:] = gate_total[...].astype(LOW)


def run_experts_back(
    first, rank_rows, rank_cols, gate_rows, mine, other, mine_grad, other_grad, weights,
    gate_part, up_part, capacity, hidden_width, shared_width, shards, gate_lanes,
):
    experts = rank_rows.shape[0]
    tokens = 2 * mine.shape[0]
    slots = 2 * capacity
    whole, fixed, row_spec, weight_spec, part_spec = expert_specs(
        experts, hidden_width, slots, tokens
    )
    return pl.pallas_call(
        functools.partial(expert_back_kernel, capacity, experts, shared_width),
        grid_spec=pltpu.PrefetchScalarGridSpec(
            num_scalar_prefetch=1,
            grid=(experts + 1,),
            in_specs=[
                row_spec,
                fixed(rank_cols),
                row_spec,
                fixed(mine),
                fixed(other),
                fixed(mine_grad),
                fixed(other_grad),
                weight_spec,
                part_spec,
                part_spec,
            ],
            out_specs=[
                pl.BlockSpec((tokens, D + gate_lanes), whole),
                pl.BlockSpec(
                    (shards, 3 * hidden_width, D // shards), lambda e, first_ref: (0, e, 0)
                ),
            ],
            scratch_shapes=[
                pltpu.VMEM((tokens, D), FULL),
                pltpu.VMEM((tokens, gate_lanes), FULL),
            ],
        ),
        out_shape=[
            jax.ShapeDtypeStruct((tokens, D + gate_lanes), LOW),
            jax.ShapeDtypeStruct((shards, weights.shape[0], D // shards), LOW),
        ],
        compiler_params=params_of(),
        name="experts_back",
    )(
        first, rank_rows, rank_cols, gate_rows, mine, other, mine_grad, other_grad, weights,
        gate_part, up_part,
    )


def head_kernel(valid_ref, rows_ref, table_ref, goal_ref, logit_ref, stat_ref, top, total, goal):
    step = pl.program_id(0)
    tokens = rows_ref.shape[0]
    block = table_ref.shape[0]
    lane = lax.broadcasted_iota(jnp.int32, (ROW_BLOCK, block), 1)

    @pl.when(step == 0)
    def _():
        top[...] = jnp.full_like(top, FAR)
        total[...] = jnp.zeros_like(total)
        goal[...] = jnp.zeros_like(goal)

    def work(masked):
        for start in range(0, tokens, ROW_BLOCK):
            part = slice(start, start + ROW_BLOCK)
            logits = dot_nt(rows_ref[part, :], table_ref[...])
            if masked:
                logits = jnp.where(lane < valid_ref[0] - step * block, logits, FAR)
            logit_ref[part, :] = logits
            old_top = top[part, :]
            new_top = jnp.maximum(old_top, jnp.max(logits, axis=1, keepdims=True))
            total[part, :] = total[part, :] * jnp.exp(old_top - new_top) + jnp.sum(
                jnp.exp(logits - new_top), axis=1, keepdims=True
            )
            top[part, :] = new_top
            hit = lane == goal_ref[part, :] - step * block
            goal[part, :] += jnp.sum(jnp.where(hit, logits, 0.0), axis=1, keepdims=True)

    inside = (step + 1) * block <= valid_ref[0]

    @pl.when(inside)
    def _():
        work(False)

    @pl.when(jnp.logical_not(inside))
    def _():
        work(True)

    @pl.when(step == pl.num_programs(0) - 1)
    def _():
        lane = lax.broadcasted_iota(jnp.int32, (tokens, LANES), 1)
        stat_ref[...] = jnp.where(
            lane == 0, top[...], jnp.where(lane == 1, total[...], goal[...])
        )


def run_head(rows, table, goal_local, valid):
    tokens = rows.shape[0]
    padded = table.shape[0]
    return pl.pallas_call(
        head_kernel,
        grid_spec=pltpu.PrefetchScalarGridSpec(
            num_scalar_prefetch=1,
            grid=(padded // VOCAB_BLOCK,),
            in_specs=[
                pl.BlockSpec((tokens, D), lambda j, valid_ref: (0, 0)),
                pl.BlockSpec((VOCAB_BLOCK, D), lambda j, valid_ref: (j, 0)),
                pl.BlockSpec((tokens, 1), lambda j, valid_ref: (0, 0)),
            ],
            out_specs=[
                pl.BlockSpec((tokens, VOCAB_BLOCK), lambda j, valid_ref: (0, j)),
                pl.BlockSpec((tokens, LANES), lambda j, valid_ref: (0, 0)),
            ],
            scratch_shapes=[pltpu.VMEM((tokens, 1), FULL)] * 3,
        ),
        out_shape=[
            jax.ShapeDtypeStruct((tokens, padded), FULL),
            jax.ShapeDtypeStruct((tokens, LANES), FULL),
        ],
        compiler_params=params_of(),
        name="head",
    )(valid, rows, table, goal_local)


def head_back_kernel(
    rows_ref, table_ref, goal_ref, scale_ref, logit_ref, out_ref, table_grad_ref, total, grads_ref
):
    step = pl.program_id(0)
    tokens = rows_ref.shape[0]
    block = table_ref.shape[0]
    shards, _, width = table_grad_ref.shape
    lane = lax.broadcasted_iota(jnp.int32, (ROW_BLOCK, block), 1)

    @pl.when(step == 0)
    def _():
        total[...] = jnp.zeros_like(total)

    for start in range(0, tokens, ROW_BLOCK):
        part = slice(start, start + ROW_BLOCK)
        grads = jnp.exp(logit_ref[part, :] - scale_ref[part, 0:1]) * scale_ref[part, 1:2]
        hit = lane == goal_ref[part, :] - step * block
        grads = jnp.where(hit, grads - 1.0, grads) * scale_ref[part, 2:3]
        grads = grads.astype(LOW)
        grads_ref[part, :] = grads
        total[part, :] += dot_nn(grads, table_ref[...])
    for shard in range(shards):
        cols = slice(shard * width, (shard + 1) * width)
        table_grad_ref[shard] = dot_tn(grads_ref[...], rows_ref[:, cols]).astype(LOW)

    @pl.when(step == pl.num_programs(0) - 1)
    def _():
        out_ref[...] = total[...].astype(LOW)


def run_head_back(rows, table, goal_local, scales, logits, shards):
    tokens = rows.shape[0]
    padded = table.shape[0]
    return pl.pallas_call(
        head_back_kernel,
        grid=(padded // VOCAB_BLOCK,),
        in_specs=[
            pl.BlockSpec((tokens, D), lambda j: (0, 0)),
            pl.BlockSpec((VOCAB_BLOCK, D), lambda j: (j, 0)),
            pl.BlockSpec((tokens, 1), lambda j: (0, 0)),
            pl.BlockSpec((tokens, 4), lambda j: (0, 0)),
            pl.BlockSpec((tokens, VOCAB_BLOCK), lambda j: (0, j)),
        ],
        out_specs=[
            pl.BlockSpec((tokens, D), lambda j: (0, 0)),
            pl.BlockSpec((shards, VOCAB_BLOCK, D // shards), lambda j: (0, j, 0)),
        ],
        out_shape=[
            jax.ShapeDtypeStruct((tokens, D), LOW),
            jax.ShapeDtypeStruct((shards, padded, D // shards), LOW),
        ],
        scratch_shapes=[
            pltpu.VMEM((tokens, D), FULL),
            pltpu.VMEM((tokens, VOCAB_BLOCK), LOW),
        ],
        compiler_params=params_of(),
        name="head_back",
    )(rows, table, goal_local, scales, logits)


def table_step_kernel(
    factor_ref, weight_ref, moment_ref, square_ref, first_ref, second_ref, *out_refs
):
    factor = factor_ref[0]

    def step(grads, rate):
        results = adam_update(
            weight_ref[0], moment_ref[0], square_ref[0], grads * factor, rate, DECAYS[0]
        )
        for ref, value in zip(out_refs, results):
            ref[0] = value

    @pl.when(pl.program_id(0) == 0)
    def _():
        step(first_ref[...], TABLE_RATES[0])

    @pl.when(pl.program_id(0) == 1)
    def _():
        step(second_ref[...].astype(FULL), TABLE_RATES[1])


def table_step(factor, weight, moment, square, first, second):
    vocab, width = weight.shape[1:]
    steps = pl.cdiv(vocab, STEP_BLOCK)
    block = pl.BlockSpec((1, STEP_BLOCK, width), lambda t, j, factor_ref: (t, j, 0))
    return pl.pallas_call(
        table_step_kernel,
        grid_spec=pltpu.PrefetchScalarGridSpec(
            num_scalar_prefetch=1,
            grid=(2, steps),
            in_specs=[
                block,
                block,
                block,
                pl.BlockSpec(
                    (STEP_BLOCK, width),
                    lambda t, j, factor_ref: (jnp.where(t == 0, j, steps - 1), 0),
                ),
                pl.BlockSpec(
                    (STEP_BLOCK, width), lambda t, j, factor_ref: (jnp.where(t == 1, j, 0), 0)
                ),
            ],
            out_specs=[block] * 3,
        ),
        out_shape=[jax.ShapeDtypeStruct(weight.shape, FULL)] * 3,
        compiler_params=params_of(2),
        name="table_step",
    )(factor, weight, moment, square, first, second)


def expert_step_kernel(factor_ref, core_ref, mine_ref, other_ref, *refs):
    factor = factor_ref[0]
    inner, outer = refs[:3], refs[3:6]
    inner_out, outer_out = refs[6:9], refs[9:]
    split = inner[0].shape[1]
    rows = mine_ref.shape[0]
    half = pl.num_programs(0) // 2

    def step(grads):
        for part, ins, outs, rate in (
            (slice(0, split), inner, inner_out, 6),
            (slice(split, rows), outer, outer_out, 7),
        ):
            results = adam_update(
                ins[0][0],
                ins[1][0],
                ins[2][0],
                grads[part, :].astype(FULL) * factor,
                RATES[rate + 1],
                DECAYS[rate + 1],
            )
            for ref, value in zip(outs, results):
                ref[0] = value

    is_mine = pl.program_id(0) // half == core_ref[0]

    @pl.when(is_mine)
    def _():
        step(mine_ref)

    @pl.when(jnp.logical_not(is_mine))
    def _():
        step(other_ref)


def expert_step(factor, core, mine, other, inner, outer):
    experts, _, width = inner[0].shape
    half = experts // 2
    rows = inner[0].shape[1] + outer[0].shape[1]
    spec = lambda item: pl.BlockSpec((1,) + item.shape[1:], lambda e, f_ref, c_ref: (e, 0, 0))
    held = lambda turn: pl.BlockSpec(
        (rows, width),
        lambda e, f_ref, c_ref: (
            jnp.clip(e - jnp.bitwise_xor(c_ref[0], turn) * half, 0, half - 1),
            0,
        ),
    )
    return pl.pallas_call(
        expert_step_kernel,
        grid_spec=pltpu.PrefetchScalarGridSpec(
            num_scalar_prefetch=2,
            grid=(experts,),
            in_specs=[held(0), held(1)] + [spec(item) for item in inner + outer],
            out_specs=[spec(item) for item in inner + outer],
        ),
        out_shape=[jax.ShapeDtypeStruct(item.shape, FULL) for item in inner + outer],
        compiler_params=params_of(),
        name="expert_step",
    )(factor, core, mine, other, *inner, *outer)


def rows_of_attention(item):
    return item.transpose(1, 2, 0).reshape(-1, item.shape[0])


def rows_of_shared(shared_in, shared_out, padded):
    width = shared_out.shape[1]
    shared = jnp.concatenate([shared_in.transpose(1, 2, 0), shared_out[None]])
    shared = shared.reshape(3, 2, -1, width).transpose(1, 0, 2, 3)
    shared = jnp.pad(shared, ((0, 0), (0, 0), (0, padded - shared.shape[2]), (0, 0)))
    return shared.reshape(2, -1, width)


def shards(
    token_ids,
    target_ids,
    counted,
    routes,
    vocab_tables,
    norm_gains,
    attn_in,
    attention_output_weight,
    router,
    shared_in,
    shared_out,
    expert_in,
    expert_out,
    vocab_tables_moment,
    norm_gains_moment,
    attn_in_moment,
    attn_out_moment,
    router_moment,
    shared_in_moment,
    shared_out_moment,
    expert_in_moment,
    expert_out_moment,
    vocab_tables_square,
    norm_gains_square,
    attn_in_square,
    attn_out_square,
    router_square,
    shared_in_square,
    shared_out_square,
    expert_in_square,
    expert_out_square,
):
    seq_rows, seqs = token_ids.shape
    tokens = seq_rows * seqs
    model_size = lax.axis_size("mp")
    model_place = lax.axis_index("mp")
    data_size = lax.axis_size("dp")
    data_place = lax.axis_index("dp")
    width = vocab_tables.shape[1]
    vocab = vocab_tables.shape[2]
    experts = expert_in.shape[0]
    expert_total = experts * model_size
    capacity = min(2 * tokens * TOPK // expert_total, tokens)
    hidden_width = expert_out.shape[2]
    head_width = attention_output_weight.shape[0]
    shared_width = shared_out.shape[0]
    own = tokens // model_size
    gate_lanes = round_up(expert_total, LANES)
    place = data_place.reshape(1).astype(jnp.int32)

    counts = counted.T.reshape(tokens).astype(FULL)
    small = jnp.concatenate(
        [
            token_ids.T.reshape(tokens).astype(FULL),
            lax.optimization_barrier(norm_gains.astype(LOW)).astype(FULL).reshape(-1),
            jnp.sum(counts).reshape(1),
        ]
    )
    small = jnp.pad(small, (0, round_up(small.shape[0], 1024) - small.shape[0]))
    small = lax.all_gather(small, "dp", axis=0, tiled=False)
    shared_half = shared_width // 2
    shared_pad = round_up(shared_half, 16)
    core = core_place()
    core_item = core.reshape(1).astype(jnp.int32)
    expert_halves = split_experts(
        core_item, expert_in, expert_out, rows_of_shared(shared_in, shared_out, shared_pad)
    )
    ids = small[:, :tokens].astype(jnp.int32)
    gains = small[:, tokens : tokens + 3 * width].reshape(data_size, 3, width)
    gains = gains.transpose(1, 0, 2).reshape(3, D)
    token_count = jnp.sum(small[:, tokens + 3 * width])

    marks = jnp.concatenate(
        [
            routes.transpose(2, 1, 0).reshape(TOPK, tokens),
            target_ids.T.reshape(1, tokens),
            counted.T.reshape(1, tokens),
        ]
    )
    marks = jnp.stack([marks, swap(marks, 1)], axis=1)

    small_pieces = gather_blocks(
        jnp.concatenate([rows_of_attention(attn_in), attention_output_weight, router.T]).astype(
            LOW
        ),
        False,
    )
    expert_all = gather_half(core_item, *expert_halves)
    tables = vocab_tables.transpose(0, 2, 1)
    padded = round_up(vocab, 2 * VOCAB_BLOCK)
    table_low = jnp.pad(tables[1].astype(LOW), ((0, padded - vocab), (0, 0)))
    table_low = table_low.reshape(2, padded // 2, width)
    table_half = lambda place: lax.dynamic_index_in_dim(table_low, place, 0, keepdims=False)
    table_all = gather_half(core_item, table_half(core), table_half(1 - core))
    local_ids = ids.reshape(data_size, model_size, own).transpose(1, 0, 2).reshape(-1)
    local_ids = local_ids - model_place * vocab
    inside = (local_ids >= 0) & (local_ids < vocab)
    looked_up = lookup(jnp.clip(local_ids, 0, vocab - 1), tables)
    looked_up = jnp.where(inside[:, None], looked_up, 0.0).astype(LOW)
    embedded = sum_rows(looked_up).astype(LOW).reshape(data_size, own, width)
    state_zero = lax.all_to_all(embedded, "dp", 0, 0, tiled=True)
    state_zero, *small_pieces = lax.optimization_barrier((state_zero, *small_pieces))
    small_all = jnp.concatenate(by_place(small_pieces), axis=1)
    attn_width = 4 * head_width
    weight_qkv = small_all[: 3 * head_width]
    weight_out = small_all[3 * head_width : attn_width]
    weight_router = small_all[attn_width:]
    state_zero = state_zero.transpose(1, 0, 2).reshape(own, D).astype(FULL)

    first_in = gather_rows(normed(state_zero, gains[0]).astype(LOW))
    projected = dot_nt(first_in, weight_qkv).astype(LOW)
    projected, weight_out = lax.optimization_barrier((projected, weight_out))
    weight_out_all = jnp.concatenate(
        [weight_out] + [shift(weight_out, step) for step in range(1, model_size)]
    )
    key_blocks = gather_blocks(projected[:, head_width:], True)
    attended, log_total = attend(place, projected, key_blocks, seqs)
    attended_pieces = attended.reshape(model_size, own, head_width)
    piece_of = lambda step: lax.dynamic_index_in_dim(
        attended_pieces, (model_place + step) % model_size, 0, keepdims=False
    )
    attended_own = [piece_of(0)] + [shift(piece_of(step), step) for step in range(1, model_size)]
    state_one = state_zero + dot_nn(jnp.concatenate(attended_own, axis=1), weight_out_all)

    expert_ids = jnp.arange(expert_total, dtype=jnp.int32)
    named = jnp.any(marks[:TOPK, :, None, :] == expert_ids[None, None, :, None], axis=0)
    earlier = jnp.arange(tokens)[:, None] < jnp.arange(tokens)[None, :]
    ranks = dot_nn(named.reshape(-1, tokens).astype(LOW), earlier.astype(LOW)).astype(jnp.int32)
    ranks = jnp.where(named, ranks.reshape(named.shape), -1)
    named_cols = named.transpose(0, 2, 1).reshape(2 * tokens, expert_total)
    rank_cols = ranks.transpose(0, 2, 1).reshape(2 * tokens, expert_total)
    part_experts = experts // 2
    first_expert = model_place * experts + core * part_experts
    local_rows = lambda table: lax.dynamic_slice_in_dim(table, first_expert, part_experts, 0)[
        :, None, :
    ]
    rank_rows = local_rows(ranks.transpose(1, 0, 2).reshape(expert_total, 2 * tokens))
    first_place = first_expert.reshape(1).astype(jnp.int32)
    second_in = gather_rows(normed(state_one, gains[1]).astype(LOW))
    second_other = swap(second_in, 1)
    router_logits = jnp.concatenate(
        [dot_nt(second_in, weight_router), dot_nt(second_other, weight_router)]
    )
    gates = jax.nn.softmax(jnp.where(named_cols, router_logits, FAR), axis=1)
    gates = jnp.where(named_cols, gates, 0.0)
    gate_rows = local_rows(gates.T)
    moe_part, gate_part, up_part = run_experts(
        first_place, rank_rows, rank_cols, gates, second_in, second_other, expert_all, capacity,
        hidden_width, shared_pad,
    )
    state_two = state_one + sum_rows(sum_pair(moe_part))

    third_in = pair_rows(gather_rows(normed(state_two, gains[2]).astype(LOW)))
    half_vocab = padded // 2
    goal_local = marks[TOPK].reshape(2 * tokens, 1) - model_place * vocab
    goal_local = jnp.where(goal_local < vocab, goal_local - core * half_vocab, -1)
    valid = (vocab - core * half_vocab).reshape(1).astype(jnp.int32)
    logits, stats = run_head(third_in, table_all, goal_local, valid)
    stats = stats[:, :3].T
    stats = join_stats([stats, jnp.roll(swap(stats, 1), tokens, axis=1)])
    stats = join_stats(
        [stats]
        + [
            lax.ppermute(stats, "mp", [(i, i ^ mask) for i in range(model_size)])
            for mask in range(1, model_size)
        ]
    )
    log_head = stats[0] + jnp.log(stats[1])
    goal_logit = stats[2]
    pair_counts = marks[TOPK + 1].reshape(2 * tokens).astype(FULL)
    loss_rows = pair_counts * (log_head - goal_logit + Z_COEF * log_head * log_head)
    loss_part = jnp.sum(loss_rows[:tokens])
    scales = jnp.stack(
        [log_head, 1.0 + 2.0 * Z_COEF * log_head, pair_counts / token_count, pair_counts], axis=1
    )
    third_part, table_part = run_head_back(
        third_in, table_all, goal_local, scales, logits, data_size // 2
    )
    table_second = scatter_half(table_part)
    state_two_grad, gain_three = norm_back(state_two, gains[2], sum_rows(sum_pair(third_part)))

    two_low = gather_rows(state_two_grad.astype(LOW))
    second_part, expert_part = run_experts_back(
        first_place, rank_rows, rank_cols, gate_rows, second_in, second_other, two_low,
        swap(two_low, 1), expert_all, gate_part, up_part, capacity, hidden_width, shared_pad,
        data_size // 2, gate_lanes,
    )
    expert_grad = scatter_half(expert_part)
    second_sum = sum_rows(sum_pair(second_part))
    second_grad = second_sum[:, :D]
    gate_grad = second_sum[:, D : D + expert_total]
    own_gates = lax.dynamic_slice_in_dim(gates, model_place * own, own, 0)
    choice_grad = own_gates * (
        gate_grad - jnp.sum(own_gates * gate_grad, axis=1, keepdims=True)
    )
    choice_grad = choice_grad.astype(LOW)
    second_grad = second_grad + dot_nn(choice_grad, weight_router)
    norm_grad, gain_two = norm_back(state_one, gains[1], second_grad)
    state_one_grad = state_two_grad + norm_grad

    own_low = state_one_grad.astype(LOW)
    out_grads = dot_nt(own_low, weight_out_all).astype(LOW)
    out_grad = jnp.zeros((tokens, head_width), LOW)
    for step in range(model_size):
        piece = out_grads[:, step * head_width : (step + 1) * head_width]
        if step > 0:
            piece = shift(piece, model_size - step)
        out_grad = lax.dynamic_update_slice(
            out_grad, piece, ((model_place + step) % model_size * own, 0)
        )
    own_low, out_grad = lax.optimization_barrier((own_low, out_grad))
    attn_out_grad = dot_tn(attended, gather_rows(own_low))
    query_grad, even_grads, odd_grads = attend_back(
        place, projected, log_total, out_grad, key_blocks, seqs, table_second
    )
    key_grad = scatter_blocks(even_grads, odd_grads, True).astype(LOW)
    projected_grad = jnp.concatenate([query_grad, key_grad], axis=1)
    first_part = dot_nn(projected_grad, weight_qkv).astype(LOW)
    attn_in_grad = dot_tn(projected_grad, first_in)
    attn_sums = scatter_features(jnp.concatenate([attn_in_grad, attn_out_grad]))
    norm_grad, gain_one = norm_back(state_zero, gains[0], sum_rows(first_part))
    state_zero_grad = state_one_grad + norm_grad

    tokens_part = data_size * own
    second_own = lax.dynamic_slice_in_dim(second_in, model_place * own, own, 0)
    gain_part = jnp.concatenate(
        [dot_tn(choice_grad, second_own), jnp.stack([gain_one, gain_two, gain_three])]
    ).astype(LOW)
    gain_rows = gain_part.shape[0]
    gain_pad = round_up(gain_rows, 16)
    gain_part = jnp.pad(gain_part, ((0, gain_pad - gain_rows), (0, 0)))
    back_rows = jnp.concatenate([state_zero_grad.astype(LOW), gain_part])
    back_rows = back_rows.reshape(own + gain_pad, data_size, width).transpose(1, 0, 2)
    back_rows = lax.all_to_all(back_rows, "dp", 0, 0, tiled=True)
    back_parts = [back_rows] + [
        lax.ppermute(back_rows, "mp", [(i, i ^ mask) for i in range(model_size)])
        for mask in range(1, model_size)
    ]
    id_parts = [
        lax.dynamic_slice_in_dim(
            local_ids, jnp.bitwise_xor(model_place, mask) * tokens_part, tokens_part, 0
        )
        for mask in range(model_size)
    ]
    square = lambda item: jnp.sum(jnp.square(item.astype(FULL)))
    bulk_square = square(table_second) + square(expert_grad)
    gain_sums = jnp.sum(
        sum(part[:, own : own + gain_rows].astype(FULL) for part in back_parts), axis=0
    )
    router_sums, gain_grad = gain_sums[:expert_total], gain_sums[expert_total:]
    table_first = []
    for part in (slice(0, 1), slice(1, model_size)):
        *table_first, first_square = table_grad(
            jnp.concatenate(id_parts[part]),
            jnp.concatenate([rows[:, :own].reshape(-1, width) for rows in back_parts[part]]),
            vocab,
            *table_first,
        )
    (table_first,) = table_first

    local_square = (
        bulk_square
        + jnp.sum(first_square)
        + square(attn_sums)
        + square(gain_sums) / model_size
    )
    table_second = in_order(*halves_back(table_second), 0)[:vocab]
    expert_grads = halves_back(expert_grad)
    shared_sums = in_order(
        *[
            item[3 * part_experts * hidden_width :].reshape(3, shared_pad, width)[:, :shared_half]
            for item in expert_grads
        ],
        1,
    ).astype(FULL)
    sums = jnp.stack([local_square, loss_part / model_size])
    sums = add_all(jnp.broadcast_to(sums[:, None], (2, LANES)))[:, 0]
    grad_norm = jnp.sqrt(sums[0])
    factor = CLIP / jnp.maximum(grad_norm, CLIP)

    table_results = table_step(
        factor.reshape(1),
        tables,
        vocab_tables_moment.transpose(0, 2, 1),
        vocab_tables_square.transpose(0, 2, 1),
        table_first,
        table_second,
    )
    results = [sums[1], token_count, grad_norm]
    results.extend(item.transpose(0, 2, 1) for item in table_results)
    gradients = (
        gain_grad,
        attn_sums[: 3 * head_width].reshape(3, head_width, width).transpose(2, 0, 1),
        attn_sums[3 * head_width :],
        router_sums.T,
        shared_sums[:2].transpose(2, 0, 1),
        shared_sums[2],
    )
    params = (
        norm_gains, attn_in, attention_output_weight, router, shared_in, shared_out,
    )
    moments = (
        norm_gains_moment, attn_in_moment, attn_out_moment, router_moment, shared_in_moment,
        shared_out_moment,
    )
    squares = (
        norm_gains_square, attn_in_square, attn_out_square, router_square, shared_in_square,
        shared_out_square,
    )
    for index in range(6):
        results.extend(
            adam_update(
                params[index],
                moments[index],
                squares[index],
                gradients[index] * factor,
                RATES[index + 1],
                DECAYS[index + 1],
            )
        )
    expert_results = expert_step(
        factor.reshape(1),
        core_item,
        *expert_grads,
        [
            item.transpose(0, 2, 3, 1).reshape(experts, 2 * hidden_width, width)
            for item in (expert_in, expert_in_moment, expert_in_square)
        ],
        [
            item.transpose(0, 2, 1)
            for item in (expert_out, expert_out_moment, expert_out_square)
        ],
    )
    results.extend(
        item.reshape(experts, 2, hidden_width, width).transpose(0, 3, 1, 2)
        for item in expert_results[:3]
    )
    results.extend(item.transpose(0, 2, 1) for item in expert_results[3:])
    return tuple(results)


def solution(mesh):
    in_specs = (
        P("dp", None),
        P("dp", None),
        P("dp", None),
        P("dp", None, None),
        P(None, "dp", "mp"),
        P(None, "dp"),
        P("dp", None, "mp"),
        P("mp", "dp"),
        P("dp", None),
        P("dp", None, "mp"),
        P("mp", "dp"),
        P("mp", "dp", None, None),
        P("mp", "dp", None),
        P(None, "dp", "mp"),
        P(None, "dp"),
        P("dp", None, "mp"),
        P("mp", "dp"),
        P("dp", None),
        P("dp", None, "mp"),
        P("mp", "dp"),
        P("mp", "dp", None, None),
        P("mp", "dp", None),
        P(None, "dp", "mp"),
        P(None, "dp"),
        P("dp", None, "mp"),
        P("mp", "dp"),
        P("dp", None),
        P("dp", None, "mp"),
        P("mp", "dp"),
        P("mp", "dp", None, None),
        P("mp", "dp", None),
    )
    out_specs = (
        P(),
        P(),
        P(),
        P(None, "dp", "mp"),
        P(None, "dp", "mp"),
        P(None, "dp", "mp"),
        P(None, "dp"),
        P(None, "dp"),
        P(None, "dp"),
        P("dp", None, "mp"),
        P("dp", None, "mp"),
        P("dp", None, "mp"),
        P("mp", "dp"),
        P("mp", "dp"),
        P("mp", "dp"),
        P("dp", None),
        P("dp", None),
        P("dp", None),
        P("dp", None, "mp"),
        P("dp", None, "mp"),
        P("dp", None, "mp"),
        P("mp", "dp"),
        P("mp", "dp"),
        P("mp", "dp"),
        P("mp", "dp", None, None),
        P("mp", "dp", None, None),
        P("mp", "dp", None, None),
        P("mp", "dp", None),
        P("mp", "dp", None),
        P("mp", "dp", None),
    )
    return jax.shard_map(shards, mesh=mesh, in_specs=in_specs, out_specs=out_specs, check_vma=False)
```

```python
import functools

import jax
import jax.numpy as jnp
from jax import lax
from jax.experimental import pallas as pl
from jax.experimental.pallas import tpu as pltpu
from jax.sharding import PartitionSpec as P

D = 1024
HD = 128
TOPK = 6
STEP = 10
LANES = 128
VOCAB_BLOCK = 1024
STEP_BLOCK = 2672
PAIR_BLOCK = 2304
ROW_BLOCK = 256

NORM_EPS = 1e-06
Z_COEF = 0.01
CLIP = 0.01
BETA_ONE = 0.9
BETA_TWO = 0.95
ADAM_EPS = 1e-08
TABLE_RATES = (1.0, 0.06)
RATES = (0.0, 1.0, 0.02, 0.05, 0.01, 0.02, 0.02, 0.02, 0.02)
DECAYS = (0.1, 0.0, 0.1, 0.1, 0.1, 0.1, 0.1, 0.1, 0.1)
FAR = -1e30
LOW = jnp.bfloat16
FULL = jnp.float32


def dot_nn(left, right):
    return lax.dot_general(left, right, (((1,), (0,)), ((), ())), preferred_element_type=FULL)


def dot_nt(left, right):
    return lax.dot_general(left, right, (((1,), (1,)), ((), ())), preferred_element_type=FULL)


def dot_tn(left, right):
    return lax.dot_general(left, right, (((0,), (0,)), ((), ())), preferred_element_type=FULL)


def params_of(dims=1, mib=50):
    return pltpu.CompilerParams(
        dimension_semantics=("arbitrary",) * dims, vmem_limit_bytes=mib * 1024 * 1024
    )


def round_up(number, unit):
    return (number + unit - 1) // unit * unit


def normed(values, gain_row):
    return (
        values * lax.rsqrt(jnp.mean(values * values, axis=-1, keepdims=True) + NORM_EPS) * gain_row
    )


def norm_back(values, gain_row, upstream):
    inv_rms = lax.rsqrt(jnp.mean(values * values, axis=-1, keepdims=True) + NORM_EPS)
    unit_rows = values * inv_rms
    scaled = upstream * gain_row
    gain_grad = jnp.sum(upstream * unit_rows, axis=0)
    return (
        inv_rms * (scaled - unit_rows * jnp.mean(scaled * unit_rows, axis=-1, keepdims=True)),
        gain_grad,
    )


def swiglu_grads(gate_part, up_part, upstream):
    sigmoid_gate = jax.nn.sigmoid(gate_part)
    silu_gate = gate_part * sigmoid_gate
    gate_grad = upstream * up_part * sigmoid_gate * (1.0 + gate_part * (1.0 - sigmoid_gate))
    return gate_grad, upstream * silu_gate


def adam_update(weight, moment, square, grad_item, rate, decay):
    new_moment = BETA_ONE * moment + (1.0 - BETA_ONE) * grad_item
    new_square = BETA_TWO * square + (1.0 - BETA_TWO) * grad_item * grad_item
    scaled = new_square * (1.0 / (1.0 - BETA_TWO**STEP))
    step_ratio = (new_moment * (1.0 / (1.0 - BETA_ONE**STEP))) / (
        scaled * lax.rsqrt(scaled) + ADAM_EPS
    )
    return (weight - rate * (step_ratio + decay * weight), new_moment, new_square)


def sum_rows(partial):
    size = lax.axis_size("mp")
    place = lax.axis_index("mp")
    pieces = partial.reshape((size, partial.shape[0] // size) + partial.shape[1:])
    total = lax.dynamic_index_in_dim(pieces, place, 0, keepdims=False).astype(FULL)
    for step in range(1, size):
        sent = lax.dynamic_index_in_dim(pieces, (place + step) % size, 0, keepdims=False)
        got = lax.ppermute(sent, "mp", [(i, (i + step) % size) for i in range(size)])
        total = total + got.astype(FULL)
    return total


def gather_rows(rows):
    size = lax.axis_size("mp")
    place = lax.axis_index("mp")
    count = rows.shape[0]
    whole = jnp.zeros((size * count,) + rows.shape[1:], rows.dtype)
    rest = (0,) * (rows.ndim - 1)
    whole = lax.dynamic_update_slice(whole, rows, (place * count,) + rest)
    for step in range(1, size):
        got = lax.ppermute(rows, "mp", [(i, (i + step) % size) for i in range(size)])
        whole = lax.dynamic_update_slice(whole, got, ((place - step) % size * count,) + rest)
    return whole


def swap(item, mask):
    size = lax.axis_size("dp")
    return lax.ppermute(item, "dp", [(i, i ^ mask) for i in range(size)])


def chips_of(size):
    return [list(range(core, size, 2)) for core in range(2)]


def core_place():
    return lax.axis_index("dp") % 2


def pair_rows(rows):
    return jnp.concatenate([rows, swap(rows, 1)])


def sum_pair(partial):
    count = partial.shape[0] // 2
    return (partial[:count].astype(FULL) + swap(partial[count:], 1).astype(FULL)).astype(LOW)


def in_order(mine, other, axis):
    first = core_place() == 0
    return jnp.concatenate(
        [jnp.where(first, mine, other), jnp.where(first, other, mine)], axis=axis
    )


def gather_half(core, mine, other):
    size = lax.axis_size("dp")
    return lax.all_gather(
        pair_features(core, mine, swap(other, 1)),
        "dp",
        axis=1,
        tiled=True,
        axis_index_groups=chips_of(size),
    )


def scatter_half(grads):
    size = lax.axis_size("dp")
    part = lax.psum_scatter(
        grads, "dp", scatter_dimension=0, tiled=False, axis_index_groups=chips_of(size)
    )
    return lax.optimization_barrier(part)


def gather_half(core, mine, other):
    size = lax.axis_size("dp")
    return lax.all_gather(
        pair_features(core, mine, swap(other, 1)),
        "dp",
        axis=1,
        tiled=True,
        axis_index_groups=chips_of(size),
    )


def scatter_half(grads):
    size = lax.axis_size("dp")
    part = lax.psum_scatter(
        grads, "dp", scatter_dimension=0, tiled=False, axis_index_groups=chips_of(size)
    )
    return lax.optimization_barrier(part)


def halves_back(part):
    width = part.shape[1] // 2
    place = core_place()
    mine = lax.dynamic_slice_in_dim(part, place * width, width, 1)
    return mine, swap(lax.dynamic_slice_in_dim(part, (1 - place) * width, width, 1), 1)


def by_place(pieces):
    place = lax.axis_index("dp")
    stacked = jnp.stack(pieces)
    return [
        lax.dynamic_index_in_dim(stacked, jnp.bitwise_xor(place, index), 0, keepdims=False)
        for index in range(len(pieces))
    ]


def pair_sums(grads):
    size = lax.axis_size("dp")
    place = lax.axis_index("dp")
    width = grads.shape[1] // size
    pieces = grads.astype(LOW).reshape(-1, size, width).transpose(1, 0, 2)
    picked = lambda core: jnp.stack(
        [
            lax.dynamic_index_in_dim(pieces, jnp.bitwise_xor(place, mask), 0, keepdims=False)
            for mask in range(core, size, 2)
        ]
    )
    return (picked(0).astype(FULL) + swap(picked(1), 1).astype(FULL)).astype(LOW)


def scatter_pairs(pairs, causal):
    total = pairs[0].astype(FULL)
    for index in range(1, pairs.shape[0]):
        mask = 2 * index
        keep = lambda i: not causal or i ^ mask < i
        total = total + send_blocks(pairs[index].astype(LOW), mask, keep).astype(FULL)
    return total


def tree_sum(items):
    while len(items) > 1:
        items = [items[index] + items[index + 1] for index in range(0, len(items), 2)]
    return items[0]


def add_all(item):
    item = item + swap(item, 1)
    item = tree_sum([item] + [swap(item, mask) for mask in range(2, lax.axis_size("dp"), 2)])
    size = lax.axis_size("mp")
    return tree_sum(
        [item]
        + [
            lax.ppermute(item, "mp", [(i, i ^ mask) for i in range(size)])
            for mask in range(1, size)
        ]
    )


def send_blocks(item, mask, keep):
    size = lax.axis_size("dp")
    return lax.ppermute(item, "dp", [(i, i ^ mask) for i in range(size) if keep(i)])


def gather_blocks(item, causal):
    both = []
    for mask in range(0, lax.axis_size("dp"), 2):
        block, keep = item, lambda i: not causal or i % 2 == 0
        if mask > 0:
            block = send_blocks(item, mask, lambda i: not causal or i ^ mask > i)
            keep = lambda i: not causal or i ^ mask < i
        both.extend([block, send_blocks(block, 1, keep)])
    return both


def shift(item, step):
    size = lax.axis_size("mp")
    return lax.ppermute(item, "mp", [(i, (i + step) % size) for i in range(size)])


def join_stats(parts):
    parts = jnp.stack(parts)
    top = jnp.max(parts[:, 0], axis=0)
    total = jnp.sum(parts[:, 1] * jnp.exp(parts[:, 0] - top), axis=0)
    return jnp.stack([top, total, jnp.sum(parts[:, 2], axis=0)])


def split_kernel(core_ref, inner_ref, outer_ref, shared_ref, out_ref):
    step = pl.program_id(0)
    steps = pl.num_programs(0)
    split = inner_ref.shape[1]

    @pl.when(step < steps - 1)
    def _():
        out_ref[:split, :] = inner_ref[0].astype(LOW)
        out_ref[split:, :] = outer_ref[0].astype(LOW)

    @pl.when(step == steps - 1)
    def _():
        out_ref[: shared_ref.shape[1], :] = shared_ref[0].astype(LOW)


def split_experts(core, expert_in, expert_out, shared):
    experts, width, _, hidden_width = expert_in.shape
    half = experts // 2
    rows = 3 * hidden_width

    def expert_of(step, core_ref):
        return (core_ref[0] * half + jnp.minimum(step, half - 1), 0, 0)

    return pl.pallas_call(
        split_kernel,
        grid_spec=pltpu.PrefetchScalarGridSpec(
            num_scalar_prefetch=1,
            grid=(half + 1,),
            in_specs=[
                pl.BlockSpec((1, 2 * hidden_width, width), expert_of),
                pl.BlockSpec((1, hidden_width, width), expert_of),
                pl.BlockSpec((1,) + shared.shape[1:], lambda j, core_ref: (core_ref[0], 0, 0)),
            ],
            out_specs=pl.BlockSpec((rows, width), lambda j, core_ref: (j, 0)),
        ),
        out_shape=jax.ShapeDtypeStruct((half * rows + shared.shape[1], width), LOW),
        compiler_params=params_of(),
        name="split_experts",
    )(
        core,
        expert_in.transpose(0, 2, 3, 1).reshape(experts, 2 * hidden_width, width),
        expert_out.transpose(0, 2, 1),
        shared,
    )


def pair_kernel(core_ref, mine_ref, other_ref, out_ref):
    width = mine_ref.shape[1]

    @pl.when(core_ref[0] == 0)
    def _():
        out_ref[:, :width] = mine_ref[...]
        out_ref[:, width:] = other_ref[...]

    @pl.when(core_ref[0] != 0)
    def _():
        out_ref[:, :width] = other_ref[...]
        out_ref[:, width:] = mine_ref[...]


def part_kernel(rows, core_ref, part_ref, mine_ref, other_ref, square_ref):
    step = pl.program_id(0)
    width = mine_ref.shape[1]

    @pl.when(step == 0)
    def _():
        square_ref[...] = jnp.zeros_like(square_ref)

    values = part_ref[...]
    for core in range(2):

        @pl.when(core_ref[0] == core)
        def _():
            mine_ref[...] = values[:, core * width : (core + 1) * width]
            other_ref[...] = values[:, (1 - core) * width : (2 - core) * width]

    values = values.astype(FULL)
    place = step * values.shape[0] + lax.broadcasted_iota(jnp.int32, values.shape, 0)
    values = jnp.where(place < rows, values * values, 0.0)
    square_ref[...] += jnp.sum(values.reshape(-1, 8, values.shape[1]), axis=0)


def part_features(core, part):
    rows, width = part.shape
    spec = pl.BlockSpec((PAIR_BLOCK, width // 2), lambda j, core_ref: (j, 0))
    mine, other, squares = pl.pallas_call(
        functools.partial(part_kernel, rows),
        grid_spec=pltpu.PrefetchScalarGridSpec(
            num_scalar_prefetch=1,
            grid=(pl.cdiv(rows, PAIR_BLOCK),),
            in_specs=[pl.BlockSpec((PAIR_BLOCK, width), lambda j, core_ref: (j, 0))],
            out_specs=[spec, spec, pl.BlockSpec((8, width), lambda j, core_ref: (0, 0))],
        ),
        out_shape=[jax.ShapeDtypeStruct((rows, width // 2), LOW)] * 2
        + [jax.ShapeDtypeStruct((8, width), FULL)],
        compiler_params=params_of(),
        name="part_features",
    )(core, part)
    return mine, other, jnp.sum(squares)


def pair_features(core, mine, other):
    rows, width = mine.shape
    spec = pl.BlockSpec((PAIR_BLOCK, width), lambda j, core_ref: (j, 0))
    return pl.pallas_call(
        pair_kernel,
        grid_spec=pltpu.PrefetchScalarGridSpec(
            num_scalar_prefetch=1,
            grid=(pl.cdiv(rows, PAIR_BLOCK),),
            in_specs=[spec, spec],
            out_specs=pl.BlockSpec((PAIR_BLOCK, 2 * width), lambda j, core_ref: (j, 0)),
        ),
        out_shape=jax.ShapeDtypeStruct((rows, 2 * width), LOW),
        compiler_params=params_of(),
        name="pair_features",
    )(core, mine, other)


def lookup_kernel(ids_ref, table_ref, out_ref):
    base = pl.program_id(0) * out_ref.shape[0]

    def copy_rows(step, carry):
        for inner in range(8):
            row = step * 8 + inner
            out_ref[pl.ds(row, 1), :] = table_ref[0, pl.ds(ids_ref[base + row], 1), :]
        return carry

    lax.fori_loop(0, out_ref.shape[0] // 8, copy_rows, 0)


def lookup(ids, tables):
    count = ids.shape[0]
    vocab, width = tables.shape[1:]
    block = 512
    return pl.pallas_call(
        lookup_kernel,
        grid_spec=pltpu.PrefetchScalarGridSpec(
            num_scalar_prefetch=1,
            grid=(count // block,),
            in_specs=[pl.BlockSpec((1, vocab, width), lambda i, ids_ref: (0, 0, 0))],
            out_specs=pl.BlockSpec((block, width), lambda i, ids_ref: (i, 0)),
        ),
        out_shape=jax.ShapeDtypeStruct((count, width), FULL),
        compiler_params=params_of(),
        name="lookup",
    )(ids, tables)


def table_grad_kernel(vocab, ids_ref, rows_ref, *refs):
    *before_refs, out_ref, square_ref = refs
    block = out_ref.shape[0]
    span = 512
    step = pl.program_id(0)
    token_of = step * block + lax.broadcasted_iota(jnp.int32, (block, span), 0)
    total = jnp.zeros(out_ref.shape, FULL)
    for start in range(0, rows_ref.shape[0], span):
        hit = (token_of == ids_ref[:, start : start + span]).astype(FULL).astype(LOW)
        total = total + dot_nn(hit, rows_ref[start : start + span, :])
    for before_ref in before_refs:
        total = total + before_ref[...]
    out_ref[...] = total

    @pl.when(step == 0)
    def _():
        square_ref[...] = jnp.zeros_like(square_ref)

    row = step * block + lax.broadcasted_iota(jnp.int32, total.shape, 0)
    kept = jnp.where(row < vocab, total * total, 0.0)
    square_ref[...] += jnp.sum(kept.reshape(-1, 8, total.shape[1]), axis=0)


def table_grad(ids, rows, vocab, *before):
    count, width = rows.shape
    block = pl.BlockSpec((VOCAB_BLOCK, width), lambda j: (j, 0))
    return pl.pallas_call(
        functools.partial(table_grad_kernel, vocab),
        grid=(pl.cdiv(vocab, VOCAB_BLOCK),),
        in_specs=[
            pl.BlockSpec((1, count), lambda j: (0, 0)),
            pl.BlockSpec((count, width), lambda j: (0, 0)),
        ]
        + [block] * len(before),
        out_specs=[block, pl.BlockSpec((8, width), lambda j: (0, 0))],
        out_shape=[
            jax.ShapeDtypeStruct((vocab, width), FULL),
            jax.ShapeDtypeStruct((8, width), FULL),
        ],
        compiler_params=params_of(),
        cost_estimate=pl.CostEstimate(
            flops=4 * count * vocab * width, bytes_accessed=8 * vocab * width, transcendentals=0
        ),
        name="table_grad",
    )(ids.reshape(1, count), rows, *before)


def masked_scores(place, query, keys, rows, blocks):
    scores = dot_nt(query, keys) * HD ** (-0.5)
    offset = lax.broadcasted_iota(jnp.int32, (1, rows), 1)
    key_pos = jnp.concatenate(
        [jnp.bitwise_xor(place, mask) * rows + offset for mask in range(blocks)], axis=1
    )
    query_pos = place * rows + lax.broadcasted_iota(jnp.int32, (rows, 1), 0)
    return jnp.where(key_pos <= query_pos, scores, FAR)


def head_cols(refs, index):
    return jnp.concatenate([ref[:, index * HD : (index + 1) * HD] for ref in refs], axis=0)


def attend_kernel(blocks, place_ref, query_ref, *refs):
    key_refs = refs[:blocks]
    out_ref, log_ref = refs[blocks:]
    place = place_ref[0]
    rows, width = query_ref.shape
    heads = width // HD
    for head in range(heads):
        cols = slice(head * HD, (head + 1) * HD)
        keys = head_cols(key_refs, head)
        values = head_cols(key_refs, heads + head)
        scores = masked_scores(place, query_ref[:, cols], keys, rows, blocks)
        top = jnp.max(scores, axis=1, keepdims=True)
        powers = jnp.exp(scores - top)
        total = jnp.sum(powers, axis=1, keepdims=True)
        probs = (powers * (1.0 / total)).astype(LOW)
        out_ref[:, cols] = dot_nn(probs, values).astype(LOW)
        log_ref[0, :, head : head + 1] = top + jnp.log(total)


def attend(place, projected, key_blocks, seqs):
    blocks = len(key_blocks)
    tokens = projected.shape[0]
    rows = tokens // seqs
    width = projected.shape[1] // 3
    heads = width // HD
    return pl.pallas_call(
        functools.partial(attend_kernel, blocks),
        grid_spec=pltpu.PrefetchScalarGridSpec(
            num_scalar_prefetch=1,
            grid=(seqs,),
            in_specs=[pl.BlockSpec((rows, width), lambda s, place_ref: (s, 0))]
            + [pl.BlockSpec((rows, 2 * width), lambda s, place_ref: (s, 0))] * blocks,
            out_specs=[
                pl.BlockSpec((rows, width), lambda s, place_ref: (s, 0)),
                pl.BlockSpec((1, rows, heads), lambda s, place_ref: (s, 0, 0)),
            ],
        ),
        out_shape=[
            jax.ShapeDtypeStruct((tokens, width), LOW),
            jax.ShapeDtypeStruct((seqs, rows, heads), FULL),
        ],
        compiler_params=params_of(),
        name="attend",
    )(place, projected, *key_blocks)


def attend_back_kernel(blocks, place_ref, query_ref, log_ref, grad_ref, after_ref, *refs):
    del after_ref
    key_refs = refs[:blocks]
    query_grad_ref = refs[blocks]
    key_grad_refs = refs[blocks + 1 :]
    place = place_ref[0]
    rows, width = query_ref.shape
    heads = width // HD
    for head in range(heads):
        cols = slice(head * HD, (head + 1) * HD)
        keys = head_cols(key_refs, head)
        values = head_cols(key_refs, heads + head)
        query = query_ref[:, cols]
        out_grad = grad_ref[:, cols]
        scores = masked_scores(place, query, keys, rows, blocks)
        probs = jnp.exp(scores - log_ref[0, :, head : head + 1])
        prob_grad = dot_nt(out_grad, values)
        delta = jnp.sum(probs * prob_grad, axis=1, keepdims=True)
        score_grad = (probs * (prob_grad - delta)).astype(LOW)
        query_grad_ref[:, cols] = (dot_nn(score_grad, keys) * HD ** (-0.5)).astype(LOW)
        key_grad = (dot_tn(score_grad, query) * HD ** (-0.5)).astype(LOW)
        value_grad = dot_tn(probs.astype(LOW), out_grad).astype(LOW)
        value_cols = slice((heads + head) * HD, (heads + head + 1) * HD)
        for mask in range(blocks):
            part = slice(mask * rows, (mask + 1) * rows)
            key_grad_refs[mask % 2][mask // 2, :, cols] = key_grad[part]
            key_grad_refs[mask % 2][mask // 2, :, value_cols] = value_grad[part]


def attend_back(place, projected, log_total, out_grad, key_blocks, seqs, after):
    blocks = len(key_blocks)
    tokens = projected.shape[0]
    rows = tokens // seqs
    width = projected.shape[1] // 3
    heads = width // HD
    row_spec = pl.BlockSpec((rows, width), lambda s, place_ref: (s, 0))
    key_spec = pl.BlockSpec((rows, 2 * width), lambda s, place_ref: (s, 0))
    return pl.pallas_call(
        functools.partial(attend_back_kernel, blocks),
        grid_spec=pltpu.PrefetchScalarGridSpec(
            num_scalar_prefetch=1,
            grid=(seqs,),
            in_specs=[
                row_spec,
                pl.BlockSpec((1, rows, heads), lambda s, place_ref: (s, 0, 0)),
                row_spec,
                pl.BlockSpec(memory_space=pl.ANY),
            ]
            + [key_spec] * blocks,
            out_specs=[row_spec]
            + [pl.BlockSpec((blocks // 2, rows, 2 * width), lambda s, place_ref: (0, s, 0))] * 2,
        ),
        out_shape=[jax.ShapeDtypeStruct((tokens, width), LOW)]
        + [jax.ShapeDtypeStruct((blocks // 2, tokens, 2 * width), LOW)] * 2,
        compiler_params=params_of(),
        name="attend_back",
    )(place, projected, log_total, out_grad, after, *key_blocks)


def column_of(table, index):
    lane = lax.broadcasted_iota(jnp.int32, table.shape, 1)
    return jnp.sum(jnp.where(lane == index, table, 0), axis=1, keepdims=True)


def swiglu_low(gate_part, up_part):
    return (gate_part * jax.nn.sigmoid(gate_part) * up_part).astype(LOW)


def expert_kernel(
    capacity,
    experts,
    shared_width,
    first_ref,
    rank_row_ref,
    rank_col_ref,
    gate_ref,
    mine_ref,
    other_ref,
    weight_ref,
    out_ref,
    gate_part_ref,
    up_part_ref,
    picked_ref,
    total,
):
    expert = pl.program_id(0)
    row_refs = (mine_ref, other_ref)
    tokens = mine_ref.shape[0]
    blocks = [slice(index * tokens, (index + 1) * tokens) for index in range(2)]
    hidden_width = weight_ref.shape[0] // 3

    @pl.when(expert == 0)
    def _():
        total[...] = jnp.zeros_like(total)

    @pl.when(expert < experts)
    def _():
        number = first_ref[0] + expert
        slot = lax.broadcasted_iota(jnp.int32, (capacity, tokens), 0)
        parts = []
        for block, rows_ref in zip(blocks, row_refs):
            pick = (slot == rank_row_ref[0, :, block]).astype(FULL).astype(LOW)
            parts.append(dot_nn(pick, rows_ref[...]).astype(LOW))
        picked = jnp.concatenate(parts)
        picked_ref[0] = picked
        gate_part = dot_nt(picked, weight_ref[:hidden_width, :])
        up_part = dot_nt(picked, weight_ref[hidden_width : 2 * hidden_width, :])
        gate_part_ref[0] = gate_part
        up_part_ref[0] = up_part
        hidden = swiglu_low(gate_part, up_part)
        output = dot_nn(hidden, weight_ref[2 * hidden_width :, :]).astype(LOW)
        for index, block in enumerate(blocks):
            rank_col = column_of(rank_col_ref[block, :], number)
            back = lax.broadcasted_iota(jnp.int32, (tokens, capacity), 1) == rank_col
            spread = dot_nn(
                back.astype(FULL).astype(LOW), output[index * capacity : (index + 1) * capacity]
            )
            total[block, :] += column_of(gate_ref[block, :], number) * spread

    @pl.when(expert == experts)
    def _():
        for block, rows_ref in zip(blocks, row_refs):
            rows = rows_ref[...]
            gate_part = dot_nt(rows, weight_ref[:shared_width, :])
            up_part = dot_nt(rows, weight_ref[shared_width : 2 * shared_width, :])
            hidden = swiglu_low(gate_part, up_part)
            part = dot_nn(hidden, weight_ref[2 * shared_width : 3 * shared_width, :])
            out_ref[block, :] = (total[block, :] + part).astype(LOW)


def expert_specs(experts, hidden_width, slots, tokens):
    whole = lambda e, first_ref: (0, 0)
    fixed = lambda item: pl.BlockSpec(item.shape, whole, pipeline_mode=pl.Buffered(1))
    part = lambda e, first_ref: (jnp.minimum(e, experts - 1), 0, 0)
    return (
        whole,
        fixed,
        pl.BlockSpec((1, 1, tokens), part),
        pl.BlockSpec((3 * hidden_width, D), lambda e, first_ref: (e, 0)),
        pl.BlockSpec((1, slots, hidden_width), part),
        pl.BlockSpec((1, slots, D), part),
    )


def run_experts(
    first, rank_rows, rank_cols, gates, mine, other, weights, capacity, hidden_width, shared_width
):
    experts = rank_rows.shape[0]
    tokens = 2 * mine.shape[0]
    slots = 2 * capacity
    whole, fixed, row_spec, weight_spec, part_spec, picked_spec = expert_specs(
        experts, hidden_width, slots, tokens
    )
    return pl.pallas_call(
        functools.partial(expert_kernel, capacity, experts, shared_width),
        grid_spec=pltpu.PrefetchScalarGridSpec(
            num_scalar_prefetch=1,
            grid=(experts + 1,),
            in_specs=[
                row_spec,
                fixed(rank_cols),
                fixed(gates),
                fixed(mine),
                fixed(other),
                weight_spec,
            ],
            out_specs=[pl.BlockSpec((tokens, D), whole), part_spec, part_spec, picked_spec],
            scratch_shapes=[pltpu.VMEM((tokens, D), FULL)],
        ),
        out_shape=[
            jax.ShapeDtypeStruct((tokens, D), LOW),
            jax.ShapeDtypeStruct((experts, slots, hidden_width), FULL),
            jax.ShapeDtypeStruct((experts, slots, hidden_width), FULL),
            jax.ShapeDtypeStruct((experts, slots, D), LOW),
        ],
        compiler_params=params_of(),
        name="experts",
    )(first, rank_rows, rank_cols, gates, mine, other, weights)


def expert_back_kernel(
    capacity,
    experts,
    shared_width,
    first_ref,
    rank_row_ref,
    rank_col_ref,
    gate_row_ref,
    mine_ref,
    other_ref,
    mine_grad_ref,
    other_grad_ref,
    weight_ref,
    gate_part_ref,
    up_part_ref,
    picked_ref,
    out_ref,
    weight_grad_ref,
    total,
    gate_total,
):
    expert = pl.program_id(0)
    row_refs = (mine_ref, other_ref)
    grad_refs = (mine_grad_ref, other_grad_ref)
    tokens = mine_ref.shape[0]
    blocks = [slice(index * tokens, (index + 1) * tokens) for index in range(2)]
    hidden_width = weight_ref.shape[0] // 3
    shards, _, width = weight_grad_ref.shape

    @pl.when(expert == 0)
    def _():
        total[...] = jnp.zeros_like(total)
        gate_total[...] = jnp.zeros_like(gate_total)

    def put(start, grads):
        grads = grads.astype(LOW)
        for shard in range(shards):
            weight_grad_ref[shard, start : start + grads.shape[0], :] = grads[
                :, shard * width : (shard + 1) * width
            ]

    @pl.when(expert < experts)
    def _():
        number = first_ref[0] + expert
        slot = lax.broadcasted_iota(jnp.int32, (capacity, tokens), 0)
        slot_gates, grad_parts = [], []
        for block, grad_ref in zip(blocks, grad_refs):
            hit = slot == rank_row_ref[0, :, block]
            pick = hit.astype(FULL).astype(LOW)
            slot_gates.append(
                jnp.sum(jnp.where(hit, gate_row_ref[0, :, block], 0.0), axis=1, keepdims=True)
            )
            grad_parts.append(dot_nn(pick, grad_ref[...]))
        slot_gate = jnp.concatenate(slot_gates)
        picked = picked_ref[0]
        upstream = jnp.concatenate(grad_parts)
        gated = (slot_gate * upstream).astype(LOW)
        gate_part = gate_part_ref[0]
        up_part = up_part_ref[0]
        hidden = swiglu_low(gate_part, up_part)
        plain = dot_nt(upstream.astype(LOW), weight_ref[2 * hidden_width :, :])
        slot_grad = jnp.sum(hidden.astype(FULL) * plain, axis=1, keepdims=True)
        gate_grad, up_grad = swiglu_grads(gate_part, up_part, slot_gate * plain)
        gate_grad = gate_grad.astype(LOW)
        up_grad = up_grad.astype(LOW)
        put(0, dot_tn(gate_grad, picked))
        put(hidden_width, dot_tn(up_grad, picked))
        put(2 * hidden_width, dot_tn(hidden, gated))
        row_grad = dot_nn(gate_grad, weight_ref[:hidden_width, :])
        row_grad += dot_nn(up_grad, weight_ref[hidden_width : 2 * hidden_width, :])
        row_grad = row_grad.astype(LOW)
        lane = lax.broadcasted_iota(jnp.int32, (picked.shape[0], gate_total.shape[1]), 1)
        slot_grad = jnp.where(lane == number, slot_grad, 0.0).astype(LOW)
        for index, block in enumerate(blocks):
            rank_col = column_of(rank_col_ref[block, :], number)
            back = lax.broadcasted_iota(jnp.int32, (tokens, capacity), 1) == rank_col
            back = back.astype(FULL).astype(LOW)
            part = slice(index * capacity, (index + 1) * capacity)
            total[block, :] += dot_nn(back, row_grad[part])
            gate_total[block, :] += dot_nn(back, slot_grad[part])

    @pl.when(expert == experts)
    def _():
        weight_gate = weight_ref[:shared_width, :]
        weight_up = weight_ref[shared_width : 2 * shared_width, :]
        weight_down = weight_ref[2 * shared_width : 3 * shared_width, :]
        sums = [0.0, 0.0, 0.0]
        for block, rows_ref, grad_ref in zip(blocks, row_refs, grad_refs):
            rows = rows_ref[...]
            grads = grad_ref[...]
            gate_part = dot_nt(rows, weight_gate)
            up_part = dot_nt(rows, weight_up)
            hidden = swiglu_low(gate_part, up_part)
            gate_grad, up_grad = swiglu_grads(gate_part, up_part, dot_nt(grads, weight_down))
            gate_grad = gate_grad.astype(LOW)
            up_grad = up_grad.astype(LOW)
            pairs = ((gate_grad, rows), (up_grad, rows), (hidden, grads))
            sums = [item + dot_tn(*pair) for item, pair in zip(sums, pairs)]
            row_grad = dot_nn(gate_grad, weight_gate) + dot_nn(up_grad, weight_up)
            out_ref[block, :D] = (total[block, :] + row_grad).astype(LOW)
        for index, item in enumerate(sums):
            put(index * shared_width, item)
        out_ref[:, D:] = gate_total[...].astype(LOW)


def run_experts_back(
    first, rank_rows, rank_cols, gate_rows, mine, other, mine_grad, other_grad, weights,
    gate_part, up_part, picked, capacity, hidden_width, shared_width, shards, gate_lanes,
):
    experts = rank_rows.shape[0]
    tokens = 2 * mine.shape[0]
    slots = 2 * capacity
    whole, fixed, row_spec, weight_spec, part_spec, picked_spec = expert_specs(
        experts, hidden_width, slots, tokens
    )
    return pl.pallas_call(
        functools.partial(expert_back_kernel, capacity, experts, shared_width),
        grid_spec=pltpu.PrefetchScalarGridSpec(
            num_scalar_prefetch=1,
            grid=(experts + 1,),
            in_specs=[
                row_spec,
                fixed(rank_cols),
                row_spec,
                fixed(mine),
                fixed(other),
                fixed(mine_grad),
                fixed(other_grad),
                weight_spec,
                part_spec,
                part_spec,
                picked_spec,
            ],
            out_specs=[
                pl.BlockSpec((tokens, D + gate_lanes), whole),
                pl.BlockSpec(
                    (shards, 3 * hidden_width, D // shards), lambda e, first_ref: (0, e, 0)
                ),
            ],
            scratch_shapes=[
                pltpu.VMEM((tokens, D), FULL),
                pltpu.VMEM((tokens, gate_lanes), FULL),
            ],
        ),
        out_shape=[
            jax.ShapeDtypeStruct((tokens, D + gate_lanes), LOW),
            jax.ShapeDtypeStruct((shards, weights.shape[0], D // shards), LOW),
        ],
        compiler_params=params_of(),
        name="experts_back",
    )(
        first, rank_rows, rank_cols, gate_rows, mine, other, mine_grad, other_grad, weights,
        gate_part, up_part, picked,
    )


def head_kernel(valid_ref, rows_ref, table_ref, goal_ref, logit_ref, stat_ref, top, total, goal):
    step = pl.program_id(0)
    tokens = rows_ref.shape[0]
    block = table_ref.shape[0]
    lane = lax.broadcasted_iota(jnp.int32, (ROW_BLOCK, block), 1)

    @pl.when(step == 0)
    def _():
        top[...] = jnp.full_like(top, FAR)
        total[...] = jnp.zeros_like(total)
        goal[...] = jnp.zeros_like(goal)

    def work(masked):
        for start in range(0, tokens, ROW_BLOCK):
            part = slice(start, start + ROW_BLOCK)
            logits = dot_nt(rows_ref[part, :], table_ref[...])
            if masked:
                logits = jnp.where(lane < valid_ref[0] - step * block, logits, FAR)
            logit_ref[part, :] = logits
            old_top = top[part, :]
            new_top = jnp.maximum(old_top, jnp.max(logits, axis=1, keepdims=True))
            total[part, :] = total[part, :] * jnp.exp(old_top - new_top) + jnp.sum(
                jnp.exp(logits - new_top), axis=1, keepdims=True
            )
            top[part, :] = new_top
            hit = lane == goal_ref[part, :] - step * block
            goal[part, :] += jnp.sum(jnp.where(hit, logits, 0.0), axis=1, keepdims=True)

    inside = (step + 1) * block <= valid_ref[0]

    @pl.when(inside)
    def _():
        work(False)

    @pl.when(jnp.logical_not(inside))
    def _():
        work(True)

    @pl.when(step == pl.num_programs(0) - 1)
    def _():
        lane = lax.broadcasted_iota(jnp.int32, (tokens, LANES), 1)
        stat_ref[...] = jnp.where(
            lane == 0, top[...], jnp.where(lane == 1, total[...], goal[...])
        )


def run_head(rows, table, goal_local, valid):
    tokens = rows.shape[0]
    padded = table.shape[0]
    return pl.pallas_call(
        head_kernel,
        grid_spec=pltpu.PrefetchScalarGridSpec(
            num_scalar_prefetch=1,
            grid=(padded // VOCAB_BLOCK,),
            in_specs=[
                pl.BlockSpec((tokens, D), lambda j, valid_ref: (0, 0)),
                pl.BlockSpec((VOCAB_BLOCK, D), lambda j, valid_ref: (j, 0)),
                pl.BlockSpec((tokens, 1), lambda j, valid_ref: (0, 0)),
            ],
            out_specs=[
                pl.BlockSpec((tokens, VOCAB_BLOCK), lambda j, valid_ref: (0, j)),
                pl.BlockSpec((tokens, LANES), lambda j, valid_ref: (0, 0)),
            ],
            scratch_shapes=[pltpu.VMEM((tokens, 1), FULL)] * 3,
        ),
        out_shape=[
            jax.ShapeDtypeStruct((tokens, padded), FULL),
            jax.ShapeDtypeStruct((tokens, LANES), FULL),
        ],
        compiler_params=params_of(),
        name="head",
    )(valid, rows, table, goal_local)


def head_back_kernel(
    rows_ref, table_ref, goal_ref, scale_ref, logit_ref, out_ref, table_grad_ref, total, grads_ref
):
    step = pl.program_id(0)
    tokens = rows_ref.shape[0]
    block = table_ref.shape[0]
    shards, _, width = table_grad_ref.shape
    lane = lax.broadcasted_iota(jnp.int32, (ROW_BLOCK, block), 1)

    @pl.when(step == 0)
    def _():
        total[...] = jnp.zeros_like(total)

    for start in range(0, tokens, ROW_BLOCK):
        part = slice(start, start + ROW_BLOCK)
        grads = jnp.exp(logit_ref[part, :] - scale_ref[part, 0:1]) * scale_ref[part, 1:2]
        hit = lane == goal_ref[part, :] - step * block
        grads = jnp.where(hit, grads - 1.0, grads) * scale_ref[part, 2:3]
        grads = grads.astype(LOW)
        grads_ref[part, :] = grads
        total[part, :] += dot_nn(grads, table_ref[...])
    turned = grads_ref[...].T
    for shard in range(shards):
        cols = slice(shard * width, (shard + 1) * width)
        table_grad_ref[shard] = dot_nn(turned, rows_ref[:, cols]).astype(LOW)

    @pl.when(step == pl.num_programs(0) - 1)
    def _():
        out_ref[...] = total[...].astype(LOW)


def run_head_back(rows, table, goal_local, scales, logits, shards):
    tokens = rows.shape[0]
    padded = table.shape[0]
    return pl.pallas_call(
        head_back_kernel,
        grid=(padded // VOCAB_BLOCK,),
        in_specs=[
            pl.BlockSpec((tokens, D), lambda j: (0, 0)),
            pl.BlockSpec((VOCAB_BLOCK, D), lambda j: (j, 0)),
            pl.BlockSpec((tokens, 1), lambda j: (0, 0)),
            pl.BlockSpec((tokens, 4), lambda j: (0, 0)),
            pl.BlockSpec((tokens, VOCAB_BLOCK), lambda j: (0, j)),
        ],
        out_specs=[
            pl.BlockSpec((tokens, D), lambda j: (0, 0)),
            pl.BlockSpec((shards, VOCAB_BLOCK, D // shards), lambda j: (0, j, 0)),
        ],
        out_shape=[
            jax.ShapeDtypeStruct((tokens, D), LOW),
            jax.ShapeDtypeStruct((shards, padded, D // shards), LOW),
        ],
        scratch_shapes=[
            pltpu.VMEM((tokens, D), FULL),
            pltpu.VMEM((tokens, VOCAB_BLOCK), LOW),
        ],
        compiler_params=params_of(),
        name="head_back",
    )(rows, table, goal_local, scales, logits)


def table_step_kernel(
    factor_ref, weight_ref, moment_ref, square_ref, first_ref, second_ref, *out_refs
):
    factor = factor_ref[0]

    def step(grads, rate):
        results = adam_update(
            weight_ref[0], moment_ref[0], square_ref[0], grads * factor, rate, DECAYS[0]
        )
        for ref, value in zip(out_refs, results):
            ref[0] = value

    @pl.when(pl.program_id(0) == 0)
    def _():
        step(first_ref[...], TABLE_RATES[0])

    @pl.when(pl.program_id(0) == 1)
    def _():
        step(second_ref[...].astype(FULL), TABLE_RATES[1])


def table_step(factor, weight, moment, square, first, second):
    vocab, width = weight.shape[1:]
    steps = pl.cdiv(vocab, STEP_BLOCK)
    block = pl.BlockSpec((1, STEP_BLOCK, width), lambda t, j, factor_ref: (t, j, 0))
    return pl.pallas_call(
        table_step_kernel,
        grid_spec=pltpu.PrefetchScalarGridSpec(
            num_scalar_prefetch=1,
            grid=(2, steps),
            in_specs=[
                block,
                block,
                block,
                pl.BlockSpec(
                    (STEP_BLOCK, width),
                    lambda t, j, factor_ref: (jnp.where(t == 0, j, steps - 1), 0),
                ),
                pl.BlockSpec(
                    (STEP_BLOCK, width), lambda t, j, factor_ref: (jnp.where(t == 1, j, 0), 0)
                ),
            ],
            out_specs=[block] * 3,
        ),
        out_shape=[jax.ShapeDtypeStruct(weight.shape, FULL)] * 3,
        compiler_params=params_of(2),
        name="table_step",
    )(factor, weight, moment, square, first, second)


def expert_step_kernel(factor_ref, core_ref, mine_ref, other_ref, *refs):
    factor = factor_ref[0]
    inner, outer = refs[:3], refs[3:6]
    inner_out, outer_out = refs[6:9], refs[9:]
    split = inner[0].shape[1]
    rows = mine_ref.shape[0]
    half = pl.num_programs(0) // 2

    def step(grads):
        for part, ins, outs, rate in (
            (slice(0, split), inner, inner_out, 6),
            (slice(split, rows), outer, outer_out, 7),
        ):
            results = adam_update(
                ins[0][0],
                ins[1][0],
                ins[2][0],
                grads[part, :].astype(FULL) * factor,
                RATES[rate + 1],
                DECAYS[rate + 1],
            )
            for ref, value in zip(outs, results):
                ref[0] = value

    is_mine = pl.program_id(0) // half == core_ref[0]

    @pl.when(is_mine)
    def _():
        step(mine_ref)

    @pl.when(jnp.logical_not(is_mine))
    def _():
        step(other_ref)


def expert_step(factor, core, mine, other, inner, outer):
    experts, _, width = inner[0].shape
    half = experts // 2
    rows = inner[0].shape[1] + outer[0].shape[1]
    spec = lambda item: pl.BlockSpec((1,) + item.shape[1:], lambda e, f_ref, c_ref: (e, 0, 0))
    held = lambda turn: pl.BlockSpec(
        (rows, width),
        lambda e, f_ref, c_ref: (
            jnp.clip(e - jnp.bitwise_xor(c_ref[0], turn) * half, 0, half - 1),
            0,
        ),
    )
    return pl.pallas_call(
        expert_step_kernel,
        grid_spec=pltpu.PrefetchScalarGridSpec(
            num_scalar_prefetch=2,
            grid=(experts,),
            in_specs=[held(0), held(1)] + [spec(item) for item in inner + outer],
            out_specs=[spec(item) for item in inner + outer],
        ),
        out_shape=[jax.ShapeDtypeStruct(item.shape, FULL) for item in inner + outer],
        compiler_params=params_of(),
        name="expert_step",
    )(factor, core, mine, other, *inner, *outer)


def rows_of_attention(item):
    return item.transpose(1, 2, 0).reshape(-1, item.shape[0])


def rows_of_shared(shared_in, shared_out, padded):
    width = shared_out.shape[1]
    shared = jnp.concatenate([shared_in.transpose(1, 2, 0), shared_out[None]])
    shared = shared.reshape(3, 2, -1, width).transpose(1, 0, 2, 3)
    shared = jnp.pad(shared, ((0, 0), (0, 0), (0, padded - shared.shape[2]), (0, 0)))
    return shared.reshape(2, -1, width)


def shards(
    token_ids,
    target_ids,
    counted,
    routes,
    vocab_tables,
    norm_gains,
    attn_in,
    attention_output_weight,
    router,
    shared_in,
    shared_out,
    expert_in,
    expert_out,
    vocab_tables_moment,
    norm_gains_moment,
    attn_in_moment,
    attn_out_moment,
    router_moment,
    shared_in_moment,
    shared_out_moment,
    expert_in_moment,
    expert_out_moment,
    vocab_tables_square,
    norm_gains_square,
    attn_in_square,
    attn_out_square,
    router_square,
    shared_in_square,
    shared_out_square,
    expert_in_square,
    expert_out_square,
):
    seq_rows, seqs = token_ids.shape
    tokens = seq_rows * seqs
    model_size = lax.axis_size("mp")
    model_place = lax.axis_index("mp")
    data_size = lax.axis_size("dp")
    data_place = lax.axis_index("dp")
    width = vocab_tables.shape[1]
    vocab = vocab_tables.shape[2]
    experts = expert_in.shape[0]
    expert_total = experts * model_size
    capacity = min(2 * tokens * TOPK // expert_total, tokens)
    hidden_width = expert_out.shape[2]
    head_width = attention_output_weight.shape[0]
    shared_width = shared_out.shape[0]
    own = tokens // model_size
    gate_lanes = round_up(expert_total, LANES)
    place = data_place.reshape(1).astype(jnp.int32)

    counts = counted.T.reshape(tokens).astype(FULL)
    small = jnp.concatenate(
        [
            token_ids.T.reshape(tokens).astype(FULL),
            lax.optimization_barrier(norm_gains.astype(LOW)).astype(FULL).reshape(-1),
            jnp.sum(counts).reshape(1),
        ]
    )
    small = jnp.pad(small, (0, round_up(small.shape[0], 1024) - small.shape[0]))
    small = lax.all_gather(small, "dp", axis=0, tiled=False)
    shared_half = shared_width // 2
    shared_pad = round_up(shared_half, 16)
    core = core_place()
    core_item = core.reshape(1).astype(jnp.int32)
    shared_rows = rows_of_shared(shared_in, shared_out, shared_pad)
    expert_other = split_experts(1 - core_item, expert_in, expert_out, shared_rows)
    expert_mine = split_experts(core_item, expert_in, expert_out, shared_rows)
    ids = small[:, :tokens].astype(jnp.int32)
    gains = small[:, tokens : tokens + 3 * width].reshape(data_size, 3, width)
    gains = gains.transpose(1, 0, 2).reshape(3, D)
    token_count = jnp.sum(small[:, tokens + 3 * width])

    marks = jnp.concatenate(
        [
            routes.transpose(2, 1, 0).reshape(TOPK, tokens),
            target_ids.T.reshape(1, tokens),
            counted.T.reshape(1, tokens),
        ]
    )
    marks = jnp.stack([marks, swap(marks, 1)], axis=1)

    small_pieces = gather_blocks(
        jnp.concatenate([rows_of_attention(attn_in), attention_output_weight, router.T]).astype(
            LOW
        ),
        False,
    )
    expert_all = gather_half(core_item, expert_mine, expert_other)
    tables = vocab_tables.transpose(0, 2, 1)
    padded = round_up(vocab, 2 * VOCAB_BLOCK)
    table_low = jnp.pad(tables[1].astype(LOW), ((0, padded - vocab), (0, 0)))
    table_low = table_low.reshape(2, padded // 2, width)
    table_half = lambda place: lax.dynamic_index_in_dim(table_low, place, 0, keepdims=False)
    table_all = gather_half(core_item, table_half(core), table_half(1 - core))
    local_ids = ids.reshape(data_size, model_size, own).transpose(1, 0, 2).reshape(-1)
    local_ids = local_ids - model_place * vocab
    inside = (local_ids >= 0) & (local_ids < vocab)
    looked_up = lookup(jnp.clip(local_ids, 0, vocab - 1), tables)
    looked_up = jnp.where(inside[:, None], looked_up, 0.0).astype(LOW)
    embedded = sum_rows(looked_up).astype(LOW).reshape(data_size, own, width)
    state_zero = lax.all_to_all(embedded, "dp", 0, 0, tiled=True)
    state_zero, *small_pieces = lax.optimization_barrier((state_zero, *small_pieces))
    small_all = jnp.concatenate(by_place(small_pieces), axis=1)
    attn_width = 4 * head_width
    weight_qkv = small_all[: 3 * head_width]
    weight_out = small_all[3 * head_width : attn_width]
    weight_router = small_all[attn_width:]
    state_zero = state_zero.transpose(1, 0, 2).reshape(own, D).astype(FULL)

    first_in = gather_rows(normed(state_zero, gains[0]).astype(LOW))
    projected = dot_nt(first_in, weight_qkv).astype(LOW)
    projected, weight_out = lax.optimization_barrier((projected, weight_out))
    weight_out_all = jnp.concatenate(
        [weight_out] + [shift(weight_out, step) for step in range(1, model_size)]
    )
    key_blocks = gather_blocks(projected[:, head_width:], True)
    attended, log_total = attend(place, projected, key_blocks, seqs)
    attended_pieces = attended.reshape(model_size, own, head_width)
    piece_of = lambda step: lax.dynamic_index_in_dim(
        attended_pieces, (model_place + step) % model_size, 0, keepdims=False
    )
    attended_own = [piece_of(0)] + [shift(piece_of(step), step) for step in range(1, model_size)]
    state_one = state_zero + dot_nn(jnp.concatenate(attended_own, axis=1), weight_out_all)

    expert_ids = jnp.arange(expert_total, dtype=jnp.int32)
    named = jnp.any(marks[:TOPK, :, None, :] == expert_ids[None, None, :, None], axis=0)
    earlier = jnp.arange(tokens)[:, None] < jnp.arange(tokens)[None, :]
    ranks = dot_nn(named.reshape(-1, tokens).astype(LOW), earlier.astype(LOW)).astype(jnp.int32)
    ranks = jnp.where(named, ranks.reshape(named.shape), -1)
    named_cols = named.transpose(0, 2, 1).reshape(2 * tokens, expert_total)
    rank_cols = ranks.transpose(0, 2, 1).reshape(2 * tokens, expert_total)
    part_experts = experts // 2
    first_expert = model_place * experts + core * part_experts
    local_rows = lambda table: lax.dynamic_slice_in_dim(table, first_expert, part_experts, 0)[
        :, None, :
    ]
    rank_rows = local_rows(ranks.transpose(1, 0, 2).reshape(expert_total, 2 * tokens))
    first_place = first_expert.reshape(1).astype(jnp.int32)
    second_in = gather_rows(normed(state_one, gains[1]).astype(LOW))
    second_other = swap(second_in, 1)
    router_logits = jnp.concatenate(
        [dot_nt(second_in, weight_router), dot_nt(second_other, weight_router)]
    )
    gates = jax.nn.softmax(jnp.where(named_cols, router_logits, FAR), axis=1)
    gates = jnp.where(named_cols, gates, 0.0)
    gate_rows = local_rows(gates.T)
    moe_part, gate_part, up_part, picked = run_experts(
        first_place, rank_rows, rank_cols, gates, second_in, second_other, expert_all, capacity,
        hidden_width, shared_pad,
    )
    state_two = state_one + sum_rows(sum_pair(moe_part))

    third_in = pair_rows(gather_rows(normed(state_two, gains[2]).astype(LOW)))
    half_vocab = padded // 2
    goal_local = marks[TOPK].reshape(2 * tokens, 1) - model_place * vocab
    goal_local = jnp.where(goal_local < vocab, goal_local - core * half_vocab, -1)
    valid = (vocab - core * half_vocab).reshape(1).astype(jnp.int32)
    logits, stats = run_head(third_in, table_all, goal_local, valid)
    stats = stats[:, :3].T
    stats = join_stats([stats, jnp.roll(swap(stats, 1), tokens, axis=1)])
    stats = join_stats(
        [stats]
        + [
            lax.ppermute(stats, "mp", [(i, i ^ mask) for i in range(model_size)])
            for mask in range(1, model_size)
        ]
    )
    log_head = stats[0] + jnp.log(stats[1])
    goal_logit = stats[2]
    pair_counts = marks[TOPK + 1].reshape(2 * tokens).astype(FULL)
    loss_rows = pair_counts * (log_head - goal_logit + Z_COEF * log_head * log_head)
    loss_part = jnp.sum(loss_rows[:tokens])
    scales = jnp.stack(
        [log_head, 1.0 + 2.0 * Z_COEF * log_head, pair_counts / token_count, pair_counts], axis=1
    )
    third_part, table_part = run_head_back(
        third_in, table_all, goal_local, scales, logits, data_size // 2
    )
    table_second = scatter_half(table_part)
    state_two_grad, gain_three = norm_back(state_two, gains[2], sum_rows(sum_pair(third_part)))

    two_low = gather_rows(state_two_grad.astype(LOW))
    second_part, expert_part = run_experts_back(
        first_place, rank_rows, rank_cols, gate_rows, second_in, second_other, two_low,
        swap(two_low, 1), expert_all, gate_part, up_part, picked, capacity, hidden_width, shared_pad,
        data_size // 2, gate_lanes,
    )
    expert_grad = scatter_half(expert_part)
    second_sum = sum_rows(sum_pair(second_part))
    second_grad = second_sum[:, :D]
    gate_grad = second_sum[:, D : D + expert_total]
    own_gates = lax.dynamic_slice_in_dim(gates, model_place * own, own, 0)
    choice_grad = own_gates * (
        gate_grad - jnp.sum(own_gates * gate_grad, axis=1, keepdims=True)
    )
    choice_grad = choice_grad.astype(LOW)
    second_grad = second_grad + dot_nn(choice_grad, weight_router)
    norm_grad, gain_two = norm_back(state_one, gains[1], second_grad)
    state_one_grad = state_two_grad + norm_grad

    own_low = state_one_grad.astype(LOW)
    out_grads = dot_nt(own_low, weight_out_all).astype(LOW)
    out_grad = jnp.zeros((tokens, head_width), LOW)
    for step in range(model_size):
        piece = out_grads[:, step * head_width : (step + 1) * head_width]
        if step > 0:
            piece = shift(piece, model_size - step)
        out_grad = lax.dynamic_update_slice(
            out_grad, piece, ((model_place + step) % model_size * own, 0)
        )
    own_low, out_grad = lax.optimization_barrier((own_low, out_grad))
    attn_out_grad = dot_tn(attended, gather_rows(own_low))
    query_grad, even_grads, odd_grads = attend_back(
        place, projected, log_total, out_grad, key_blocks, seqs, table_second
    )
    key_pairs = even_grads.astype(FULL) + swap(odd_grads, 1).astype(FULL)
    key_grad = scatter_pairs(key_pairs, True).astype(LOW)
    projected_grad = jnp.concatenate([query_grad, key_grad], axis=1)
    first_part = dot_nn(projected_grad, weight_qkv).astype(LOW)
    attn_in_grad = dot_tn(projected_grad, first_in)
    attn_pairs = pair_sums(jnp.concatenate([attn_in_grad, attn_out_grad]))
    norm_grad, gain_one = norm_back(state_zero, gains[0], sum_rows(first_part))
    state_zero_grad = state_one_grad + norm_grad

    tokens_part = data_size * own
    second_own = lax.dynamic_slice_in_dim(second_in, model_place * own, own, 0)
    gain_part = jnp.concatenate(
        [dot_tn(choice_grad, second_own), jnp.stack([gain_one, gain_two, gain_three])]
    ).astype(LOW)
    gain_rows = gain_part.shape[0]
    gain_pad = round_up(gain_rows, 16)
    gain_part = jnp.pad(gain_part, ((0, gain_pad - gain_rows), (0, 0)))
    back_rows = jnp.concatenate([state_zero_grad.astype(LOW), gain_part])
    back_rows = back_rows.reshape(own + gain_pad, data_size, width).transpose(1, 0, 2)
    attn_pairs, back_rows = lax.optimization_barrier((attn_pairs, back_rows))
    back_rows = lax.all_to_all(back_rows, "dp", 0, 0, tiled=True)
    attn_pairs, back_rows = lax.optimization_barrier((attn_pairs, back_rows))
    attn_sums = scatter_pairs(attn_pairs, False)
    back_parts = [back_rows] + [
        lax.ppermute(back_rows, "mp", [(i, i ^ mask) for i in range(model_size)])
        for mask in range(1, model_size)
    ]
    id_parts = [
        lax.dynamic_slice_in_dim(
            local_ids, jnp.bitwise_xor(model_place, mask) * tokens_part, tokens_part, 0
        )
        for mask in range(model_size)
    ]
    table_mine, table_other, second_square = part_features(core_item, table_second)
    table_other = swap(table_other, 1)
    second_square, back_parts[0] = lax.optimization_barrier((second_square, back_parts[0]))
    gain_sums = jnp.sum(
        sum(part[:, own : own + gain_rows].astype(FULL) for part in back_parts), axis=0
    )
    router_sums, gain_grad = gain_sums[:expert_total], gain_sums[expert_total:]
    table_first = []
    for part in (slice(0, 1), slice(1, model_size)):
        *table_first, first_square = table_grad(
            jnp.concatenate(id_parts[part]),
            jnp.concatenate([rows[:, :own].reshape(-1, width) for rows in back_parts[part]]),
            vocab,
            *table_first,
        )
    (table_first,) = table_first

    expert_grad_mine, expert_grad_other, expert_square = part_features(core_item, expert_grad)
    expert_grads = (expert_grad_mine, swap(expert_grad_other, 1))
    square = lambda item: jnp.sum(jnp.square(item))
    local_square = (
        second_square
        + expert_square
        + jnp.sum(first_square)
        + square(attn_sums)
        + square(gain_sums) / model_size
    )
    table_second = in_order(table_mine, table_other, 0)[:vocab]
    shared_sums = in_order(
        *[
            item[3 * part_experts * hidden_width :].reshape(3, shared_pad, width)[:, :shared_half]
            for item in expert_grads
        ],
        1,
    ).astype(FULL)
    sums = jnp.stack([local_square, loss_part / model_size])
    sums = add_all(jnp.broadcast_to(sums[:, None], (2, LANES)))[:, 0]
    grad_norm = jnp.sqrt(sums[0])
    factor = CLIP / jnp.maximum(grad_norm, CLIP)

    table_results = table_step(
        factor.reshape(1),
        tables,
        vocab_tables_moment.transpose(0, 2, 1),
        vocab_tables_square.transpose(0, 2, 1),
        table_first,
        table_second,
    )
    results = [sums[1], token_count, grad_norm]
    results.extend(item.transpose(0, 2, 1) for item in table_results)
    gradients = (
        gain_grad,
        attn_sums[: 3 * head_width].reshape(3, head_width, width).transpose(2, 0, 1),
        attn_sums[3 * head_width :],
        router_sums.T,
        shared_sums[:2].transpose(2, 0, 1),
        shared_sums[2],
    )
    params = (
        norm_gains, attn_in, attention_output_weight, router, shared_in, shared_out,
    )
    moments = (
        norm_gains_moment, attn_in_moment, attn_out_moment, router_moment, shared_in_moment,
        shared_out_moment,
    )
    squares = (
        norm_gains_square, attn_in_square, attn_out_square, router_square, shared_in_square,
        shared_out_square,
    )
    for index in range(6):
        results.extend(
            adam_update(
                params[index],
                moments[index],
                squares[index],
                gradients[index] * factor,
                RATES[index + 1],
                DECAYS[index + 1],
            )
        )
    expert_results = expert_step(
        factor.reshape(1),
        core_item,
        *expert_grads,
        [
            item.transpose(0, 2, 3, 1).reshape(experts, 2 * hidden_width, width)
            for item in (expert_in, expert_in_moment, expert_in_square)
        ],
        [
            item.transpose(0, 2, 1)
            for item in (expert_out, expert_out_moment, expert_out_square)
        ],
    )
    results.extend(
        item.reshape(experts, 2, hidden_width, width).transpose(0, 3, 1, 2)
        for item in expert_results[:3]
    )
    results.extend(item.transpose(0, 2, 1) for item in expert_results[3:])
    return tuple(results)


def solution(mesh):
    in_specs = (
        P("dp", None),
        P("dp", None),
        P("dp", None),
        P("dp", None, None),
        P(None, "dp", "mp"),
        P(None, "dp"),
        P("dp", None, "mp"),
        P("mp", "dp"),
        P("dp", None),
        P("dp", None, "mp"),
        P("mp", "dp"),
        P("mp", "dp", None, None),
        P("mp", "dp", None),
        P(None, "dp", "mp"),
        P(None, "dp"),
        P("dp", None, "mp"),
        P("mp", "dp"),
        P("dp", None),
        P("dp", None, "mp"),
        P("mp", "dp"),
        P("mp", "dp", None, None),
        P("mp", "dp", None),
        P(None, "dp", "mp"),
        P(None, "dp"),
        P("dp", None, "mp"),
        P("mp", "dp"),
        P("dp", None),
        P("dp", None, "mp"),
        P("mp", "dp"),
        P("mp", "dp", None, None),
        P("mp", "dp", None),
    )
    out_specs = (
        P(),
        P(),
        P(),
        P(None, "dp", "mp"),
        P(None, "dp", "mp"),
        P(None, "dp", "mp"),
        P(None, "dp"),
        P(None, "dp"),
        P(None, "dp"),
        P("dp", None, "mp"),
        P("dp", None, "mp"),
        P("dp", None, "mp"),
        P("mp", "dp"),
        P("mp", "dp"),
        P("mp", "dp"),
        P("dp", None),
        P("dp", None),
        P("dp", None),
        P("dp", None, "mp"),
        P("dp", None, "mp"),
        P("dp", None, "mp"),
        P("mp", "dp"),
        P("mp", "dp"),
        P("mp", "dp"),
        P("mp", "dp", None, None),
        P("mp", "dp", None, None),
        P("mp", "dp", None, None),
        P("mp", "dp", None),
        P("mp", "dp", None),
        P("mp", "dp", None),
    )
    return jax.shard_map(shards, mesh=mesh, in_specs=in_specs, out_specs=out_specs, check_vma=False)
```

```python
import functools

import jax
import jax.numpy as jnp
from jax import lax
from jax.experimental import pallas as pl
from jax.experimental.pallas import tpu as pltpu
from jax.sharding import PartitionSpec as P

D = 1024
HD = 128
TOPK = 6
STEP = 10
LANES = 128
VOCAB_BLOCK = 1024
STEP_BLOCK = 4008
BACK_BLOCK = 512
PAIR_BLOCK = 2304
ROW_BLOCK = 256

NORM_EPS = 1e-06
Z_COEF = 0.01
CLIP = 0.01
BETA_ONE = 0.9
BETA_TWO = 0.95
ADAM_EPS = 1e-08
TABLE_RATES = (1.0, 0.06)
RATES = (0.0, 1.0, 0.02, 0.05, 0.01, 0.02, 0.02, 0.02, 0.02)
DECAYS = (0.1, 0.0, 0.1, 0.1, 0.1, 0.1, 0.1, 0.1, 0.1)
FAR = -1e30
LOW = jnp.bfloat16
FULL = jnp.float32


def dot_nn(left, right):
    return lax.dot_general(left, right, (((1,), (0,)), ((), ())), preferred_element_type=FULL)


def dot_nt(left, right):
    return lax.dot_general(left, right, (((1,), (1,)), ((), ())), preferred_element_type=FULL)


def dot_tn(left, right):
    return lax.dot_general(left, right, (((0,), (0,)), ((), ())), preferred_element_type=FULL)


def params_of(dims=1, mib=50):
    return pltpu.CompilerParams(
        dimension_semantics=("arbitrary",) * dims, vmem_limit_bytes=mib * 1024 * 1024
    )


def round_up(number, unit):
    return (number + unit - 1) // unit * unit


def normed(values, gain_row):
    return (
        values * lax.rsqrt(jnp.mean(values * values, axis=-1, keepdims=True) + NORM_EPS) * gain_row
    )


def norm_back(values, gain_row, upstream):
    inv_rms = lax.rsqrt(jnp.mean(values * values, axis=-1, keepdims=True) + NORM_EPS)
    unit_rows = values * inv_rms
    scaled = upstream * gain_row
    gain_grad = jnp.sum(upstream * unit_rows, axis=0)
    return (
        inv_rms * (scaled - unit_rows * jnp.mean(scaled * unit_rows, axis=-1, keepdims=True)),
        gain_grad,
    )


def swiglu_grads(gate_part, up_part, upstream):
    sigmoid_gate = jax.nn.sigmoid(gate_part)
    silu_gate = gate_part * sigmoid_gate
    gate_grad = upstream * up_part * sigmoid_gate * (1.0 + gate_part * (1.0 - sigmoid_gate))
    return gate_grad, upstream * silu_gate


def adam_update(weight, moment, square, grad_item, rate, decay):
    new_moment = BETA_ONE * moment + (1.0 - BETA_ONE) * grad_item
    new_square = BETA_TWO * square + (1.0 - BETA_TWO) * grad_item * grad_item
    scaled = new_square * (1.0 / (1.0 - BETA_TWO**STEP))
    step_ratio = (new_moment * (1.0 / (1.0 - BETA_ONE**STEP))) / (
        scaled * lax.rsqrt(scaled) + ADAM_EPS
    )
    return (weight - rate * (step_ratio + decay * weight), new_moment, new_square)


def sum_rows(partial, ring=False):
    size = lax.axis_size("mp")
    place = lax.axis_index("mp")
    pieces = partial.reshape((size, partial.shape[0] // size) + partial.shape[1:])
    total = lax.dynamic_index_in_dim(pieces, place, 0, keepdims=False).astype(FULL)
    for step in range(1, size):
        other = (lambda i: (i + step) % size) if ring else (lambda i: i ^ step)
        target = (place + step) % size if ring else jnp.bitwise_xor(place, step)
        sent = lax.dynamic_index_in_dim(pieces, target, 0, keepdims=False)
        got = lax.ppermute(sent, "mp", [(i, other(i)) for i in range(size)])
        total = total + got.astype(FULL)
    return total


def gather_rows(rows):
    size = lax.axis_size("mp")
    place = lax.axis_index("mp")
    count = rows.shape[0]
    whole = jnp.zeros((size * count,) + rows.shape[1:], rows.dtype)
    rest = (0,) * (rows.ndim - 1)
    whole = lax.dynamic_update_slice(whole, rows, (place * count,) + rest)
    for step in range(1, size):
        got = lax.ppermute(rows, "mp", [(i, (i + step) % size) for i in range(size)])
        whole = lax.dynamic_update_slice(whole, got, ((place - step) % size * count,) + rest)
    return whole


def swap(item, mask):
    size = lax.axis_size("dp")
    return lax.ppermute(item, "dp", [(i, i ^ mask) for i in range(size)])


def chips_of(size):
    return [list(range(core, size, 2)) for core in range(2)]


def core_place():
    return lax.axis_index("dp") % 2


def pair_rows(rows):
    return jnp.concatenate([rows, swap(rows, 1)])


def sum_pair(partial):
    count = partial.shape[0] // 2
    return (partial[:count].astype(FULL) + swap(partial[count:], 1).astype(FULL)).astype(LOW)


def in_order(mine, other, axis):
    first = core_place() == 0
    return jnp.concatenate(
        [jnp.where(first, mine, other), jnp.where(first, other, mine)], axis=axis
    )


def gather_half(core, mine, other):
    size = lax.axis_size("dp")
    return lax.all_gather(
        pair_features(core, mine, swap(other, 1)),
        "dp",
        axis=1,
        tiled=True,
        axis_index_groups=chips_of(size),
    )


def scatter_half(grads):
    size = lax.axis_size("dp")
    part = lax.psum_scatter(
        grads, "dp", scatter_dimension=0, tiled=False, axis_index_groups=chips_of(size)
    )
    return lax.optimization_barrier(part)


def gather_half(core, mine, other):
    size = lax.axis_size("dp")
    return lax.all_gather(
        pair_features(core, mine, swap(other, 1)),
        "dp",
        axis=1,
        tiled=True,
        axis_index_groups=chips_of(size),
    )


def scatter_half(grads):
    size = lax.axis_size("dp")
    part = lax.psum_scatter(
        grads, "dp", scatter_dimension=0, tiled=False, axis_index_groups=chips_of(size)
    )
    return lax.optimization_barrier(part)


def halves_back(part):
    width = part.shape[1] // 2
    place = core_place()
    mine = lax.dynamic_slice_in_dim(part, place * width, width, 1)
    return mine, swap(lax.dynamic_slice_in_dim(part, (1 - place) * width, width, 1), 1)


def by_place(pieces):
    place = lax.axis_index("dp")
    stacked = jnp.stack(pieces)
    return [
        lax.dynamic_index_in_dim(stacked, jnp.bitwise_xor(place, index), 0, keepdims=False)
        for index in range(len(pieces))
    ]


def pair_sums(grads):
    size = lax.axis_size("dp")
    place = lax.axis_index("dp")
    width = grads.shape[1] // size
    pieces = grads.astype(LOW).reshape(-1, size, width).transpose(1, 0, 2)
    picked = lambda core: jnp.stack(
        [
            lax.dynamic_index_in_dim(pieces, jnp.bitwise_xor(place, mask), 0, keepdims=False)
            for mask in range(core, size, 2)
        ]
    )
    return (picked(0).astype(FULL) + swap(picked(1), 1).astype(FULL)).astype(LOW)


def scatter_pairs(pairs, causal):
    total = pairs[0].astype(FULL)
    for index in range(1, pairs.shape[0]):
        mask = 2 * index
        keep = lambda i: not causal or i ^ mask < i
        total = total + send_blocks(pairs[index].astype(LOW), mask, keep).astype(FULL)
    return total


def tree_sum(items):
    while len(items) > 1:
        items = [items[index] + items[index + 1] for index in range(0, len(items), 2)]
    return items[0]


def add_all(item):
    item = item + swap(item, 1)
    item = tree_sum([item] + [swap(item, mask) for mask in range(2, lax.axis_size("dp"), 2)])
    size = lax.axis_size("mp")
    return tree_sum(
        [item]
        + [
            lax.ppermute(item, "mp", [(i, i ^ mask) for i in range(size)])
            for mask in range(1, size)
        ]
    )


def send_blocks(item, mask, keep):
    size = lax.axis_size("dp")
    return lax.ppermute(item, "dp", [(i, i ^ mask) for i in range(size) if keep(i)])


def gather_blocks(item, causal):
    both = []
    for mask in range(0, lax.axis_size("dp"), 2):
        block, keep = item, lambda i: not causal or i % 2 == 0
        if mask > 0:
            block = send_blocks(item, mask, lambda i: not causal or i ^ mask > i)
            keep = lambda i: not causal or i ^ mask < i
        both.extend([block, send_blocks(block, 1, keep)])
    return both


def shift(item, step):
    size = lax.axis_size("mp")
    return lax.ppermute(item, "mp", [(i, (i + step) % size) for i in range(size)])


def join_stats(parts):
    parts = jnp.stack(parts)
    top = jnp.max(parts[:, 0], axis=0)
    total = jnp.sum(parts[:, 1] * jnp.exp(parts[:, 0] - top), axis=0)
    return jnp.stack([top, total, jnp.sum(parts[:, 2], axis=0)])


def split_kernel(core_ref, inner_ref, outer_ref, shared_ref, out_ref):
    step = pl.program_id(0)
    steps = pl.num_programs(0)
    split = inner_ref.shape[1]

    @pl.when(step < steps - 1)
    def _():
        out_ref[:split, :] = inner_ref[0].astype(LOW)
        out_ref[split:, :] = outer_ref[0].astype(LOW)

    @pl.when(step == steps - 1)
    def _():
        out_ref[: shared_ref.shape[1], :] = shared_ref[0].astype(LOW)


def split_experts(core, expert_in, expert_out, shared):
    experts, width, _, hidden_width = expert_in.shape
    half = experts // 2
    rows = 3 * hidden_width

    def expert_of(step, core_ref):
        return (core_ref[0] * half + jnp.minimum(step, half - 1), 0, 0)

    return pl.pallas_call(
        split_kernel,
        grid_spec=pltpu.PrefetchScalarGridSpec(
            num_scalar_prefetch=1,
            grid=(half + 1,),
            in_specs=[
                pl.BlockSpec((1, 2 * hidden_width, width), expert_of),
                pl.BlockSpec((1, hidden_width, width), expert_of),
                pl.BlockSpec((1,) + shared.shape[1:], lambda j, core_ref: (core_ref[0], 0, 0)),
            ],
            out_specs=pl.BlockSpec((rows, width), lambda j, core_ref: (j, 0)),
        ),
        out_shape=jax.ShapeDtypeStruct((half * rows + shared.shape[1], width), LOW),
        compiler_params=params_of(),
        name="split_experts",
    )(
        core,
        expert_in.transpose(0, 2, 3, 1).reshape(experts, 2 * hidden_width, width),
        expert_out.transpose(0, 2, 1),
        shared,
    )


def pair_kernel(core_ref, mine_ref, other_ref, out_ref):
    width = mine_ref.shape[1]

    @pl.when(core_ref[0] == 0)
    def _():
        out_ref[:, :width] = mine_ref[...]
        out_ref[:, width:] = other_ref[...]

    @pl.when(core_ref[0] != 0)
    def _():
        out_ref[:, :width] = other_ref[...]
        out_ref[:, width:] = mine_ref[...]


def part_kernel(rows, core_ref, part_ref, mine_ref, other_ref, square_ref):
    step = pl.program_id(0)
    width = mine_ref.shape[1]

    @pl.when(step == 0)
    def _():
        square_ref[...] = jnp.zeros_like(square_ref)

    values = part_ref[...]
    for core in range(2):

        @pl.when(core_ref[0] == core)
        def _():
            mine_ref[...] = values[:, core * width : (core + 1) * width]
            other_ref[...] = values[:, (1 - core) * width : (2 - core) * width]

    values = values.astype(FULL)
    place = step * values.shape[0] + lax.broadcasted_iota(jnp.int32, values.shape, 0)
    values = jnp.where(place < rows, values * values, 0.0)
    square_ref[...] += jnp.sum(values.reshape(-1, 8, values.shape[1]), axis=0)


def part_features(core, part):
    rows, width = part.shape
    spec = pl.BlockSpec((PAIR_BLOCK, width // 2), lambda j, core_ref: (j, 0))
    mine, other, squares = pl.pallas_call(
        functools.partial(part_kernel, rows),
        grid_spec=pltpu.PrefetchScalarGridSpec(
            num_scalar_prefetch=1,
            grid=(pl.cdiv(rows, PAIR_BLOCK),),
            in_specs=[pl.BlockSpec((PAIR_BLOCK, width), lambda j, core_ref: (j, 0))],
            out_specs=[spec, spec, pl.BlockSpec((8, width), lambda j, core_ref: (0, 0))],
        ),
        out_shape=[jax.ShapeDtypeStruct((rows, width // 2), LOW)] * 2
        + [jax.ShapeDtypeStruct((8, width), FULL)],
        compiler_params=params_of(),
        name="part_features",
    )(core, part)
    return mine, other, jnp.sum(squares)


def pair_features(core, mine, other):
    rows, width = mine.shape
    spec = pl.BlockSpec((PAIR_BLOCK, width), lambda j, core_ref: (j, 0))
    return pl.pallas_call(
        pair_kernel,
        grid_spec=pltpu.PrefetchScalarGridSpec(
            num_scalar_prefetch=1,
            grid=(pl.cdiv(rows, PAIR_BLOCK),),
            in_specs=[spec, spec],
            out_specs=pl.BlockSpec((PAIR_BLOCK, 2 * width), lambda j, core_ref: (j, 0)),
        ),
        out_shape=jax.ShapeDtypeStruct((rows, 2 * width), LOW),
        compiler_params=params_of(),
        name="pair_features",
    )(core, mine, other)


def lookup_kernel(ids_ref, table_ref, out_ref):
    base = pl.program_id(0) * out_ref.shape[0]

    def copy_rows(step, carry):
        for inner in range(8):
            row = step * 8 + inner
            out_ref[pl.ds(row, 1), :] = table_ref[0, pl.ds(ids_ref[base + row], 1), :]
        return carry

    lax.fori_loop(0, out_ref.shape[0] // 8, copy_rows, 0)


def lookup(ids, tables):
    count = ids.shape[0]
    vocab, width = tables.shape[1:]
    block = 512
    return pl.pallas_call(
        lookup_kernel,
        grid_spec=pltpu.PrefetchScalarGridSpec(
            num_scalar_prefetch=1,
            grid=(count // block,),
            in_specs=[pl.BlockSpec((1, vocab, width), lambda i, ids_ref: (0, 0, 0))],
            out_specs=pl.BlockSpec((block, width), lambda i, ids_ref: (i, 0)),
        ),
        out_shape=jax.ShapeDtypeStruct((count, width), FULL),
        compiler_params=params_of(),
        name="lookup",
    )(ids, tables)


def table_grad_kernel(vocab, ids_ref, rows_ref, *refs):
    *before_refs, out_ref, square_ref = refs
    block = out_ref.shape[0]
    span = 512
    step = pl.program_id(0)
    token_of = step * block + lax.broadcasted_iota(jnp.int32, (block, span), 0)
    total = jnp.zeros(out_ref.shape, FULL)
    for start in range(0, rows_ref.shape[0], span):
        hit = (token_of == ids_ref[:, start : start + span]).astype(FULL).astype(LOW)
        total = total + dot_nn(hit, rows_ref[start : start + span, :])
    for before_ref in before_refs:
        total = total + before_ref[...]
    out_ref[...] = total

    @pl.when(step == 0)
    def _():
        square_ref[...] = jnp.zeros_like(square_ref)

    row = step * block + lax.broadcasted_iota(jnp.int32, total.shape, 0)
    kept = jnp.where(row < vocab, total * total, 0.0)
    square_ref[...] += jnp.sum(kept.reshape(-1, 8, total.shape[1]), axis=0)


def table_grad(ids, rows, vocab, *before):
    count, width = rows.shape
    block = pl.BlockSpec((VOCAB_BLOCK, width), lambda j: (j, 0))
    return pl.pallas_call(
        functools.partial(table_grad_kernel, vocab),
        grid=(pl.cdiv(vocab, VOCAB_BLOCK),),
        in_specs=[
            pl.BlockSpec((1, count), lambda j: (0, 0)),
            pl.BlockSpec((count, width), lambda j: (0, 0)),
        ]
        + [block] * len(before),
        out_specs=[block, pl.BlockSpec((8, width), lambda j: (0, 0))],
        out_shape=[
            jax.ShapeDtypeStruct((vocab, width), FULL),
            jax.ShapeDtypeStruct((8, width), FULL),
        ],
        compiler_params=params_of(),
        cost_estimate=pl.CostEstimate(
            flops=4 * count * vocab * width, bytes_accessed=8 * vocab * width, transcendentals=0
        ),
        name="table_grad",
    )(ids.reshape(1, count), rows, *before)


def masked_scores(place, query, keys, rows, blocks):
    scores = dot_nt(query, keys) * HD ** (-0.5)
    offset = lax.broadcasted_iota(jnp.int32, (1, rows), 1)
    key_pos = jnp.concatenate(
        [jnp.bitwise_xor(place, mask) * rows + offset for mask in range(blocks)], axis=1
    )
    query_pos = place * rows + lax.broadcasted_iota(jnp.int32, (rows, 1), 0)
    return jnp.where(key_pos <= query_pos, scores, FAR)


def head_cols(refs, index):
    return jnp.concatenate([ref[:, index * HD : (index + 1) * HD] for ref in refs], axis=0)


def attend_kernel(blocks, place_ref, query_ref, *refs):
    key_refs = refs[:blocks]
    out_ref, log_ref = refs[blocks:]
    place = place_ref[0]
    rows, width = query_ref.shape
    heads = width // HD
    for head in range(heads):
        cols = slice(head * HD, (head + 1) * HD)
        keys = head_cols(key_refs, head)
        values = head_cols(key_refs, heads + head)
        scores = masked_scores(place, query_ref[:, cols], keys, rows, blocks)
        top = jnp.max(scores, axis=1, keepdims=True)
        powers = jnp.exp(scores - top)
        total = jnp.sum(powers, axis=1, keepdims=True)
        probs = (powers * (1.0 / total)).astype(LOW)
        out_ref[:, cols] = dot_nn(probs, values).astype(LOW)
        log_ref[0, :, head : head + 1] = top + jnp.log(total)


def attend(place, projected, key_blocks, seqs):
    blocks = len(key_blocks)
    tokens = projected.shape[0]
    rows = tokens // seqs
    width = projected.shape[1] // 3
    heads = width // HD
    return pl.pallas_call(
        functools.partial(attend_kernel, blocks),
        grid_spec=pltpu.PrefetchScalarGridSpec(
            num_scalar_prefetch=1,
            grid=(seqs,),
            in_specs=[pl.BlockSpec((rows, width), lambda s, place_ref: (s, 0))]
            + [pl.BlockSpec((rows, 2 * width), lambda s, place_ref: (s, 0))] * blocks,
            out_specs=[
                pl.BlockSpec((rows, width), lambda s, place_ref: (s, 0)),
                pl.BlockSpec((1, rows, heads), lambda s, place_ref: (s, 0, 0)),
            ],
        ),
        out_shape=[
            jax.ShapeDtypeStruct((tokens, width), LOW),
            jax.ShapeDtypeStruct((seqs, rows, heads), FULL),
        ],
        compiler_params=params_of(),
        name="attend",
    )(place, projected, *key_blocks)


def attend_back_kernel(blocks, place_ref, query_ref, log_ref, grad_ref, after_ref, *refs):
    del after_ref
    key_refs = refs[:blocks]
    query_grad_ref = refs[blocks]
    key_grad_refs = refs[blocks + 1 :]
    place = place_ref[0]
    rows, width = query_ref.shape
    heads = width // HD
    for head in range(heads):
        cols = slice(head * HD, (head + 1) * HD)
        keys = head_cols(key_refs, head)
        values = head_cols(key_refs, heads + head)
        query = query_ref[:, cols]
        out_grad = grad_ref[:, cols]
        scores = masked_scores(place, query, keys, rows, blocks)
        probs = jnp.exp(scores - log_ref[0, :, head : head + 1])
        prob_grad = dot_nt(out_grad, values)
        delta = jnp.sum(probs * prob_grad, axis=1, keepdims=True)
        score_grad = (probs * (prob_grad - delta)).astype(LOW)
        query_grad_ref[:, cols] = (dot_nn(score_grad, keys) * HD ** (-0.5)).astype(LOW)
        key_grad = (dot_tn(score_grad, query) * HD ** (-0.5)).astype(LOW)
        value_grad = dot_tn(probs.astype(LOW), out_grad).astype(LOW)
        value_cols = slice((heads + head) * HD, (heads + head + 1) * HD)
        for mask in range(blocks):
            part = slice(mask * rows, (mask + 1) * rows)
            key_grad_refs[mask % 2][mask // 2, :, cols] = key_grad[part]
            key_grad_refs[mask % 2][mask // 2, :, value_cols] = value_grad[part]


def attend_back(place, projected, log_total, out_grad, key_blocks, seqs, after):
    blocks = len(key_blocks)
    tokens = projected.shape[0]
    rows = tokens // seqs
    width = projected.shape[1] // 3
    heads = width // HD
    row_spec = pl.BlockSpec((rows, width), lambda s, place_ref: (s, 0))
    key_spec = pl.BlockSpec((rows, 2 * width), lambda s, place_ref: (s, 0))
    return pl.pallas_call(
        functools.partial(attend_back_kernel, blocks),
        grid_spec=pltpu.PrefetchScalarGridSpec(
            num_scalar_prefetch=1,
            grid=(seqs,),
            in_specs=[
                row_spec,
                pl.BlockSpec((1, rows, heads), lambda s, place_ref: (s, 0, 0)),
                row_spec,
                pl.BlockSpec(memory_space=pl.ANY),
            ]
            + [key_spec] * blocks,
            out_specs=[row_spec]
            + [pl.BlockSpec((blocks // 2, rows, 2 * width), lambda s, place_ref: (0, s, 0))] * 2,
        ),
        out_shape=[jax.ShapeDtypeStruct((tokens, width), LOW)]
        + [jax.ShapeDtypeStruct((blocks // 2, tokens, 2 * width), LOW)] * 2,
        compiler_params=params_of(),
        name="attend_back",
    )(place, projected, log_total, out_grad, after, *key_blocks)


def column_of(table, index):
    lane = lax.broadcasted_iota(jnp.int32, table.shape, 1)
    return jnp.sum(jnp.where(lane == index, table, 0), axis=1, keepdims=True)


def swiglu_low(gate_part, up_part):
    return (gate_part * jax.nn.sigmoid(gate_part) * up_part).astype(LOW)


def expert_kernel(
    capacity,
    experts,
    shared_width,
    first_ref,
    rank_row_ref,
    rank_col_ref,
    gate_ref,
    mine_ref,
    other_ref,
    weight_ref,
    out_ref,
    gate_part_ref,
    up_part_ref,
    picked_ref,
    total,
):
    expert = pl.program_id(0)
    row_refs = (mine_ref, other_ref)
    tokens = mine_ref.shape[0]
    blocks = [slice(index * tokens, (index + 1) * tokens) for index in range(2)]
    hidden_width = weight_ref.shape[0] // 3

    @pl.when(expert == 0)
    def _():
        total[...] = jnp.zeros_like(total)

    @pl.when(expert < experts)
    def _():
        number = first_ref[0] + expert
        slot = lax.broadcasted_iota(jnp.int32, (capacity, tokens), 0)
        parts = []
        for block, rows_ref in zip(blocks, row_refs):
            pick = (slot == rank_row_ref[0, :, block]).astype(FULL).astype(LOW)
            parts.append(dot_nn(pick, rows_ref[...]).astype(LOW))
        picked = jnp.concatenate(parts)
        picked_ref[0] = picked
        gate_part = dot_nt(picked, weight_ref[:hidden_width, :])
        up_part = dot_nt(picked, weight_ref[hidden_width : 2 * hidden_width, :])
        gate_part_ref[0] = gate_part
        up_part_ref[0] = up_part
        hidden = swiglu_low(gate_part, up_part)
        output = dot_nn(hidden, weight_ref[2 * hidden_width :, :]).astype(LOW)
        for index, block in enumerate(blocks):
            rank_col = column_of(rank_col_ref[block, :], number)
            back = lax.broadcasted_iota(jnp.int32, (tokens, capacity), 1) == rank_col
            spread = dot_nn(
                back.astype(FULL).astype(LOW), output[index * capacity : (index + 1) * capacity]
            )
            total[block, :] += column_of(gate_ref[block, :], number) * spread

    @pl.when(expert == experts)
    def _():
        for block, rows_ref in zip(blocks, row_refs):
            rows = rows_ref[...]
            gate_part = dot_nt(rows, weight_ref[:shared_width, :])
            up_part = dot_nt(rows, weight_ref[shared_width : 2 * shared_width, :])
            hidden = swiglu_low(gate_part, up_part)
            part = dot_nn(hidden, weight_ref[2 * shared_width : 3 * shared_width, :])
            out_ref[block, :] = (total[block, :] + part).astype(LOW)


def expert_specs(experts, hidden_width, slots, tokens):
    whole = lambda e, first_ref: (0, 0)
    fixed = lambda item: pl.BlockSpec(item.shape, whole, pipeline_mode=pl.Buffered(1))
    part = lambda e, first_ref: (jnp.minimum(e, experts - 1), 0, 0)
    return (
        whole,
        fixed,
        pl.BlockSpec((1, 1, tokens), part),
        pl.BlockSpec((3 * hidden_width, D), lambda e, first_ref: (e, 0)),
        pl.BlockSpec((1, slots, hidden_width), part),
        pl.BlockSpec((1, slots, D), part),
    )


def run_experts(
    first, rank_rows, rank_cols, gates, mine, other, weights, capacity, hidden_width, shared_width
):
    experts = rank_rows.shape[0]
    tokens = 2 * mine.shape[0]
    slots = 2 * capacity
    whole, fixed, row_spec, weight_spec, part_spec, picked_spec = expert_specs(
        experts, hidden_width, slots, tokens
    )
    return pl.pallas_call(
        functools.partial(expert_kernel, capacity, experts, shared_width),
        grid_spec=pltpu.PrefetchScalarGridSpec(
            num_scalar_prefetch=1,
            grid=(experts + 1,),
            in_specs=[
                row_spec,
                fixed(rank_cols),
                fixed(gates),
                fixed(mine),
                fixed(other),
                weight_spec,
            ],
            out_specs=[pl.BlockSpec((tokens, D), whole), part_spec, part_spec, picked_spec],
            scratch_shapes=[pltpu.VMEM((tokens, D), FULL)],
        ),
        out_shape=[
            jax.ShapeDtypeStruct((tokens, D), LOW),
            jax.ShapeDtypeStruct((experts, slots, hidden_width), FULL),
            jax.ShapeDtypeStruct((experts, slots, hidden_width), FULL),
            jax.ShapeDtypeStruct((experts, slots, D), LOW),
        ],
        compiler_params=params_of(),
        name="experts",
    )(first, rank_rows, rank_cols, gates, mine, other, weights)


def expert_back_kernel(
    capacity,
    experts,
    shared_width,
    first_ref,
    rank_row_ref,
    rank_col_ref,
    gate_row_ref,
    mine_ref,
    other_ref,
    mine_grad_ref,
    other_grad_ref,
    weight_ref,
    gate_part_ref,
    up_part_ref,
    picked_ref,
    out_ref,
    weight_grad_ref,
    total,
    gate_total,
):
    expert = pl.program_id(0)
    row_refs = (mine_ref, other_ref)
    grad_refs = (mine_grad_ref, other_grad_ref)
    tokens = mine_ref.shape[0]
    blocks = [slice(index * tokens, (index + 1) * tokens) for index in range(2)]
    hidden_width = weight_ref.shape[0] // 3
    shards, _, width = weight_grad_ref.shape

    @pl.when(expert == 0)
    def _():
        total[...] = jnp.zeros_like(total)
        gate_total[...] = jnp.zeros_like(gate_total)

    def put(start, grads):
        grads = grads.astype(LOW)
        for shard in range(shards):
            weight_grad_ref[shard, start : start + grads.shape[0], :] = grads[
                :, shard * width : (shard + 1) * width
            ]

    @pl.when(expert < experts)
    def _():
        number = first_ref[0] + expert
        slot = lax.broadcasted_iota(jnp.int32, (capacity, tokens), 0)
        slot_gates, grad_parts = [], []
        for block, grad_ref in zip(blocks, grad_refs):
            hit = slot == rank_row_ref[0, :, block]
            pick = hit.astype(FULL).astype(LOW)
            slot_gates.append(
                jnp.sum(jnp.where(hit, gate_row_ref[0, :, block], 0.0), axis=1, keepdims=True)
            )
            grad_parts.append(dot_nn(pick, grad_ref[...]))
        slot_gate = jnp.concatenate(slot_gates)
        picked = picked_ref[0]
        upstream = jnp.concatenate(grad_parts)
        gated = (slot_gate * upstream).astype(LOW)
        gate_part = gate_part_ref[0]
        up_part = up_part_ref[0]
        hidden = swiglu_low(gate_part, up_part)
        plain = dot_nt(upstream.astype(LOW), weight_ref[2 * hidden_width :, :])
        slot_grad = jnp.sum(hidden.astype(FULL) * plain, axis=1, keepdims=True)
        gate_grad, up_grad = swiglu_grads(gate_part, up_part, slot_gate * plain)
        gate_grad = gate_grad.astype(LOW)
        up_grad = up_grad.astype(LOW)
        put(0, dot_tn(gate_grad, picked))
        put(hidden_width, dot_tn(up_grad, picked))
        put(2 * hidden_width, dot_tn(hidden, gated))
        row_grad = dot_nn(gate_grad, weight_ref[:hidden_width, :])
        row_grad += dot_nn(up_grad, weight_ref[hidden_width : 2 * hidden_width, :])
        row_grad = row_grad.astype(LOW)
        lane = lax.broadcasted_iota(jnp.int32, (picked.shape[0], gate_total.shape[1]), 1)
        slot_grad = jnp.where(lane == number, slot_grad, 0.0).astype(LOW)
        for index, block in enumerate(blocks):
            rank_col = column_of(rank_col_ref[block, :], number)
            back = lax.broadcasted_iota(jnp.int32, (tokens, capacity), 1) == rank_col
            back = back.astype(FULL).astype(LOW)
            part = slice(index * capacity, (index + 1) * capacity)
            total[block, :] += dot_nn(back, row_grad[part])
            gate_total[block, :] += dot_nn(back, slot_grad[part])

    @pl.when(expert == experts)
    def _():
        weight_gate = weight_ref[:shared_width, :]
        weight_up = weight_ref[shared_width : 2 * shared_width, :]
        weight_down = weight_ref[2 * shared_width : 3 * shared_width, :]
        sums = [0.0, 0.0, 0.0]
        for block, rows_ref, grad_ref in zip(blocks, row_refs, grad_refs):
            rows = rows_ref[...]
            grads = grad_ref[...]
            gate_part = dot_nt(rows, weight_gate)
            up_part = dot_nt(rows, weight_up)
            hidden = swiglu_low(gate_part, up_part)
            gate_grad, up_grad = swiglu_grads(gate_part, up_part, dot_nt(grads, weight_down))
            gate_grad = gate_grad.astype(LOW)
            up_grad = up_grad.astype(LOW)
            pairs = ((gate_grad, rows), (up_grad, rows), (hidden, grads))
            sums = [item + dot_tn(*pair) for item, pair in zip(sums, pairs)]
            row_grad = dot_nn(gate_grad, weight_gate) + dot_nn(up_grad, weight_up)
            out_ref[block, :D] = (total[block, :] + row_grad).astype(LOW)
        for index, item in enumerate(sums):
            put(index * shared_width, item)
        out_ref[:, D:] = gate_total[...].astype(LOW)


def run_experts_back(
    first, rank_rows, rank_cols, gate_rows, mine, other, mine_grad, other_grad, weights,
    gate_part, up_part, picked, capacity, hidden_width, shared_width, shards, gate_lanes,
):
    experts = rank_rows.shape[0]
    tokens = 2 * mine.shape[0]
    slots = 2 * capacity
    whole, fixed, row_spec, weight_spec, part_spec, picked_spec = expert_specs(
        experts, hidden_width, slots, tokens
    )
    return pl.pallas_call(
        functools.partial(expert_back_kernel, capacity, experts, shared_width),
        grid_spec=pltpu.PrefetchScalarGridSpec(
            num_scalar_prefetch=1,
            grid=(experts + 1,),
            in_specs=[
                row_spec,
                fixed(rank_cols),
                row_spec,
                fixed(mine),
                fixed(other),
                fixed(mine_grad),
                fixed(other_grad),
                weight_spec,
                part_spec,
                part_spec,
                picked_spec,
            ],
            out_specs=[
                pl.BlockSpec((tokens, D + gate_lanes), whole),
                pl.BlockSpec(
                    (shards, 3 * hidden_width, D // shards), lambda e, first_ref: (0, e, 0)
                ),
            ],
            scratch_shapes=[
                pltpu.VMEM((tokens, D), FULL),
                pltpu.VMEM((tokens, gate_lanes), FULL),
            ],
        ),
        out_shape=[
            jax.ShapeDtypeStruct((tokens, D + gate_lanes), LOW),
            jax.ShapeDtypeStruct((shards, weights.shape[0], D // shards), LOW),
        ],
        compiler_params=params_of(),
        name="experts_back",
    )(
        first, rank_rows, rank_cols, gate_rows, mine, other, mine_grad, other_grad, weights,
        gate_part, up_part, picked,
    )


def head_kernel(valid_ref, rows_ref, table_ref, goal_ref, logit_ref, stat_ref, top, total, goal):
    step = pl.program_id(0)
    tokens = rows_ref.shape[0]
    block = table_ref.shape[0]
    lane = lax.broadcasted_iota(jnp.int32, (ROW_BLOCK, block), 1)

    @pl.when(step == 0)
    def _():
        top[...] = jnp.full_like(top, FAR)
        total[...] = jnp.zeros_like(total)
        goal[...] = jnp.zeros_like(goal)

    def work(masked):
        for start in range(0, tokens, ROW_BLOCK):
            part = slice(start, start + ROW_BLOCK)
            logits = dot_nt(rows_ref[part, :], table_ref[...])
            if masked:
                logits = jnp.where(lane < valid_ref[0] - step * block, logits, FAR)
            logit_ref[part, :] = logits
            old_top = top[part, :]
            new_top = jnp.maximum(old_top, jnp.max(logits, axis=1, keepdims=True))
            total[part, :] = total[part, :] * jnp.exp(old_top - new_top) + jnp.sum(
                jnp.exp(logits - new_top), axis=1, keepdims=True
            )
            top[part, :] = new_top
            hit = lane == goal_ref[part, :] - step * block
            goal[part, :] += jnp.sum(jnp.where(hit, logits, 0.0), axis=1, keepdims=True)

    inside = (step + 1) * block <= valid_ref[0]

    @pl.when(inside)
    def _():
        work(False)

    @pl.when(jnp.logical_not(inside))
    def _():
        work(True)

    @pl.when(step == pl.num_programs(0) - 1)
    def _():
        lane = lax.broadcasted_iota(jnp.int32, (tokens, LANES), 1)
        stat_ref[...] = jnp.where(
            lane == 0, top[...], jnp.where(lane == 1, total[...], goal[...])
        )


def run_head(rows, table, goal_local, valid):
    tokens = rows.shape[0]
    padded = table.shape[0]
    return pl.pallas_call(
        head_kernel,
        grid_spec=pltpu.PrefetchScalarGridSpec(
            num_scalar_prefetch=1,
            grid=(padded // VOCAB_BLOCK,),
            in_specs=[
                pl.BlockSpec((tokens, D), lambda j, valid_ref: (0, 0)),
                pl.BlockSpec((VOCAB_BLOCK, D), lambda j, valid_ref: (j, 0)),
                pl.BlockSpec((tokens, 1), lambda j, valid_ref: (0, 0)),
            ],
            out_specs=[
                pl.BlockSpec((tokens, VOCAB_BLOCK), lambda j, valid_ref: (0, j)),
                pl.BlockSpec((tokens, LANES), lambda j, valid_ref: (0, 0)),
            ],
            scratch_shapes=[pltpu.VMEM((tokens, 1), FULL)] * 3,
        ),
        out_shape=[
            jax.ShapeDtypeStruct((tokens, padded), FULL),
            jax.ShapeDtypeStruct((tokens, LANES), FULL),
        ],
        compiler_params=params_of(),
        name="head",
    )(valid, rows, table, goal_local)


def head_back_kernel(
    rows_ref, table_ref, goal_ref, scale_ref, logit_ref, out_ref, table_grad_ref, total, grads_ref
):
    step = pl.program_id(0)
    tokens = rows_ref.shape[0]
    block = table_ref.shape[0]
    shards, _, width = table_grad_ref.shape
    lane = lax.broadcasted_iota(jnp.int32, (ROW_BLOCK, block), 1)

    @pl.when(step == 0)
    def _():
        total[...] = jnp.zeros_like(total)

    for start in range(0, tokens, ROW_BLOCK):
        part = slice(start, start + ROW_BLOCK)
        grads = jnp.exp(logit_ref[part, :] - scale_ref[part, 0:1]) * scale_ref[part, 1:2]
        hit = lane == goal_ref[part, :] - step * block
        grads = jnp.where(hit, grads - 1.0, grads) * scale_ref[part, 2:3]
        grads = grads.astype(LOW)
        grads_ref[part, :] = grads
        total[part, :] += dot_nn(grads, table_ref[...])
    turned = grads_ref[...].T
    for shard in range(shards):
        cols = slice(shard * width, (shard + 1) * width)
        table_grad_ref[shard] = dot_nn(turned, rows_ref[:, cols]).astype(LOW)

    @pl.when(step == pl.num_programs(0) - 1)
    def _():
        out_ref[...] = total[...].astype(LOW)


def run_head_back(rows, table, goal_local, scales, logits, shards):
    tokens = rows.shape[0]
    padded = table.shape[0]
    return pl.pallas_call(
        head_back_kernel,
        grid=(padded // BACK_BLOCK,),
        in_specs=[
            pl.BlockSpec((tokens, D), lambda j: (0, 0)),
            pl.BlockSpec((BACK_BLOCK, D), lambda j: (j, 0)),
            pl.BlockSpec((tokens, 1), lambda j: (0, 0)),
            pl.BlockSpec((tokens, 4), lambda j: (0, 0)),
            pl.BlockSpec((tokens, BACK_BLOCK), lambda j: (0, j)),
        ],
        out_specs=[
            pl.BlockSpec((tokens, D), lambda j: (0, 0)),
            pl.BlockSpec((shards, BACK_BLOCK, D // shards), lambda j: (0, j, 0)),
        ],
        out_shape=[
            jax.ShapeDtypeStruct((tokens, D), LOW),
            jax.ShapeDtypeStruct((shards, padded, D // shards), LOW),
        ],
        scratch_shapes=[
            pltpu.VMEM((tokens, D), FULL),
            pltpu.VMEM((tokens, BACK_BLOCK), LOW),
        ],
        compiler_params=params_of(),
        name="head_back",
    )(rows, table, goal_local, scales, logits)


def table_step_kernel(
    factor_ref, weight_ref, moment_ref, square_ref, first_ref, second_ref, *out_refs
):
    factor = factor_ref[0]

    def step(grads, rate):
        results = adam_update(
            weight_ref[0], moment_ref[0], square_ref[0], grads * factor, rate, DECAYS[0]
        )
        for ref, value in zip(out_refs, results):
            ref[0] = value

    @pl.when(pl.program_id(0) == 0)
    def _():
        step(first_ref[...], TABLE_RATES[0])

    @pl.when(pl.program_id(0) == 1)
    def _():
        step(second_ref[...].astype(FULL), TABLE_RATES[1])


def table_step(factor, weight, moment, square, first, second):
    vocab, width = weight.shape[1:]
    rows = min(STEP_BLOCK, vocab)
    steps = pl.cdiv(vocab, rows)
    block = pl.BlockSpec((1, rows, width), lambda t, j, factor_ref: (t, j, 0))
    return pl.pallas_call(
        table_step_kernel,
        grid_spec=pltpu.PrefetchScalarGridSpec(
            num_scalar_prefetch=1,
            grid=(2, steps),
            in_specs=[
                block,
                block,
                block,
                pl.BlockSpec(
                    (rows, width),
                    lambda t, j, factor_ref: (jnp.where(t == 0, j, steps - 1), 0),
                ),
                pl.BlockSpec(
                    (rows, width), lambda t, j, factor_ref: (jnp.where(t == 1, j, 0), 0)
                ),
            ],
            out_specs=[block] * 3,
        ),
        out_shape=[jax.ShapeDtypeStruct(weight.shape, FULL)] * 3,
        compiler_params=params_of(2),
        name="table_step",
    )(factor, weight, moment, square, first, second)


def expert_step_kernel(factor_ref, core_ref, mine_ref, other_ref, *refs):
    factor = factor_ref[0]
    inner, outer = refs[:3], refs[3:6]
    inner_out, outer_out = refs[6:9], refs[9:]
    split = inner[0].shape[1]
    rows = mine_ref.shape[0] // 2
    half = pl.num_programs(0) // 2

    def step(grads):
        for index, part, ins, outs, rate in [
            item
            for index in range(2)
            for item in (
                (index, slice(index * rows, index * rows + split), inner, inner_out, 6),
                (index, slice(index * rows + split, (index + 1) * rows), outer, outer_out, 7),
            )
        ]:
            results = adam_update(
                ins[0][index],
                ins[1][index],
                ins[2][index],
                grads[part, :].astype(FULL) * factor,
                RATES[rate + 1],
                DECAYS[rate + 1],
            )
            for ref, value in zip(outs, results):
                ref[index] = value

    is_mine = pl.program_id(0) // half == core_ref[0]

    @pl.when(is_mine)
    def _():
        step(mine_ref)

    @pl.when(jnp.logical_not(is_mine))
    def _():
        step(other_ref)


def expert_step(factor, core, mine, other, inner, outer):
    experts, _, width = inner[0].shape
    half = experts // 4
    rows = inner[0].shape[1] + outer[0].shape[1]
    spec = lambda item: pl.BlockSpec((2,) + item.shape[1:], lambda e, f_ref, c_ref: (e, 0, 0))
    held = lambda turn: pl.BlockSpec(
        (2 * rows, width),
        lambda e, f_ref, c_ref: (
            jnp.clip(e - jnp.bitwise_xor(c_ref[0], turn) * half, 0, half - 1),
            0,
        ),
    )
    return pl.pallas_call(
        expert_step_kernel,
        grid_spec=pltpu.PrefetchScalarGridSpec(
            num_scalar_prefetch=2,
            grid=(experts // 2,),
            in_specs=[held(0), held(1)] + [spec(item) for item in inner + outer],
            out_specs=[spec(item) for item in inner + outer],
        ),
        out_shape=[jax.ShapeDtypeStruct(item.shape, FULL) for item in inner + outer],
        compiler_params=params_of(),
        name="expert_step",
    )(factor, core, mine, other, *inner, *outer)


def rows_of_attention(item):
    return item.transpose(1, 2, 0).reshape(-1, item.shape[0])


def rows_of_shared(shared_in, shared_out, padded):
    width = shared_out.shape[1]
    shared = jnp.concatenate([shared_in.transpose(1, 2, 0), shared_out[None]])
    shared = shared.reshape(3, 2, -1, width).transpose(1, 0, 2, 3)
    shared = jnp.pad(shared, ((0, 0), (0, 0), (0, padded - shared.shape[2]), (0, 0)))
    return shared.reshape(2, -1, width)


def shards(
    token_ids,
    target_ids,
    counted,
    routes,
    vocab_tables,
    norm_gains,
    attn_in,
    attention_output_weight,
    router,
    shared_in,
    shared_out,
    expert_in,
    expert_out,
    vocab_tables_moment,
    norm_gains_moment,
    attn_in_moment,
    attn_out_moment,
    router_moment,
    shared_in_moment,
    shared_out_moment,
    expert_in_moment,
    expert_out_moment,
    vocab_tables_square,
    norm_gains_square,
    attn_in_square,
    attn_out_square,
    router_square,
    shared_in_square,
    shared_out_square,
    expert_in_square,
    expert_out_square,
):
    seq_rows, seqs = token_ids.shape
    tokens = seq_rows * seqs
    model_size = lax.axis_size("mp")
    model_place = lax.axis_index("mp")
    data_size = lax.axis_size("dp")
    data_place = lax.axis_index("dp")
    width = vocab_tables.shape[1]
    vocab = vocab_tables.shape[2]
    experts = expert_in.shape[0]
    expert_total = experts * model_size
    capacity = min(2 * tokens * TOPK // expert_total, tokens)
    hidden_width = expert_out.shape[2]
    head_width = attention_output_weight.shape[0]
    shared_width = shared_out.shape[0]
    own = tokens // model_size
    gate_lanes = round_up(expert_total, LANES)
    place = data_place.reshape(1).astype(jnp.int32)

    counts = counted.T.reshape(tokens).astype(FULL)
    small = jnp.concatenate(
        [
            token_ids.T.reshape(tokens).astype(FULL),
            lax.optimization_barrier(norm_gains.astype(LOW)).astype(FULL).reshape(-1),
            jnp.sum(counts).reshape(1),
        ]
    )
    small = jnp.pad(small, (0, round_up(small.shape[0], 1024) - small.shape[0]))
    small = lax.all_gather(small, "dp", axis=0, tiled=False)
    shared_half = shared_width // 2
    shared_pad = round_up(shared_half, 16)
    core = core_place()
    core_item = core.reshape(1).astype(jnp.int32)
    shared_rows = rows_of_shared(shared_in, shared_out, shared_pad)
    expert_other = split_experts(1 - core_item, expert_in, expert_out, shared_rows)
    expert_mine = split_experts(core_item, expert_in, expert_out, shared_rows)
    ids = small[:, :tokens].astype(jnp.int32)
    gains = small[:, tokens : tokens + 3 * width].reshape(data_size, 3, width)
    gains = gains.transpose(1, 0, 2).reshape(3, D)
    token_count = jnp.sum(small[:, tokens + 3 * width])

    marks = jnp.concatenate(
        [
            routes.transpose(2, 1, 0).reshape(TOPK, tokens),
            target_ids.T.reshape(1, tokens),
            counted.T.reshape(1, tokens),
        ]
    )
    marks = jnp.stack([marks, swap(marks, 1)], axis=1)

    small_pieces = gather_blocks(
        jnp.concatenate([rows_of_attention(attn_in), attention_output_weight, router.T]).astype(
            LOW
        ),
        False,
    )
    expert_all = gather_half(core_item, expert_mine, expert_other)
    tables = vocab_tables.transpose(0, 2, 1)
    padded = round_up(vocab, 2 * VOCAB_BLOCK)
    table_low = jnp.pad(tables[1].astype(LOW), ((0, padded - vocab), (0, 0)))
    table_low = table_low.reshape(2, padded // 2, width)
    table_half = lambda place: lax.dynamic_index_in_dim(table_low, place, 0, keepdims=False)
    table_all = gather_half(core_item, table_half(core), table_half(1 - core))
    local_ids = ids.reshape(data_size, model_size, own).transpose(1, 0, 2).reshape(-1)
    local_ids = local_ids - model_place * vocab
    inside = (local_ids >= 0) & (local_ids < vocab)
    looked_up = lookup(jnp.clip(local_ids, 0, vocab - 1), tables)
    looked_up = jnp.where(inside[:, None], looked_up, 0.0).astype(LOW)
    embedded = sum_rows(looked_up, ring=True).astype(LOW).reshape(data_size, own, width)
    state_zero = lax.all_to_all(embedded, "dp", 0, 0, tiled=True)
    state_zero, *small_pieces = lax.optimization_barrier((state_zero, *small_pieces))
    small_all = jnp.concatenate(by_place(small_pieces), axis=1)
    attn_width = 4 * head_width
    weight_qkv = small_all[: 3 * head_width]
    weight_out = small_all[3 * head_width : attn_width]
    weight_router = small_all[attn_width:]
    state_zero = state_zero.transpose(1, 0, 2).reshape(own, D).astype(FULL)

    first_in = gather_rows(normed(state_zero, gains[0]).astype(LOW))
    projected = dot_nt(first_in, weight_qkv).astype(LOW)
    projected, weight_out = lax.optimization_barrier((projected, weight_out))
    weight_out_all = jnp.concatenate(
        [weight_out] + [shift(weight_out, step) for step in range(1, model_size)]
    )
    key_blocks = gather_blocks(projected[:, head_width:], True)
    attended, log_total = attend(place, projected, key_blocks, seqs)
    attended_pieces = attended.reshape(model_size, own, head_width)
    piece_of = lambda step: lax.dynamic_index_in_dim(
        attended_pieces, (model_place + step) % model_size, 0, keepdims=False
    )
    attended_own = [piece_of(0)] + [shift(piece_of(step), step) for step in range(1, model_size)]
    state_one = state_zero + dot_nn(jnp.concatenate(attended_own, axis=1), weight_out_all)

    expert_ids = jnp.arange(expert_total, dtype=jnp.int32)
    named = jnp.any(marks[:TOPK, :, None, :] == expert_ids[None, None, :, None], axis=0)
    earlier = jnp.arange(tokens)[:, None] < jnp.arange(tokens)[None, :]
    ranks = dot_nn(named.reshape(-1, tokens).astype(LOW), earlier.astype(LOW)).astype(jnp.int32)
    ranks = jnp.where(named, ranks.reshape(named.shape), -1)
    named_cols = named.transpose(0, 2, 1).reshape(2 * tokens, expert_total)
    rank_cols = ranks.transpose(0, 2, 1).reshape(2 * tokens, expert_total)
    part_experts = experts // 2
    first_expert = model_place * experts + core * part_experts
    local_rows = lambda table: lax.dynamic_slice_in_dim(table, first_expert, part_experts, 0)[
        :, None, :
    ]
    rank_rows = local_rows(ranks.transpose(1, 0, 2).reshape(expert_total, 2 * tokens))
    first_place = first_expert.reshape(1).astype(jnp.int32)
    second_in = gather_rows(normed(state_one, gains[1]).astype(LOW))
    second_other = swap(second_in, 1)
    router_logits = jnp.concatenate(
        [dot_nt(second_in, weight_router), dot_nt(second_other, weight_router)]
    )
    gates = jax.nn.softmax(jnp.where(named_cols, router_logits, FAR), axis=1)
    gates = jnp.where(named_cols, gates, 0.0)
    gate_rows = local_rows(gates.T)
    moe_part, gate_part, up_part, picked = run_experts(
        first_place, rank_rows, rank_cols, gates, second_in, second_other, expert_all, capacity,
        hidden_width, shared_pad,
    )
    state_two = state_one + sum_rows(sum_pair(moe_part))

    third_in = pair_rows(gather_rows(normed(state_two, gains[2]).astype(LOW)))
    half_vocab = padded // 2
    goal_local = marks[TOPK].reshape(2 * tokens, 1) - model_place * vocab
    goal_local = jnp.where(goal_local < vocab, goal_local - core * half_vocab, -1)
    valid = (vocab - core * half_vocab).reshape(1).astype(jnp.int32)
    logits, stats = run_head(third_in, table_all, goal_local, valid)
    stats = stats[:, :3].T
    stats = join_stats([stats, jnp.roll(swap(stats, 1), tokens, axis=1)])
    stats = join_stats(
        [stats]
        + [
            lax.ppermute(stats, "mp", [(i, i ^ mask) for i in range(model_size)])
            for mask in range(1, model_size)
        ]
    )
    log_head = stats[0] + jnp.log(stats[1])
    goal_logit = stats[2]
    pair_counts = marks[TOPK + 1].reshape(2 * tokens).astype(FULL)
    loss_rows = pair_counts * (log_head - goal_logit + Z_COEF * log_head * log_head)
    loss_part = jnp.sum(loss_rows[:tokens])
    scales = jnp.stack(
        [log_head, 1.0 + 2.0 * Z_COEF * log_head, pair_counts / token_count, pair_counts], axis=1
    )
    third_part, table_part = run_head_back(
        third_in, table_all, goal_local, scales, logits, data_size // 2
    )
    table_second = scatter_half(table_part)
    state_two_grad, gain_three = norm_back(state_two, gains[2], sum_rows(sum_pair(third_part)))

    two_low = gather_rows(state_two_grad.astype(LOW))
    second_part, expert_part = run_experts_back(
        first_place, rank_rows, rank_cols, gate_rows, second_in, second_other, two_low,
        swap(two_low, 1), expert_all, gate_part, up_part, picked, capacity, hidden_width, shared_pad,
        data_size // 2, gate_lanes,
    )
    expert_grad = scatter_half(expert_part)
    second_sum = sum_rows(sum_pair(second_part))
    second_grad = second_sum[:, :D]
    gate_grad = second_sum[:, D : D + expert_total]
    own_gates = lax.dynamic_slice_in_dim(gates, model_place * own, own, 0)
    choice_grad = own_gates * (
        gate_grad - jnp.sum(own_gates * gate_grad, axis=1, keepdims=True)
    )
    choice_grad = choice_grad.astype(LOW)
    second_grad = second_grad + dot_nn(choice_grad, weight_router)
    norm_grad, gain_two = norm_back(state_one, gains[1], second_grad)
    state_one_grad = state_two_grad + norm_grad

    own_low = state_one_grad.astype(LOW)
    out_grads = dot_nt(own_low, weight_out_all).astype(LOW)
    out_grad = jnp.zeros((tokens, head_width), LOW)
    for step in range(model_size):
        piece = out_grads[:, step * head_width : (step + 1) * head_width]
        if step > 0:
            piece = shift(piece, model_size - step)
        out_grad = lax.dynamic_update_slice(
            out_grad, piece, ((model_place + step) % model_size * own, 0)
        )
    own_low, out_grad = lax.optimization_barrier((own_low, out_grad))
    attn_out_grad = dot_tn(attended, gather_rows(own_low))
    query_grad, even_grads, odd_grads = attend_back(
        place, projected, log_total, out_grad, key_blocks, seqs, table_second
    )
    key_pairs = even_grads.astype(FULL) + swap(odd_grads, 1).astype(FULL)
    key_grad = scatter_pairs(key_pairs, True).astype(LOW)
    projected_grad = jnp.concatenate([query_grad, key_grad], axis=1)
    first_part = dot_nn(projected_grad, weight_qkv).astype(LOW)
    attn_in_grad = dot_tn(projected_grad, first_in)
    attn_pairs = pair_sums(jnp.concatenate([attn_in_grad, attn_out_grad]))
    norm_grad, gain_one = norm_back(state_zero, gains[0], sum_rows(first_part))
    state_zero_grad = state_one_grad + norm_grad

    tokens_part = data_size * own
    second_own = lax.dynamic_slice_in_dim(second_in, model_place * own, own, 0)
    gain_part = jnp.concatenate(
        [dot_tn(choice_grad, second_own), jnp.stack([gain_one, gain_two, gain_three])]
    ).astype(LOW)
    gain_rows = gain_part.shape[0]
    gain_pad = round_up(gain_rows, 16)
    gain_part = jnp.pad(gain_part, ((0, gain_pad - gain_rows), (0, 0)))
    back_rows = jnp.concatenate([state_zero_grad.astype(LOW), gain_part])
    back_rows = back_rows.reshape(own + gain_pad, data_size, width).transpose(1, 0, 2)
    attn_pairs, back_rows = lax.optimization_barrier((attn_pairs, back_rows))
    back_rows = lax.all_to_all(back_rows, "dp", 0, 0, tiled=True)
    attn_pairs, back_rows = lax.optimization_barrier((attn_pairs, back_rows))
    attn_sums = scatter_pairs(attn_pairs, False)
    back_parts = [back_rows] + [
        lax.ppermute(back_rows, "mp", [(i, i ^ mask) for i in range(model_size)])
        for mask in range(1, model_size)
    ]
    id_parts = [
        lax.dynamic_slice_in_dim(
            local_ids, jnp.bitwise_xor(model_place, mask) * tokens_part, tokens_part, 0
        )
        for mask in range(model_size)
    ]
    table_mine, table_other, second_square = part_features(core_item, table_second)
    table_other = swap(table_other, 1)
    second_square, back_parts[0] = lax.optimization_barrier((second_square, back_parts[0]))
    gain_sums = jnp.sum(
        sum(part[:, own : own + gain_rows].astype(FULL) for part in back_parts), axis=0
    )
    router_sums, gain_grad = gain_sums[:expert_total], gain_sums[expert_total:]
    table_first = []
    for part in (slice(0, 1), slice(1, model_size)):
        *table_first, first_square = table_grad(
            jnp.concatenate(id_parts[part]),
            jnp.concatenate([rows[:, :own].reshape(-1, width) for rows in back_parts[part]]),
            vocab,
            *table_first,
        )
    (table_first,) = table_first

    expert_grad_mine, expert_grad_other, expert_square = part_features(core_item, expert_grad)
    expert_grads = (expert_grad_mine, swap(expert_grad_other, 1))
    square = lambda item: jnp.sum(jnp.square(item))
    local_square = (
        second_square
        + expert_square
        + jnp.sum(first_square)
        + square(attn_sums)
        + square(gain_sums) / model_size
    )
    table_second = in_order(table_mine, table_other, 0)[:vocab]
    shared_sums = in_order(
        *[
            item[3 * part_experts * hidden_width :].reshape(3, shared_pad, width)[:, :shared_half]
            for item in expert_grads
        ],
        1,
    ).astype(FULL)
    sums = jnp.stack([local_square, loss_part / model_size])
    sums = add_all(jnp.broadcast_to(sums[:, None], (2, LANES)))[:, 0]
    grad_norm = jnp.sqrt(sums[0])
    factor = CLIP / jnp.maximum(grad_norm, CLIP)

    table_results = table_step(
        factor.reshape(1),
        tables,
        vocab_tables_moment.transpose(0, 2, 1),
        vocab_tables_square.transpose(0, 2, 1),
        table_first,
        table_second,
    )
    results = [sums[1], token_count, grad_norm]
    results.extend(item.transpose(0, 2, 1) for item in table_results)
    gradients = (
        gain_grad,
        attn_sums[: 3 * head_width].reshape(3, head_width, width).transpose(2, 0, 1),
        attn_sums[3 * head_width :],
        router_sums.T,
        shared_sums[:2].transpose(2, 0, 1),
        shared_sums[2],
    )
    params = (
        norm_gains, attn_in, attention_output_weight, router, shared_in, shared_out,
    )
    moments = (
        norm_gains_moment, attn_in_moment, attn_out_moment, router_moment, shared_in_moment,
        shared_out_moment,
    )
    squares = (
        norm_gains_square, attn_in_square, attn_out_square, router_square, shared_in_square,
        shared_out_square,
    )
    for index in range(6):
        results.extend(
            adam_update(
                params[index],
                moments[index],
                squares[index],
                gradients[index] * factor,
                RATES[index + 1],
                DECAYS[index + 1],
            )
        )
    expert_results = expert_step(
        factor.reshape(1),
        core_item,
        *expert_grads,
        [
            item.transpose(0, 2, 3, 1).reshape(experts, 2 * hidden_width, width)
            for item in (expert_in, expert_in_moment, expert_in_square)
        ],
        [
            item.transpose(0, 2, 1)
            for item in (expert_out, expert_out_moment, expert_out_square)
        ],
    )
    results.extend(
        item.reshape(experts, 2, hidden_width, width).transpose(0, 3, 1, 2)
        for item in expert_results[:3]
    )
    results.extend(item.transpose(0, 2, 1) for item in expert_results[3:])
    return tuple(results)


def solution(mesh):
    in_specs = (
        P("dp", None),
        P("dp", None),
        P("dp", None),
        P("dp", None, None),
        P(None, "dp", "mp"),
        P(None, "dp"),
        P("dp", None, "mp"),
        P("mp", "dp"),
        P("dp", None),
        P("dp", None, "mp"),
        P("mp", "dp"),
        P("mp", "dp", None, None),
        P("mp", "dp", None),
        P(None, "dp", "mp"),
        P(None, "dp"),
        P("dp", None, "mp"),
        P("mp", "dp"),
        P("dp", None),
        P("dp", None, "mp"),
        P("mp", "dp"),
        P("mp", "dp", None, None),
        P("mp", "dp", None),
        P(None, "dp", "mp"),
        P(None, "dp"),
        P("dp", None, "mp"),
        P("mp", "dp"),
        P("dp", None),
        P("dp", None, "mp"),
        P("mp", "dp"),
        P("mp", "dp", None, None),
        P("mp", "dp", None),
    )
    out_specs = (
        P(),
        P(),
        P(),
        P(None, "dp", "mp"),
        P(None, "dp", "mp"),
        P(None, "dp", "mp"),
        P(None, "dp"),
        P(None, "dp"),
        P(None, "dp"),
        P("dp", None, "mp"),
        P("dp", None, "mp"),
        P("dp", None, "mp"),
        P("mp", "dp"),
        P("mp", "dp"),
        P("mp", "dp"),
        P("dp", None),
        P("dp", None),
        P("dp", None),
        P("dp", None, "mp"),
        P("dp", None, "mp"),
        P("dp", None, "mp"),
        P("mp", "dp"),
        P("mp", "dp"),
        P("mp", "dp"),
        P("mp", "dp", None, None),
        P("mp", "dp", None, None),
        P("mp", "dp", None, None),
        P("mp", "dp", None),
        P("mp", "dp", None),
        P("mp", "dp", None),
    )
    return jax.shard_map(shards, mesh=mesh, in_specs=in_specs, out_specs=out_specs, check_vma=False)
```

```python
import functools

import jax
import jax.numpy as jnp
from jax import lax
from jax.experimental import pallas as pl
from jax.experimental.pallas import tpu as pltpu
from jax.sharding import PartitionSpec as P

D = 1024
HD = 128
TOPK = 6
STEP = 10
LANES = 128
VOCAB_BLOCK = 1024
STEP_BLOCK = 4008
BACK_BLOCK = 512
PAIR_BLOCK = 2304
ROW_BLOCK = 256

NORM_EPS = 1e-06
Z_COEF = 0.01
CLIP = 0.01
BETA_ONE = 0.9
BETA_TWO = 0.95
ADAM_EPS = 1e-08
TABLE_RATES = (1.0, 0.06)
RATES = (0.0, 1.0, 0.02, 0.05, 0.01, 0.02, 0.02, 0.02, 0.02)
DECAYS = (0.1, 0.0, 0.1, 0.1, 0.1, 0.1, 0.1, 0.1, 0.1)
FAR = -1e30
LOW = jnp.bfloat16
FULL = jnp.float32


def dot_nn(left, right):
    return lax.dot_general(left, right, (((1,), (0,)), ((), ())), preferred_element_type=FULL)


def dot_nt(left, right):
    return lax.dot_general(left, right, (((1,), (1,)), ((), ())), preferred_element_type=FULL)


def dot_tn(left, right):
    return lax.dot_general(left, right, (((0,), (0,)), ((), ())), preferred_element_type=FULL)


def params_of(dims=1, mib=50):
    return pltpu.CompilerParams(
        dimension_semantics=("arbitrary",) * dims, vmem_limit_bytes=mib * 1024 * 1024
    )


def round_up(number, unit):
    return (number + unit - 1) // unit * unit


def normed(values, gain_row):
    return (
        values * lax.rsqrt(jnp.mean(values * values, axis=-1, keepdims=True) + NORM_EPS) * gain_row
    )


def norm_back(values, gain_row, upstream):
    inv_rms = lax.rsqrt(jnp.mean(values * values, axis=-1, keepdims=True) + NORM_EPS)
    unit_rows = values * inv_rms
    scaled = upstream * gain_row
    gain_grad = jnp.sum(upstream * unit_rows, axis=0)
    return (
        inv_rms * (scaled - unit_rows * jnp.mean(scaled * unit_rows, axis=-1, keepdims=True)),
        gain_grad,
    )


def swiglu_grads(gate_part, up_part, upstream):
    sigmoid_gate = jax.nn.sigmoid(gate_part)
    silu_gate = gate_part * sigmoid_gate
    gate_grad = upstream * up_part * sigmoid_gate * (1.0 + gate_part * (1.0 - sigmoid_gate))
    return gate_grad, upstream * silu_gate


def adam_update(weight, moment, square, grad_item, rate, decay):
    new_moment = BETA_ONE * moment + (1.0 - BETA_ONE) * grad_item
    new_square = BETA_TWO * square + (1.0 - BETA_TWO) * grad_item * grad_item
    scaled = new_square * (1.0 / (1.0 - BETA_TWO**STEP))
    step_ratio = (new_moment * (1.0 / (1.0 - BETA_ONE**STEP))) / (
        scaled * lax.rsqrt(scaled) + ADAM_EPS
    )
    return (weight - rate * (step_ratio + decay * weight), new_moment, new_square)


def sum_rows(partial, ring=False):
    size = lax.axis_size("mp")
    place = lax.axis_index("mp")
    pieces = partial.reshape((size, partial.shape[0] // size) + partial.shape[1:])
    total = lax.dynamic_index_in_dim(pieces, place, 0, keepdims=False).astype(FULL)
    for step in range(1, size):
        other = (lambda i: (i + step) % size) if ring else (lambda i: i ^ step)
        target = (place + step) % size if ring else jnp.bitwise_xor(place, step)
        sent = lax.dynamic_index_in_dim(pieces, target, 0, keepdims=False)
        got = lax.ppermute(sent, "mp", [(i, other(i)) for i in range(size)])
        total = total + got.astype(FULL)
    return total


def gather_rows(rows):
    size = lax.axis_size("mp")
    place = lax.axis_index("mp")
    count = rows.shape[0]
    whole = jnp.zeros((size * count,) + rows.shape[1:], rows.dtype)
    rest = (0,) * (rows.ndim - 1)
    whole = lax.dynamic_update_slice(whole, rows, (place * count,) + rest)
    for step in range(1, size):
        got = lax.ppermute(rows, "mp", [(i, (i + step) % size) for i in range(size)])
        whole = lax.dynamic_update_slice(whole, got, ((place - step) % size * count,) + rest)
    return whole


def swap(item, mask):
    size = lax.axis_size("dp")
    return lax.ppermute(item, "dp", [(i, i ^ mask) for i in range(size)])


def chips_of(size):
    return [list(range(core, size, 2)) for core in range(2)]


def core_place():
    return lax.axis_index("dp") % 2


def pair_rows(rows):
    return jnp.concatenate([rows, swap(rows, 1)])


def sum_pair(partial):
    count = partial.shape[0] // 2
    return (partial[:count].astype(FULL) + swap(partial[count:], 1).astype(FULL)).astype(LOW)


def in_order(mine, other, axis):
    first = core_place() == 0
    return jnp.concatenate(
        [jnp.where(first, mine, other), jnp.where(first, other, mine)], axis=axis
    )


def gather_half(core, mine, other):
    size = lax.axis_size("dp")
    return lax.all_gather(
        pair_features(core, mine, swap(other, 1)),
        "dp",
        axis=1,
        tiled=True,
        axis_index_groups=chips_of(size),
    )


def scatter_half(grads):
    size = lax.axis_size("dp")
    part = lax.psum_scatter(
        grads, "dp", scatter_dimension=0, tiled=False, axis_index_groups=chips_of(size)
    )
    return lax.optimization_barrier(part)


def gather_half(core, mine, other):
    size = lax.axis_size("dp")
    return lax.all_gather(
        pair_features(core, mine, swap(other, 1)),
        "dp",
        axis=1,
        tiled=True,
        axis_index_groups=chips_of(size),
    )


def scatter_half(grads):
    size = lax.axis_size("dp")
    part = lax.psum_scatter(
        grads, "dp", scatter_dimension=0, tiled=False, axis_index_groups=chips_of(size)
    )
    return lax.optimization_barrier(part)


def halves_back(part):
    width = part.shape[1] // 2
    place = core_place()
    mine = lax.dynamic_slice_in_dim(part, place * width, width, 1)
    return mine, swap(lax.dynamic_slice_in_dim(part, (1 - place) * width, width, 1), 1)


def by_place(pieces):
    place = lax.axis_index("dp")
    stacked = jnp.stack(pieces)
    return [
        lax.dynamic_index_in_dim(stacked, jnp.bitwise_xor(place, index), 0, keepdims=False)
        for index in range(len(pieces))
    ]


def pair_sums(grads):
    size = lax.axis_size("dp")
    place = lax.axis_index("dp")
    width = grads.shape[1] // size
    pieces = grads.astype(LOW).reshape(-1, size, width).transpose(1, 0, 2)
    picked = lambda core: jnp.stack(
        [
            lax.dynamic_index_in_dim(pieces, jnp.bitwise_xor(place, mask), 0, keepdims=False)
            for mask in range(core, size, 2)
        ]
    )
    return (picked(0).astype(FULL) + swap(picked(1), 1).astype(FULL)).astype(LOW)


def scatter_pairs(pairs, causal):
    total = pairs[0].astype(FULL)
    for index in range(1, pairs.shape[0]):
        mask = 2 * index
        keep = lambda i: not causal or i ^ mask < i
        total = total + send_blocks(pairs[index].astype(LOW), mask, keep).astype(FULL)
    return total


def tree_sum(items):
    while len(items) > 1:
        items = [items[index] + items[index + 1] for index in range(0, len(items), 2)]
    return items[0]


def add_all(item):
    item = item + swap(item, 1)
    item = tree_sum([item] + [swap(item, mask) for mask in range(2, lax.axis_size("dp"), 2)])
    size = lax.axis_size("mp")
    return tree_sum(
        [item]
        + [
            lax.ppermute(item, "mp", [(i, i ^ mask) for i in range(size)])
            for mask in range(1, size)
        ]
    )


def send_blocks(item, mask, keep):
    size = lax.axis_size("dp")
    return lax.ppermute(item, "dp", [(i, i ^ mask) for i in range(size) if keep(i)])


def gather_blocks(item, causal):
    both = []
    for mask in range(0, lax.axis_size("dp"), 2):
        block, keep = item, lambda i: not causal or i % 2 == 0
        if mask > 0:
            block = send_blocks(item, mask, lambda i: not causal or i ^ mask > i)
            keep = lambda i: not causal or i ^ mask < i
        both.extend([block, send_blocks(block, 1, keep)])
    return both


def shift(item, step):
    size = lax.axis_size("mp")
    return lax.ppermute(item, "mp", [(i, (i + step) % size) for i in range(size)])


def join_stats(parts):
    parts = jnp.stack(parts)
    top = jnp.max(parts[:, 0], axis=0)
    total = jnp.sum(parts[:, 1] * jnp.exp(parts[:, 0] - top), axis=0)
    return jnp.stack([top, total, jnp.sum(parts[:, 2], axis=0)])


def split_kernel(core_ref, inner_ref, outer_ref, shared_ref, out_ref):
    step = pl.program_id(0)
    steps = pl.num_programs(0)
    split = inner_ref.shape[1]

    @pl.when(step < steps - 1)
    def _():
        out_ref[:split, :] = inner_ref[0].astype(LOW)
        out_ref[split:, :] = outer_ref[0].astype(LOW)

    @pl.when(step == steps - 1)
    def _():
        out_ref[: shared_ref.shape[1], :] = shared_ref[0].astype(LOW)


def split_experts(core, expert_in, expert_out, shared):
    experts, width, _, hidden_width = expert_in.shape
    half = experts // 2
    rows = 3 * hidden_width

    def expert_of(step, core_ref):
        return (core_ref[0] * half + jnp.minimum(step, half - 1), 0, 0)

    return pl.pallas_call(
        split_kernel,
        grid_spec=pltpu.PrefetchScalarGridSpec(
            num_scalar_prefetch=1,
            grid=(half + 1,),
            in_specs=[
                pl.BlockSpec((1, 2 * hidden_width, width), expert_of),
                pl.BlockSpec((1, hidden_width, width), expert_of),
                pl.BlockSpec((1,) + shared.shape[1:], lambda j, core_ref: (core_ref[0], 0, 0)),
            ],
            out_specs=pl.BlockSpec((rows, width), lambda j, core_ref: (j, 0)),
        ),
        out_shape=jax.ShapeDtypeStruct((half * rows + shared.shape[1], width), LOW),
        compiler_params=params_of(),
        name="split_experts",
    )(
        core,
        expert_in.transpose(0, 2, 3, 1).reshape(experts, 2 * hidden_width, width),
        expert_out.transpose(0, 2, 1),
        shared,
    )


def pair_kernel(core_ref, mine_ref, other_ref, out_ref):
    width = mine_ref.shape[1]

    @pl.when(core_ref[0] == 0)
    def _():
        out_ref[:, :width] = mine_ref[...]
        out_ref[:, width:] = other_ref[...]

    @pl.when(core_ref[0] != 0)
    def _():
        out_ref[:, :width] = other_ref[...]
        out_ref[:, width:] = mine_ref[...]


def part_kernel(rows, core_ref, part_ref, mine_ref, other_ref, square_ref):
    step = pl.program_id(0)
    width = mine_ref.shape[1]

    @pl.when(step == 0)
    def _():
        square_ref[...] = jnp.zeros_like(square_ref)

    values = part_ref[...]
    for core in range(2):

        @pl.when(core_ref[0] == core)
        def _():
            mine_ref[...] = values[:, core * width : (core + 1) * width]
            other_ref[...] = values[:, (1 - core) * width : (2 - core) * width]

    values = values.astype(FULL)
    place = step * values.shape[0] + lax.broadcasted_iota(jnp.int32, values.shape, 0)
    values = jnp.where(place < rows, values * values, 0.0)
    square_ref[...] += jnp.sum(values.reshape(-1, 8, values.shape[1]), axis=0)


def part_features(core, part):
    rows, width = part.shape
    spec = pl.BlockSpec((PAIR_BLOCK, width // 2), lambda j, core_ref: (j, 0))
    mine, other, squares = pl.pallas_call(
        functools.partial(part_kernel, rows),
        grid_spec=pltpu.PrefetchScalarGridSpec(
            num_scalar_prefetch=1,
            grid=(pl.cdiv(rows, PAIR_BLOCK),),
            in_specs=[pl.BlockSpec((PAIR_BLOCK, width), lambda j, core_ref: (j, 0))],
            out_specs=[spec, spec, pl.BlockSpec((8, width), lambda j, core_ref: (0, 0))],
        ),
        out_shape=[jax.ShapeDtypeStruct((rows, width // 2), LOW)] * 2
        + [jax.ShapeDtypeStruct((8, width), FULL)],
        compiler_params=params_of(),
        name="part_features",
    )(core, part)
    return mine, other, jnp.sum(squares)


def pair_features(core, mine, other):
    rows, width = mine.shape
    spec = pl.BlockSpec((PAIR_BLOCK, width), lambda j, core_ref: (j, 0))
    return pl.pallas_call(
        pair_kernel,
        grid_spec=pltpu.PrefetchScalarGridSpec(
            num_scalar_prefetch=1,
            grid=(pl.cdiv(rows, PAIR_BLOCK),),
            in_specs=[spec, spec],
            out_specs=pl.BlockSpec((PAIR_BLOCK, 2 * width), lambda j, core_ref: (j, 0)),
        ),
        out_shape=jax.ShapeDtypeStruct((rows, 2 * width), LOW),
        compiler_params=params_of(),
        name="pair_features",
    )(core, mine, other)


def lookup_kernel(ids_ref, table_ref, out_ref):
    base = pl.program_id(0) * out_ref.shape[0]

    def copy_rows(step, carry):
        for inner in range(8):
            row = step * 8 + inner
            out_ref[pl.ds(row, 1), :] = table_ref[0, pl.ds(ids_ref[base + row], 1), :]
        return carry

    lax.fori_loop(0, out_ref.shape[0] // 8, copy_rows, 0)


def lookup(ids, tables):
    count = ids.shape[0]
    vocab, width = tables.shape[1:]
    block = 512
    return pl.pallas_call(
        lookup_kernel,
        grid_spec=pltpu.PrefetchScalarGridSpec(
            num_scalar_prefetch=1,
            grid=(count // block,),
            in_specs=[pl.BlockSpec((1, vocab, width), lambda i, ids_ref: (0, 0, 0))],
            out_specs=pl.BlockSpec((block, width), lambda i, ids_ref: (i, 0)),
        ),
        out_shape=jax.ShapeDtypeStruct((count, width), FULL),
        compiler_params=params_of(),
        name="lookup",
    )(ids, tables)


def table_grad_kernel(ids_ref, side_ref, rows_ref, *refs):
    *before_refs, out_ref, square_ref, spread = refs
    _, block, width = out_ref.shape
    span = 512
    step = pl.program_id(0)
    token_of = step * block + lax.broadcasted_iota(jnp.int32, (block, span), 0)

    @pl.when(step == 0)
    def _():
        square_ref[...] = jnp.zeros_like(square_ref)
        rows = rows_ref[...].astype(FULL)
        for half in range(2):
            cols = slice(half * width, (half + 1) * width)
            spread[:, cols] = jnp.where(side_ref[...] == half, rows, 0.0).astype(LOW)

    total = jnp.zeros((block, 2 * width), FULL)
    for start in range(0, rows_ref.shape[0], span):
        hit = (token_of == ids_ref[:, start : start + span]).astype(FULL).astype(LOW)
        total = total + dot_nn(hit, spread[start : start + span, :])

    for half in range(2):
        part = total[:, half * width : (half + 1) * width]
        for before_ref in before_refs:
            part = part + before_ref[half]
        out_ref[half] = part
        square_ref[...] += jnp.sum((part * part).reshape(-1, 8, width), axis=0)


def table_grad(ids, rows, vocab, *before):
    count, width = rows.shape
    half = round_up((vocab + 1) // 2, VOCAB_BLOCK)
    inside = (ids >= 0) & (ids < vocab)
    upper = ids >= half
    sides = jnp.where(inside, upper.astype(jnp.int32), 2)[:, None]
    ids = jnp.where(inside, jnp.where(upper, ids - half, ids), -1)
    block = pl.BlockSpec((2, VOCAB_BLOCK, width), lambda j: (0, j, 0))
    return pl.pallas_call(
        table_grad_kernel,
        grid=(half // VOCAB_BLOCK,),
        in_specs=[
            pl.BlockSpec((1, count), lambda j: (0, 0)),
            pl.BlockSpec((count, 1), lambda j: (0, 0)),
            pl.BlockSpec((count, width), lambda j: (0, 0)),
        ]
        + [block] * len(before),
        out_specs=[block, pl.BlockSpec((8, width), lambda j: (0, 0))],
        out_shape=[
            jax.ShapeDtypeStruct((2, half, width), FULL),
            jax.ShapeDtypeStruct((8, width), FULL),
        ],
        scratch_shapes=[pltpu.VMEM((count, 2 * width), LOW)],
        compiler_params=params_of(),
        cost_estimate=pl.CostEstimate(
            flops=4 * count * vocab * width, bytes_accessed=8 * vocab * width, transcendentals=0
        ),
        name="table_grad",
    )(ids.reshape(1, count), sides, rows, *before)


def masked_scores(place, query, keys, rows, blocks):
    scores = dot_nt(query, keys) * HD ** (-0.5)
    offset = lax.broadcasted_iota(jnp.int32, (1, rows), 1)
    key_pos = jnp.concatenate(
        [jnp.bitwise_xor(place, mask) * rows + offset for mask in range(blocks)], axis=1
    )
    query_pos = place * rows + lax.broadcasted_iota(jnp.int32, (rows, 1), 0)
    return jnp.where(key_pos <= query_pos, scores, FAR)


def head_cols(refs, index):
    return jnp.concatenate([ref[:, index * HD : (index + 1) * HD] for ref in refs], axis=0)


def attend_kernel(blocks, place_ref, query_ref, *refs):
    key_refs = refs[:blocks]
    out_ref, log_ref = refs[blocks:]
    place = place_ref[0]
    rows, width = query_ref.shape
    heads = width // HD
    for head in range(heads):
        cols = slice(head * HD, (head + 1) * HD)
        keys = head_cols(key_refs, head)
        values = head_cols(key_refs, heads + head)
        scores = masked_scores(place, query_ref[:, cols], keys, rows, blocks)
        top = jnp.max(scores, axis=1, keepdims=True)
        powers = jnp.exp(scores - top)
        total = jnp.sum(powers, axis=1, keepdims=True)
        probs = (powers * (1.0 / total)).astype(LOW)
        out_ref[:, cols] = dot_nn(probs, values).astype(LOW)
        log_ref[0, :, head : head + 1] = top + jnp.log(total)


def attend(place, projected, key_blocks, seqs):
    blocks = len(key_blocks)
    tokens = projected.shape[0]
    rows = tokens // seqs
    width = projected.shape[1] // 3
    heads = width // HD
    return pl.pallas_call(
        functools.partial(attend_kernel, blocks),
        grid_spec=pltpu.PrefetchScalarGridSpec(
            num_scalar_prefetch=1,
            grid=(seqs,),
            in_specs=[pl.BlockSpec((rows, width), lambda s, place_ref: (s, 0))]
            + [pl.BlockSpec((rows, 2 * width), lambda s, place_ref: (s, 0))] * blocks,
            out_specs=[
                pl.BlockSpec((rows, width), lambda s, place_ref: (s, 0)),
                pl.BlockSpec((1, rows, heads), lambda s, place_ref: (s, 0, 0)),
            ],
        ),
        out_shape=[
            jax.ShapeDtypeStruct((tokens, width), LOW),
            jax.ShapeDtypeStruct((seqs, rows, heads), FULL),
        ],
        compiler_params=params_of(),
        name="attend",
    )(place, projected, *key_blocks)


def attend_back_kernel(blocks, place_ref, query_ref, log_ref, grad_ref, after_ref, *refs):
    del after_ref
    key_refs = refs[:blocks]
    query_grad_ref = refs[blocks]
    key_grad_refs = refs[blocks + 1 :]
    place = place_ref[0]
    rows, width = query_ref.shape
    heads = width // HD
    for head in range(heads):
        cols = slice(head * HD, (head + 1) * HD)
        keys = head_cols(key_refs, head)
        values = head_cols(key_refs, heads + head)
        query = query_ref[:, cols]
        out_grad = grad_ref[:, cols]
        scores = masked_scores(place, query, keys, rows, blocks)
        probs = jnp.exp(scores - log_ref[0, :, head : head + 1])
        prob_grad = dot_nt(out_grad, values)
        delta = jnp.sum(probs * prob_grad, axis=1, keepdims=True)
        score_grad = (probs * (prob_grad - delta)).astype(LOW)
        query_grad_ref[:, cols] = (dot_nn(score_grad, keys) * HD ** (-0.5)).astype(LOW)
        key_grad = (dot_tn(score_grad, query) * HD ** (-0.5)).astype(LOW)
        value_grad = dot_tn(probs.astype(LOW), out_grad).astype(LOW)
        value_cols = slice((heads + head) * HD, (heads + head + 1) * HD)
        for mask in range(blocks):
            part = slice(mask * rows, (mask + 1) * rows)
            key_grad_refs[mask % 2][mask // 2, :, cols] = key_grad[part]
            key_grad_refs[mask % 2][mask // 2, :, value_cols] = value_grad[part]


def attend_back(place, projected, log_total, out_grad, key_blocks, seqs, after):
    blocks = len(key_blocks)
    tokens = projected.shape[0]
    rows = tokens // seqs
    width = projected.shape[1] // 3
    heads = width // HD
    row_spec = pl.BlockSpec((rows, width), lambda s, place_ref: (s, 0))
    key_spec = pl.BlockSpec((rows, 2 * width), lambda s, place_ref: (s, 0))
    return pl.pallas_call(
        functools.partial(attend_back_kernel, blocks),
        grid_spec=pltpu.PrefetchScalarGridSpec(
            num_scalar_prefetch=1,
            grid=(seqs,),
            in_specs=[
                row_spec,
                pl.BlockSpec((1, rows, heads), lambda s, place_ref: (s, 0, 0)),
                row_spec,
                pl.BlockSpec(memory_space=pl.ANY),
            ]
            + [key_spec] * blocks,
            out_specs=[row_spec]
            + [pl.BlockSpec((blocks // 2, rows, 2 * width), lambda s, place_ref: (0, s, 0))] * 2,
        ),
        out_shape=[jax.ShapeDtypeStruct((tokens, width), LOW)]
        + [jax.ShapeDtypeStruct((blocks // 2, tokens, 2 * width), LOW)] * 2,
        compiler_params=params_of(),
        name="attend_back",
    )(place, projected, log_total, out_grad, after, *key_blocks)


def column_of(table, index):
    lane = lax.broadcasted_iota(jnp.int32, table.shape, 1)
    return jnp.sum(jnp.where(lane == index, table, 0), axis=1, keepdims=True)


def swiglu_low(gate_part, up_part):
    return (gate_part * jax.nn.sigmoid(gate_part) * up_part).astype(LOW)


def expert_kernel(
    capacity,
    experts,
    shared_width,
    first_ref,
    rank_row_ref,
    rank_col_ref,
    gate_ref,
    mine_ref,
    other_ref,
    weight_ref,
    out_ref,
    gate_part_ref,
    up_part_ref,
    picked_ref,
    total,
):
    expert = pl.program_id(0)
    row_refs = (mine_ref, other_ref)
    tokens = mine_ref.shape[0]
    blocks = [slice(index * tokens, (index + 1) * tokens) for index in range(2)]
    hidden_width = weight_ref.shape[0] // 3

    @pl.when(expert == 0)
    def _():
        total[...] = jnp.zeros_like(total)

    @pl.when(expert < experts)
    def _():
        number = first_ref[0] + expert
        slot = lax.broadcasted_iota(jnp.int32, (capacity, tokens), 0)
        parts = []
        for block, rows_ref in zip(blocks, row_refs):
            pick = (slot == rank_row_ref[0, :, block]).astype(FULL).astype(LOW)
            parts.append(dot_nn(pick, rows_ref[...]).astype(LOW))
        picked = jnp.concatenate(parts)
        picked_ref[0] = picked
        gate_part = dot_nt(picked, weight_ref[:hidden_width, :])
        up_part = dot_nt(picked, weight_ref[hidden_width : 2 * hidden_width, :])
        gate_part_ref[0] = gate_part
        up_part_ref[0] = up_part
        hidden = swiglu_low(gate_part, up_part)
        output = dot_nn(hidden, weight_ref[2 * hidden_width :, :]).astype(LOW)
        for index, block in enumerate(blocks):
            rank_col = column_of(rank_col_ref[block, :], number)
            back = lax.broadcasted_iota(jnp.int32, (tokens, capacity), 1) == rank_col
            spread = dot_nn(
                back.astype(FULL).astype(LOW), output[index * capacity : (index + 1) * capacity]
            )
            total[block, :] += column_of(gate_ref[block, :], number) * spread

    @pl.when(expert == experts)
    def _():
        for block, rows_ref in zip(blocks, row_refs):
            rows = rows_ref[...]
            gate_part = dot_nt(rows, weight_ref[:shared_width, :])
            up_part = dot_nt(rows, weight_ref[shared_width : 2 * shared_width, :])
            hidden = swiglu_low(gate_part, up_part)
            part = dot_nn(hidden, weight_ref[2 * shared_width : 3 * shared_width, :])
            out_ref[block, :] = (total[block, :] + part).astype(LOW)


def expert_specs(experts, hidden_width, slots, tokens):
    whole = lambda e, first_ref: (0, 0)
    fixed = lambda item: pl.BlockSpec(item.shape, whole, pipeline_mode=pl.Buffered(1))
    part = lambda e, first_ref: (jnp.minimum(e, experts - 1), 0, 0)
    return (
        whole,
        fixed,
        pl.BlockSpec((1, 1, tokens), part),
        pl.BlockSpec((3 * hidden_width, D), lambda e, first_ref: (e, 0)),
        pl.BlockSpec((1, slots, hidden_width), part),
        pl.BlockSpec((1, slots, D), part),
    )


def run_experts(
    first, rank_rows, rank_cols, gates, mine, other, weights, capacity, hidden_width, shared_width
):
    experts = rank_rows.shape[0]
    tokens = 2 * mine.shape[0]
    slots = 2 * capacity
    whole, fixed, row_spec, weight_spec, part_spec, picked_spec = expert_specs(
        experts, hidden_width, slots, tokens
    )
    return pl.pallas_call(
        functools.partial(expert_kernel, capacity, experts, shared_width),
        grid_spec=pltpu.PrefetchScalarGridSpec(
            num_scalar_prefetch=1,
            grid=(experts + 1,),
            in_specs=[
                row_spec,
                fixed(rank_cols),
                fixed(gates),
                fixed(mine),
                fixed(other),
                weight_spec,
            ],
            out_specs=[pl.BlockSpec((tokens, D), whole), part_spec, part_spec, picked_spec],
            scratch_shapes=[pltpu.VMEM((tokens, D), FULL)],
        ),
        out_shape=[
            jax.ShapeDtypeStruct((tokens, D), LOW),
            jax.ShapeDtypeStruct((experts, slots, hidden_width), FULL),
            jax.ShapeDtypeStruct((experts, slots, hidden_width), FULL),
            jax.ShapeDtypeStruct((experts, slots, D), LOW),
        ],
        compiler_params=params_of(),
        name="experts",
    )(first, rank_rows, rank_cols, gates, mine, other, weights)


def expert_back_kernel(
    capacity,
    experts,
    shared_width,
    first_ref,
    rank_row_ref,
    rank_col_ref,
    gate_row_ref,
    mine_ref,
    other_ref,
    mine_grad_ref,
    other_grad_ref,
    weight_ref,
    gate_part_ref,
    up_part_ref,
    picked_ref,
    out_ref,
    weight_grad_ref,
    total,
    gate_total,
):
    expert = pl.program_id(0)
    row_refs = (mine_ref, other_ref)
    grad_refs = (mine_grad_ref, other_grad_ref)
    tokens = mine_ref.shape[0]
    blocks = [slice(index * tokens, (index + 1) * tokens) for index in range(2)]
    hidden_width = weight_ref.shape[0] // 3
    shards, _, width = weight_grad_ref.shape

    @pl.when(expert == 0)
    def _():
        total[...] = jnp.zeros_like(total)
        gate_total[...] = jnp.zeros_like(gate_total)

    def put(start, grads):
        grads = grads.astype(LOW)
        for shard in range(shards):
            weight_grad_ref[shard, start : start + grads.shape[0], :] = grads[
                :, shard * width : (shard + 1) * width
            ]

    @pl.when(expert < experts)
    def _():
        number = first_ref[0] + expert
        slot = lax.broadcasted_iota(jnp.int32, (capacity, tokens), 0)
        slot_gates, grad_parts = [], []
        for block, grad_ref in zip(blocks, grad_refs):
            hit = slot == rank_row_ref[0, :, block]
            pick = hit.astype(FULL).astype(LOW)
            slot_gates.append(
                jnp.sum(jnp.where(hit, gate_row_ref[0, :, block], 0.0), axis=1, keepdims=True)
            )
            grad_parts.append(dot_nn(pick, grad_ref[...]))
        slot_gate = jnp.concatenate(slot_gates)
        picked = picked_ref[0]
        upstream = jnp.concatenate(grad_parts)
        gated = (slot_gate * upstream).astype(LOW)
        gate_part = gate_part_ref[0]
        up_part = up_part_ref[0]
        hidden = swiglu_low(gate_part, up_part)
        plain = dot_nt(upstream.astype(LOW), weight_ref[2 * hidden_width :, :])
        slot_grad = jnp.sum(hidden.astype(FULL) * plain, axis=1, keepdims=True)
        gate_grad, up_grad = swiglu_grads(gate_part, up_part, slot_gate * plain)
        gate_grad = gate_grad.astype(LOW)
        up_grad = up_grad.astype(LOW)
        put(0, dot_tn(gate_grad, picked))
        put(hidden_width, dot_tn(up_grad, picked))
        put(2 * hidden_width, dot_tn(hidden, gated))
        row_grad = dot_nn(gate_grad, weight_ref[:hidden_width, :])
        row_grad += dot_nn(up_grad, weight_ref[hidden_width : 2 * hidden_width, :])
        row_grad = row_grad.astype(LOW)
        lane = lax.broadcasted_iota(jnp.int32, (picked.shape[0], gate_total.shape[1]), 1)
        slot_grad = jnp.where(lane == number, slot_grad, 0.0).astype(LOW)
        for index, block in enumerate(blocks):
            rank_col = column_of(rank_col_ref[block, :], number)
            back = lax.broadcasted_iota(jnp.int32, (tokens, capacity), 1) == rank_col
            back = back.astype(FULL).astype(LOW)
            part = slice(index * capacity, (index + 1) * capacity)
            total[block, :] += dot_nn(back, row_grad[part])
            gate_total[block, :] += dot_nn(back, slot_grad[part])

    @pl.when(expert == experts)
    def _():
        weight_gate = weight_ref[:shared_width, :]
        weight_up = weight_ref[shared_width : 2 * shared_width, :]
        weight_down = weight_ref[2 * shared_width : 3 * shared_width, :]
        sums = [0.0, 0.0, 0.0]
        for block, rows_ref, grad_ref in zip(blocks, row_refs, grad_refs):
            rows = rows_ref[...]
            grads = grad_ref[...]
            gate_part = dot_nt(rows, weight_gate)
            up_part = dot_nt(rows, weight_up)
            hidden = swiglu_low(gate_part, up_part)
            gate_grad, up_grad = swiglu_grads(gate_part, up_part, dot_nt(grads, weight_down))
            gate_grad = gate_grad.astype(LOW)
            up_grad = up_grad.astype(LOW)
            pairs = ((gate_grad, rows), (up_grad, rows), (hidden, grads))
            sums = [item + dot_tn(*pair) for item, pair in zip(sums, pairs)]
            row_grad = dot_nn(gate_grad, weight_gate) + dot_nn(up_grad, weight_up)
            out_ref[block, :D] = (total[block, :] + row_grad).astype(LOW)
        for index, item in enumerate(sums):
            put(index * shared_width, item)
        out_ref[:, D:] = gate_total[...].astype(LOW)


def run_experts_back(
    first, rank_rows, rank_cols, gate_rows, mine, other, mine_grad, other_grad, weights,
    gate_part, up_part, picked, capacity, hidden_width, shared_width, shards, gate_lanes,
):
    experts = rank_rows.shape[0]
    tokens = 2 * mine.shape[0]
    slots = 2 * capacity
    whole, fixed, row_spec, weight_spec, part_spec, picked_spec = expert_specs(
        experts, hidden_width, slots, tokens
    )
    return pl.pallas_call(
        functools.partial(expert_back_kernel, capacity, experts, shared_width),
        grid_spec=pltpu.PrefetchScalarGridSpec(
            num_scalar_prefetch=1,
            grid=(experts + 1,),
            in_specs=[
                row_spec,
                fixed(rank_cols),
                row_spec,
                fixed(mine),
                fixed(other),
                fixed(mine_grad),
                fixed(other_grad),
                weight_spec,
                part_spec,
                part_spec,
                picked_spec,
            ],
            out_specs=[
                pl.BlockSpec((tokens, D + gate_lanes), whole),
                pl.BlockSpec(
                    (shards, 3 * hidden_width, D // shards), lambda e, first_ref: (0, e, 0)
                ),
            ],
            scratch_shapes=[
                pltpu.VMEM((tokens, D), FULL),
                pltpu.VMEM((tokens, gate_lanes), FULL),
            ],
        ),
        out_shape=[
            jax.ShapeDtypeStruct((tokens, D + gate_lanes), LOW),
            jax.ShapeDtypeStruct((shards, weights.shape[0], D // shards), LOW),
        ],
        compiler_params=params_of(),
        name="experts_back",
    )(
        first, rank_rows, rank_cols, gate_rows, mine, other, mine_grad, other_grad, weights,
        gate_part, up_part, picked,
    )


def head_kernel(valid_ref, rows_ref, table_ref, goal_ref, logit_ref, stat_ref, top, total, goal):
    step = pl.program_id(0)
    tokens = rows_ref.shape[0]
    block = table_ref.shape[0]
    lane = lax.broadcasted_iota(jnp.int32, (ROW_BLOCK, block), 1)

    @pl.when(step == 0)
    def _():
        top[...] = jnp.full_like(top, FAR)
        total[...] = jnp.zeros_like(total)
        goal[...] = jnp.zeros_like(goal)

    def work(masked):
        for start in range(0, tokens, ROW_BLOCK):
            part = slice(start, start + ROW_BLOCK)
            logits = dot_nt(rows_ref[part, :], table_ref[...])
            if masked:
                logits = jnp.where(lane < valid_ref[0] - step * block, logits, FAR)
            logit_ref[part, :] = logits
            old_top = top[part, :]
            new_top = jnp.maximum(old_top, jnp.max(logits, axis=1, keepdims=True))
            total[part, :] = total[part, :] * jnp.exp(old_top - new_top) + jnp.sum(
                jnp.exp(logits - new_top), axis=1, keepdims=True
            )
            top[part, :] = new_top
            hit = lane == goal_ref[part, :] - step * block
            goal[part, :] += jnp.sum(jnp.where(hit, logits, 0.0), axis=1, keepdims=True)

    inside = (step + 1) * block <= valid_ref[0]

    @pl.when(inside)
    def _():
        work(False)

    @pl.when(jnp.logical_not(inside))
    def _():
        work(True)

    @pl.when(step == pl.num_programs(0) - 1)
    def _():
        lane = lax.broadcasted_iota(jnp.int32, (tokens, LANES), 1)
        stat_ref[...] = jnp.where(
            lane == 0, top[...], jnp.where(lane == 1, total[...], goal[...])
        )


def run_head(rows, table, goal_local, valid):
    tokens = rows.shape[0]
    padded = table.shape[0]
    return pl.pallas_call(
        head_kernel,
        grid_spec=pltpu.PrefetchScalarGridSpec(
            num_scalar_prefetch=1,
            grid=(padded // VOCAB_BLOCK,),
            in_specs=[
                pl.BlockSpec((tokens, D), lambda j, valid_ref: (0, 0)),
                pl.BlockSpec((VOCAB_BLOCK, D), lambda j, valid_ref: (j, 0)),
                pl.BlockSpec((tokens, 1), lambda j, valid_ref: (0, 0)),
            ],
            out_specs=[
                pl.BlockSpec((tokens, VOCAB_BLOCK), lambda j, valid_ref: (0, j)),
                pl.BlockSpec((tokens, LANES), lambda j, valid_ref: (0, 0)),
            ],
            scratch_shapes=[pltpu.VMEM((tokens, 1), FULL)] * 3,
        ),
        out_shape=[
            jax.ShapeDtypeStruct((tokens, padded), FULL),
            jax.ShapeDtypeStruct((tokens, LANES), FULL),
        ],
        compiler_params=params_of(),
        name="head",
    )(valid, rows, table, goal_local)


def head_back_kernel(
    rows_ref, table_ref, goal_ref, scale_ref, logit_ref, out_ref, table_grad_ref, total, grads_ref
):
    step = pl.program_id(0)
    tokens = rows_ref.shape[0]
    block = table_ref.shape[0]
    shards, _, width = table_grad_ref.shape
    lane = lax.broadcasted_iota(jnp.int32, (ROW_BLOCK, block), 1)

    @pl.when(step == 0)
    def _():
        total[...] = jnp.zeros_like(total)

    for start in range(0, tokens, ROW_BLOCK):
        part = slice(start, start + ROW_BLOCK)
        grads = jnp.exp(logit_ref[part, :] - scale_ref[part, 0:1]) * scale_ref[part, 1:2]
        hit = lane == goal_ref[part, :] - step * block
        grads = jnp.where(hit, grads - 1.0, grads) * scale_ref[part, 2:3]
        grads = grads.astype(LOW)
        grads_ref[part, :] = grads
        total[part, :] += dot_nn(grads, table_ref[...])
    turned = grads_ref[...].T
    for shard in range(shards):
        cols = slice(shard * width, (shard + 1) * width)
        table_grad_ref[shard] = dot_nn(turned, rows_ref[:, cols]).astype(LOW)

    @pl.when(step == pl.num_programs(0) - 1)
    def _():
        out_ref[...] = total[...].astype(LOW)


def run_head_back(rows, table, goal_local, scales, logits, shards):
    tokens = rows.shape[0]
    padded = table.shape[0]
    return pl.pallas_call(
        head_back_kernel,
        grid=(padded // BACK_BLOCK,),
        in_specs=[
            pl.BlockSpec((tokens, D), lambda j: (0, 0)),
            pl.BlockSpec((BACK_BLOCK, D), lambda j: (j, 0)),
            pl.BlockSpec((tokens, 1), lambda j: (0, 0)),
            pl.BlockSpec((tokens, 4), lambda j: (0, 0)),
            pl.BlockSpec((tokens, BACK_BLOCK), lambda j: (0, j)),
        ],
        out_specs=[
            pl.BlockSpec((tokens, D), lambda j: (0, 0)),
            pl.BlockSpec((shards, BACK_BLOCK, D // shards), lambda j: (0, j, 0)),
        ],
        out_shape=[
            jax.ShapeDtypeStruct((tokens, D), LOW),
            jax.ShapeDtypeStruct((shards, padded, D // shards), LOW),
        ],
        scratch_shapes=[
            pltpu.VMEM((tokens, D), FULL),
            pltpu.VMEM((tokens, BACK_BLOCK), LOW),
        ],
        compiler_params=params_of(),
        name="head_back",
    )(rows, table, goal_local, scales, logits)


def table_step_kernel(
    factor_ref, weight_ref, moment_ref, square_ref, first_ref, second_ref, *out_refs
):
    factor = factor_ref[0]

    def step(grads, rate):
        results = adam_update(
            weight_ref[0], moment_ref[0], square_ref[0], grads * factor, rate, DECAYS[0]
        )
        for ref, value in zip(out_refs, results):
            ref[0] = value

    @pl.when(pl.program_id(0) == 0)
    def _():
        step(first_ref[...], TABLE_RATES[0])

    @pl.when(pl.program_id(0) == 1)
    def _():
        step(second_ref[...].astype(FULL), TABLE_RATES[1])


def table_step(factor, weight, moment, square, first, second):
    vocab, width = weight.shape[1:]
    rows = min(STEP_BLOCK, vocab)
    steps = pl.cdiv(vocab, rows)
    block = pl.BlockSpec((1, rows, width), lambda t, j, factor_ref: (t, j, 0))
    return pl.pallas_call(
        table_step_kernel,
        grid_spec=pltpu.PrefetchScalarGridSpec(
            num_scalar_prefetch=1,
            grid=(2, steps),
            in_specs=[
                block,
                block,
                block,
                pl.BlockSpec(
                    (rows, width),
                    lambda t, j, factor_ref: (jnp.where(t == 0, j, steps - 1), 0),
                ),
                pl.BlockSpec(
                    (rows, width), lambda t, j, factor_ref: (jnp.where(t == 1, j, 0), 0)
                ),
            ],
            out_specs=[block] * 3,
        ),
        out_shape=[jax.ShapeDtypeStruct(weight.shape, FULL)] * 3,
        compiler_params=params_of(2),
        name="table_step",
    )(factor, weight, moment, square, first, second)


def expert_step_kernel(factor_ref, core_ref, mine_ref, other_ref, *refs):
    factor = factor_ref[0]
    inner, outer = refs[:3], refs[3:6]
    inner_out, outer_out = refs[6:9], refs[9:]
    split = inner[0].shape[1]
    rows = mine_ref.shape[0] // 2
    half = pl.num_programs(0) // 2

    def step(grads):
        for index, part, ins, outs, rate in [
            item
            for index in range(2)
            for item in (
                (index, slice(index * rows, index * rows + split), inner, inner_out, 6),
                (index, slice(index * rows + split, (index + 1) * rows), outer, outer_out, 7),
            )
        ]:
            results = adam_update(
                ins[0][index],
                ins[1][index],
                ins[2][index],
                grads[part, :].astype(FULL) * factor,
                RATES[rate + 1],
                DECAYS[rate + 1],
            )
            for ref, value in zip(outs, results):
                ref[index] = value

    is_mine = pl.program_id(0) // half == core_ref[0]

    @pl.when(is_mine)
    def _():
        step(mine_ref)

    @pl.when(jnp.logical_not(is_mine))
    def _():
        step(other_ref)


def expert_step(factor, core, mine, other, inner, outer):
    experts, _, width = inner[0].shape
    half = experts // 4
    rows = inner[0].shape[1] + outer[0].shape[1]
    spec = lambda item: pl.BlockSpec((2,) + item.shape[1:], lambda e, f_ref, c_ref: (e, 0, 0))
    held = lambda turn: pl.BlockSpec(
        (2 * rows, width),
        lambda e, f_ref, c_ref: (
            jnp.clip(e - jnp.bitwise_xor(c_ref[0], turn) * half, 0, half - 1),
            0,
        ),
    )
    return pl.pallas_call(
        expert_step_kernel,
        grid_spec=pltpu.PrefetchScalarGridSpec(
            num_scalar_prefetch=2,
            grid=(experts // 2,),
            in_specs=[held(0), held(1)] + [spec(item) for item in inner + outer],
            out_specs=[spec(item) for item in inner + outer],
        ),
        out_shape=[jax.ShapeDtypeStruct(item.shape, FULL) for item in inner + outer],
        compiler_params=params_of(),
        name="expert_step",
    )(factor, core, mine, other, *inner, *outer)


def rows_of_attention(item):
    return item.transpose(1, 2, 0).reshape(-1, item.shape[0])


def rows_of_shared(shared_in, shared_out, padded):
    width = shared_out.shape[1]
    shared = jnp.concatenate([shared_in.transpose(1, 2, 0), shared_out[None]])
    shared = shared.reshape(3, 2, -1, width).transpose(1, 0, 2, 3)
    shared = jnp.pad(shared, ((0, 0), (0, 0), (0, padded - shared.shape[2]), (0, 0)))
    return shared.reshape(2, -1, width)


def shards(
    token_ids,
    target_ids,
    counted,
    routes,
    vocab_tables,
    norm_gains,
    attn_in,
    attention_output_weight,
    router,
    shared_in,
    shared_out,
    expert_in,
    expert_out,
    vocab_tables_moment,
    norm_gains_moment,
    attn_in_moment,
    attn_out_moment,
    router_moment,
    shared_in_moment,
    shared_out_moment,
    expert_in_moment,
    expert_out_moment,
    vocab_tables_square,
    norm_gains_square,
    attn_in_square,
    attn_out_square,
    router_square,
    shared_in_square,
    shared_out_square,
    expert_in_square,
    expert_out_square,
):
    seq_rows, seqs = token_ids.shape
    tokens = seq_rows * seqs
    model_size = lax.axis_size("mp")
    model_place = lax.axis_index("mp")
    data_size = lax.axis_size("dp")
    data_place = lax.axis_index("dp")
    width = vocab_tables.shape[1]
    vocab = vocab_tables.shape[2]
    experts = expert_in.shape[0]
    expert_total = experts * model_size
    capacity = min(2 * tokens * TOPK // expert_total, tokens)
    hidden_width = expert_out.shape[2]
    head_width = attention_output_weight.shape[0]
    shared_width = shared_out.shape[0]
    own = tokens // model_size
    gate_lanes = round_up(expert_total, LANES)
    place = data_place.reshape(1).astype(jnp.int32)

    counts = counted.T.reshape(tokens).astype(FULL)
    small = jnp.concatenate(
        [
            token_ids.T.reshape(tokens).astype(FULL),
            lax.optimization_barrier(norm_gains.astype(LOW)).astype(FULL).reshape(-1),
            jnp.sum(counts).reshape(1),
        ]
    )
    small = jnp.pad(small, (0, round_up(small.shape[0], 1024) - small.shape[0]))
    small = lax.all_gather(small, "dp", axis=0, tiled=False)
    shared_half = shared_width // 2
    shared_pad = round_up(shared_half, 16)
    core = core_place()
    core_item = core.reshape(1).astype(jnp.int32)
    shared_rows = rows_of_shared(shared_in, shared_out, shared_pad)
    expert_other = split_experts(1 - core_item, expert_in, expert_out, shared_rows)
    expert_mine = split_experts(core_item, expert_in, expert_out, shared_rows)
    ids = small[:, :tokens].astype(jnp.int32)
    gains = small[:, tokens : tokens + 3 * width].reshape(data_size, 3, width)
    gains = gains.transpose(1, 0, 2).reshape(3, D)
    token_count = jnp.sum(small[:, tokens + 3 * width])

    marks = jnp.concatenate(
        [
            routes.transpose(2, 1, 0).reshape(TOPK, tokens),
            target_ids.T.reshape(1, tokens),
            counted.T.reshape(1, tokens),
        ]
    )
    marks = jnp.stack([marks, swap(marks, 1)], axis=1)

    small_pieces = gather_blocks(
        jnp.concatenate([rows_of_attention(attn_in), attention_output_weight, router.T]).astype(
            LOW
        ),
        False,
    )
    expert_all = gather_half(core_item, expert_mine, expert_other)
    tables = vocab_tables.transpose(0, 2, 1)
    padded = round_up(vocab, 2 * VOCAB_BLOCK)
    table_low = jnp.pad(tables[1].astype(LOW), ((0, padded - vocab), (0, 0)))
    table_low = table_low.reshape(2, padded // 2, width)
    table_half = lambda place: lax.dynamic_index_in_dim(table_low, place, 0, keepdims=False)
    table_all = gather_half(core_item, table_half(core), table_half(1 - core))
    local_ids = ids.reshape(data_size, model_size, own).transpose(1, 0, 2).reshape(-1)
    local_ids = local_ids - model_place * vocab
    inside = (local_ids >= 0) & (local_ids < vocab)
    looked_up = lookup(jnp.clip(local_ids, 0, vocab - 1), tables)
    looked_up = jnp.where(inside[:, None], looked_up, 0.0).astype(LOW)
    embedded = sum_rows(looked_up, ring=True).astype(LOW).reshape(data_size, own, width)
    state_zero = lax.all_to_all(embedded, "dp", 0, 0, tiled=True)
    state_zero, *small_pieces = lax.optimization_barrier((state_zero, *small_pieces))
    small_all = jnp.concatenate(by_place(small_pieces), axis=1)
    attn_width = 4 * head_width
    weight_qkv = small_all[: 3 * head_width]
    weight_out = small_all[3 * head_width : attn_width]
    weight_router = small_all[attn_width:]
    state_zero = state_zero.transpose(1, 0, 2).reshape(own, D).astype(FULL)

    first_in = gather_rows(normed(state_zero, gains[0]).astype(LOW))
    projected = dot_nt(first_in, weight_qkv).astype(LOW)
    projected, weight_out = lax.optimization_barrier((projected, weight_out))
    weight_out_all = jnp.concatenate(
        [weight_out] + [shift(weight_out, step) for step in range(1, model_size)]
    )
    key_blocks = gather_blocks(projected[:, head_width:], True)
    attended, log_total = attend(place, projected, key_blocks, seqs)
    attended_pieces = attended.reshape(model_size, own, head_width)
    piece_of = lambda step: lax.dynamic_index_in_dim(
        attended_pieces, (model_place + step) % model_size, 0, keepdims=False
    )
    attended_own = [piece_of(0)] + [shift(piece_of(step), step) for step in range(1, model_size)]
    state_one = state_zero + dot_nn(jnp.concatenate(attended_own, axis=1), weight_out_all)

    expert_ids = jnp.arange(expert_total, dtype=jnp.int32)
    named = jnp.any(marks[:TOPK, :, None, :] == expert_ids[None, None, :, None], axis=0)
    earlier = jnp.arange(tokens)[:, None] < jnp.arange(tokens)[None, :]
    ranks = dot_nn(named.reshape(-1, tokens).astype(LOW), earlier.astype(LOW)).astype(jnp.int32)
    ranks = jnp.where(named, ranks.reshape(named.shape), -1)
    named_cols = named.transpose(0, 2, 1).reshape(2 * tokens, expert_total)
    rank_cols = ranks.transpose(0, 2, 1).reshape(2 * tokens, expert_total)
    part_experts = experts // 2
    first_expert = model_place * experts + core * part_experts
    local_rows = lambda table: lax.dynamic_slice_in_dim(table, first_expert, part_experts, 0)[
        :, None, :
    ]
    rank_rows = local_rows(ranks.transpose(1, 0, 2).reshape(expert_total, 2 * tokens))
    first_place = first_expert.reshape(1).astype(jnp.int32)
    second_in = gather_rows(normed(state_one, gains[1]).astype(LOW))
    second_other = swap(second_in, 1)
    router_logits = jnp.concatenate(
        [dot_nt(second_in, weight_router), dot_nt(second_other, weight_router)]
    )
    gates = jax.nn.softmax(jnp.where(named_cols, router_logits, FAR), axis=1)
    gates = jnp.where(named_cols, gates, 0.0)
    gate_rows = local_rows(gates.T)
    moe_part, gate_part, up_part, picked = run_experts(
        first_place, rank_rows, rank_cols, gates, second_in, second_other, expert_all, capacity,
        hidden_width, shared_pad,
    )
    state_two = state_one + sum_rows(sum_pair(moe_part))

    third_in = pair_rows(gather_rows(normed(state_two, gains[2]).astype(LOW)))
    half_vocab = padded // 2
    goal_local = marks[TOPK].reshape(2 * tokens, 1) - model_place * vocab
    goal_local = jnp.where(goal_local < vocab, goal_local - core * half_vocab, -1)
    valid = (vocab - core * half_vocab).reshape(1).astype(jnp.int32)
    logits, stats = run_head(third_in, table_all, goal_local, valid)
    stats = stats[:, :3].T
    stats = join_stats([stats, jnp.roll(swap(stats, 1), tokens, axis=1)])
    stats = join_stats(
        [stats]
        + [
            lax.ppermute(stats, "mp", [(i, i ^ mask) for i in range(model_size)])
            for mask in range(1, model_size)
        ]
    )
    log_head = stats[0] + jnp.log(stats[1])
    goal_logit = stats[2]
    pair_counts = marks[TOPK + 1].reshape(2 * tokens).astype(FULL)
    loss_rows = pair_counts * (log_head - goal_logit + Z_COEF * log_head * log_head)
    loss_part = jnp.sum(loss_rows[:tokens])
    scales = jnp.stack(
        [log_head, 1.0 + 2.0 * Z_COEF * log_head, pair_counts / token_count, pair_counts], axis=1
    )
    third_part, table_part = run_head_back(
        third_in, table_all, goal_local, scales, logits, data_size // 2
    )
    table_second = scatter_half(table_part)
    state_two_grad, gain_three = norm_back(state_two, gains[2], sum_rows(sum_pair(third_part)))

    two_low = gather_rows(state_two_grad.astype(LOW))
    second_part, expert_part = run_experts_back(
        first_place, rank_rows, rank_cols, gate_rows, second_in, second_other, two_low,
        swap(two_low, 1), expert_all, gate_part, up_part, picked, capacity, hidden_width, shared_pad,
        data_size // 2, gate_lanes,
    )
    expert_grad = scatter_half(expert_part)
    second_sum = sum_rows(sum_pair(second_part))
    second_grad = second_sum[:, :D]
    gate_grad = second_sum[:, D : D + expert_total]
    own_gates = lax.dynamic_slice_in_dim(gates, model_place * own, own, 0)
    choice_grad = own_gates * (
        gate_grad - jnp.sum(own_gates * gate_grad, axis=1, keepdims=True)
    )
    choice_grad = choice_grad.astype(LOW)
    second_grad = second_grad + dot_nn(choice_grad, weight_router)
    norm_grad, gain_two = norm_back(state_one, gains[1], second_grad)
    state_one_grad = state_two_grad + norm_grad

    own_low = state_one_grad.astype(LOW)
    out_grads = dot_nt(own_low, weight_out_all).astype(LOW)
    out_grad = jnp.zeros((tokens, head_width), LOW)
    for step in range(model_size):
        piece = out_grads[:, step * head_width : (step + 1) * head_width]
        if step > 0:
            piece = shift(piece, model_size - step)
        out_grad = lax.dynamic_update_slice(
            out_grad, piece, ((model_place + step) % model_size * own, 0)
        )
    own_low, out_grad = lax.optimization_barrier((own_low, out_grad))
    attn_out_grad = dot_tn(attended, gather_rows(own_low))
    query_grad, even_grads, odd_grads = attend_back(
        place, projected, log_total, out_grad, key_blocks, seqs, table_second
    )
    key_pairs = even_grads.astype(FULL) + swap(odd_grads, 1).astype(FULL)
    key_grad = scatter_pairs(key_pairs, True).astype(LOW)
    projected_grad = jnp.concatenate([query_grad, key_grad], axis=1)
    first_part = dot_nn(projected_grad, weight_qkv).astype(LOW)
    attn_in_grad = dot_tn(projected_grad, first_in)
    attn_pairs = pair_sums(jnp.concatenate([attn_in_grad, attn_out_grad]))
    norm_grad, gain_one = norm_back(state_zero, gains[0], sum_rows(first_part))
    state_zero_grad = state_one_grad + norm_grad

    tokens_part = data_size * own
    second_own = lax.dynamic_slice_in_dim(second_in, model_place * own, own, 0)
    gain_part = jnp.concatenate(
        [dot_tn(choice_grad, second_own), jnp.stack([gain_one, gain_two, gain_three])]
    ).astype(LOW)
    gain_rows = gain_part.shape[0]
    gain_pad = round_up(gain_rows, 16)
    gain_part = jnp.pad(gain_part, ((0, gain_pad - gain_rows), (0, 0)))
    back_rows = jnp.concatenate([state_zero_grad.astype(LOW), gain_part])
    back_rows = back_rows.reshape(own + gain_pad, data_size, width).transpose(1, 0, 2)
    attn_pairs, back_rows = lax.optimization_barrier((attn_pairs, back_rows))
    back_rows = lax.all_to_all(back_rows, "dp", 0, 0, tiled=True)
    attn_pairs, back_rows = lax.optimization_barrier((attn_pairs, back_rows))
    attn_sums = scatter_pairs(attn_pairs, False)
    back_parts = [back_rows] + [
        lax.ppermute(back_rows, "mp", [(i, i ^ mask) for i in range(model_size)])
        for mask in range(1, model_size)
    ]
    id_parts = [
        lax.dynamic_slice_in_dim(
            local_ids, jnp.bitwise_xor(model_place, mask) * tokens_part, tokens_part, 0
        )
        for mask in range(model_size)
    ]
    table_mine, table_other, second_square = part_features(core_item, table_second)
    table_other = swap(table_other, 1)
    second_square, back_parts[0] = lax.optimization_barrier((second_square, back_parts[0]))
    gain_sums = jnp.sum(
        sum(part[:, own : own + gain_rows].astype(FULL) for part in back_parts), axis=0
    )
    router_sums, gain_grad = gain_sums[:expert_total], gain_sums[expert_total:]
    table_first = []
    for part in (slice(0, 1), slice(1, model_size)):
        *table_first, first_square = table_grad(
            jnp.concatenate(id_parts[part]),
            jnp.concatenate([rows[:, :own].reshape(-1, width) for rows in back_parts[part]]),
            vocab,
            *table_first,
        )
    table_first = table_first[0].reshape(-1, width)

    expert_grad_mine, expert_grad_other, expert_square = part_features(core_item, expert_grad)
    expert_grads = (expert_grad_mine, swap(expert_grad_other, 1))
    square = lambda item: jnp.sum(jnp.square(item))
    local_square = (
        second_square
        + expert_square
        + jnp.sum(first_square)
        + square(attn_sums)
        + square(gain_sums) / model_size
    )
    table_second = in_order(table_mine, table_other, 0)[:vocab]
    shared_sums = in_order(
        *[
            item[3 * part_experts * hidden_width :].reshape(3, shared_pad, width)[:, :shared_half]
            for item in expert_grads
        ],
        1,
    ).astype(FULL)
    sums = jnp.stack([local_square, loss_part / model_size])
    sums = add_all(jnp.broadcast_to(sums[:, None], (2, LANES)))[:, 0]
    grad_norm = jnp.sqrt(sums[0])
    factor = CLIP / jnp.maximum(grad_norm, CLIP)

    table_results = table_step(
        factor.reshape(1),
        tables,
        vocab_tables_moment.transpose(0, 2, 1),
        vocab_tables_square.transpose(0, 2, 1),
        table_first,
        table_second,
    )
    results = [sums[1], token_count, grad_norm]
    results.extend(item.transpose(0, 2, 1) for item in table_results)
    gradients = (
        gain_grad,
        attn_sums[: 3 * head_width].reshape(3, head_width, width).transpose(2, 0, 1),
        attn_sums[3 * head_width :],
        router_sums.T,
        shared_sums[:2].transpose(2, 0, 1),
        shared_sums[2],
    )
    params = (
        norm_gains, attn_in, attention_output_weight, router, shared_in, shared_out,
    )
    moments = (
        norm_gains_moment, attn_in_moment, attn_out_moment, router_moment, shared_in_moment,
        shared_out_moment,
    )
    squares = (
        norm_gains_square, attn_in_square, attn_out_square, router_square, shared_in_square,
        shared_out_square,
    )
    for index in range(6):
        results.extend(
            adam_update(
                params[index],
                moments[index],
                squares[index],
                gradients[index] * factor,
                RATES[index + 1],
                DECAYS[index + 1],
            )
        )
    expert_results = expert_step(
        factor.reshape(1),
        core_item,
        *expert_grads,
        [
            item.transpose(0, 2, 3, 1).reshape(experts, 2 * hidden_width, width)
            for item in (expert_in, expert_in_moment, expert_in_square)
        ],
        [
            item.transpose(0, 2, 1)
            for item in (expert_out, expert_out_moment, expert_out_square)
        ],
    )
    results.extend(
        item.reshape(experts, 2, hidden_width, width).transpose(0, 3, 1, 2)
        for item in expert_results[:3]
    )
    results.extend(item.transpose(0, 2, 1) for item in expert_results[3:])
    return tuple(results)


def solution(mesh):
    in_specs = (
        P("dp", None),
        P("dp", None),
        P("dp", None),
        P("dp", None, None),
        P(None, "dp", "mp"),
        P(None, "dp"),
        P("dp", None, "mp"),
        P("mp", "dp"),
        P("dp", None),
        P("dp", None, "mp"),
        P("mp", "dp"),
        P("mp", "dp", None, None),
        P("mp", "dp", None),
        P(None, "dp", "mp"),
        P(None, "dp"),
        P("dp", None, "mp"),
        P("mp", "dp"),
        P("dp", None),
        P("dp", None, "mp"),
        P("mp", "dp"),
        P("mp", "dp", None, None),
        P("mp", "dp", None),
        P(None, "dp", "mp"),
        P(None, "dp"),
        P("dp", None, "mp"),
        P("mp", "dp"),
        P("dp", None),
        P("dp", None, "mp"),
        P("mp", "dp"),
        P("mp", "dp", None, None),
        P("mp", "dp", None),
    )
    out_specs = (
        P(),
        P(),
        P(),
        P(None, "dp", "mp"),
        P(None, "dp", "mp"),
        P(None, "dp", "mp"),
        P(None, "dp"),
        P(None, "dp"),
        P(None, "dp"),
        P("dp", None, "mp"),
        P("dp", None, "mp"),
        P("dp", None, "mp"),
        P("mp", "dp"),
        P("mp", "dp"),
        P("mp", "dp"),
        P("dp", None),
        P("dp", None),
        P("dp", None),
        P("dp", None, "mp"),
        P("dp", None, "mp"),
        P("dp", None, "mp"),
        P("mp", "dp"),
        P("mp", "dp"),
        P("mp", "dp"),
        P("mp", "dp", None, None),
        P("mp", "dp", None, None),
        P("mp", "dp", None, None),
        P("mp", "dp", None),
        P("mp", "dp", None),
        P("mp", "dp", None),
    )
    return jax.shard_map(shards, mesh=mesh, in_specs=in_specs, out_specs=out_specs, check_vma=False)
```
